32 devices in a mesh: groups: 2 (over y), cells: 4 (over z), sect: 2 (over x), lev: 2 (over core).
Axes of the slice: x: 2, y: 2, z: 4, core: 2. Of those that a mesh axis runs over, the one named last changes fastest.
Arguments:
- spectrum: bfloat16 [1152, 32, 256], P(('cells', 'lev'), 'groups', 'sect'), parts along dimension 1, may hold values from -6 to 6
- courant_x: float32 [1152], P(('cells', 'lev')), may hold values from -0.45 to 0.45
- courant_y: float32 [1152], P(('cells', 'lev')), may hold values from -0.45 to 0.45
- growth: float32 [1152], replicated, may hold values from 0.5 to 2
- quartet: bfloat16 [1152, 1152], replicated, may hold values from -0.1875 to 0.1875
- coupler: bfloat16 [128, 1152], replicated, may hold values from -0.1875 to 0.1875
- atmosphere: float32 [64, 32, 256], P('lev', ('groups', 'cells'), 'sect'), parts along dimension 1, may hold values from -6 to 6
- ocean_state: float32 [64, 32, 256], P('lev', ('groups', 'cells'), 'sect'), parts along dimension 1, may hold values from -6 to 6
- sea_mask: int32 [32, 256], P(('groups', 'cells'), 'sect'), parts along dimension 0, may hold values 0 or 1
Outputs:
- spectrum_out: bfloat16 [1152, 32, 256], P(('cells', 'lev'), 'groups', 'sect'), parts along dimension 1
- atmosphere_out: float32 [64, 32, 256], P('lev', ('groups', 'cells'), 'sect'), parts along dimension 1
- ocean_out: float32 [64, 32, 256], P('lev', ('groups', 'cells'), 'sect'), parts along dimension 1
The draws below stay inside these ranges and needn't reach their ends.
There are 2 independent parts, one for each index of `groups`. The reference program is written for one: setup_inputs(seed, part) draws one part's arguments, and reference() takes and returns one part's arrays. A program takes and returns all parts, laid end to end along the dimension named above; an argument that names none is the same for every part. Nothing has to cross between parts.
Inputs may be any that keep to these rules, and one draw needn't show every extreme that they name: `sea_mask`: 1 marks a sea cell, 0 a land cell.
All inputs are finite; a program needn't handle non-finite values. No bound on the sum of `sea_mask` on one device may be relied on, other than what follows from the above.
Results may differ from the reference program's by a relative error of at most 0.0062.
Values may be sent and summed in bfloat16 or wider, within the bound.
No kernel may reach another device: no remote copies, remote signals or barrier semaphores. Data moves between devices by JAX's collectives and lax.ppermute only.
A program may use at most 64 MiB of HBM per device.

```python
import math
import jax
import jax.numpy as jnp
from jax import lax

COMPS = 1152
LEVELS = 64
NSTEP = 2
GRID_Y = 16
GRID_X = 256


def place_ends(entries, stream_key, low, largest):
    shape = entries.shape
    spot = [jax.random.randint(jax.random.fold_in(stream_key, axis), (), 0, shape[axis]) for axis in range(len(shape))]
    entries = entries.at[tuple(spot)].set(low)
    longest = shape.index(max(shape))
    spot[longest] = (spot[longest] + 1) % shape[longest]
    return entries.at[tuple(spot)].set(largest)


def level_of(own_key, extent, split, smallest, high):
    def one(position, parts):
        draws = jax.random.uniform(jax.random.fold_in(jax.random.fold_in(own_key, 6), position), (parts,), jnp.float32, smallest / len(split), high / len(split))
        return jnp.repeat(jnp.exp(draws), extent[position] // parts).reshape((-1,) + (1,) * (len(extent) - position - 1))

    level = one(*split[0])
    for cut in split[1:]:
        level = level * one(*cut)
    return level


def centred(key, dims, deviation, reach, pieces=(), kind=jnp.bfloat16):
    values = deviation * jax.random.normal(key, dims, jnp.float32)
    if pieces:
        values = values * level_of(key, dims, pieces, -0.22, 0.18)
    return jnp.clip(values, -reach, reach).astype(kind)


def setup_inputs(seed: int = 0, part: int = 0) -> dict:
    arg_keys = jax.random.split(jax.random.key(seed), 10)
    own_keys = jax.random.split(jax.random.fold_in(arg_keys[9], part), 10)
    spectrum = centred(own_keys[0], (COMPS, GRID_Y, GRID_X), 1.0, 6.0, ((0, 8), (2, 2)))
    courant_x = jnp.clip(jax.random.uniform(arg_keys[1], (COMPS,), jnp.float32, -0.45, 0.45) * level_of(arg_keys[1], (COMPS,), ((0, 8),), -0.4, 0.0), -0.45, 0.45)
    courant_y = jnp.clip(jax.random.uniform(arg_keys[2], (COMPS,), jnp.float32, -0.45, 0.45) * level_of(arg_keys[2], (COMPS,), ((0, 8),), -0.4, 0.0), -0.45, 0.45)
    growth = jnp.clip(jnp.exp(jax.random.uniform(arg_keys[3], (COMPS,), jnp.float32, math.log(0.5), math.log(2.0))), 0.5, 2.0)
    quartet = centred(arg_keys[4], (COMPS, COMPS), COMPS ** -0.5, 0.1875)
    coupler = centred(arg_keys[5], (2 * LEVELS, COMPS), COMPS ** -0.5, 0.1875)
    atmosphere = centred(own_keys[6], (LEVELS, GRID_Y, GRID_X), 1.0, 6.0, ((0, 2), (1, 4), (2, 2)), jnp.float32)
    ocean_state = centred(own_keys[7], (LEVELS, GRID_Y, GRID_X), 1.0, 6.0, ((0, 2), (1, 4), (2, 2)), jnp.float32)
    sea_mask = place_ends((jax.random.randint(own_keys[8], (GRID_Y, GRID_X), 0, 4) < 3).astype(jnp.int32), jax.random.fold_in(own_keys[8], 1), 0, 1)
    return {"spectrum": spectrum, "courant_x": courant_x, "courant_y": courant_y, "growth": growth, "quartet": quartet, "coupler": coupler, "atmosphere": atmosphere, "ocean_state": ocean_state, "sea_mask": sea_mask}


def upwind(values, courant, before, after):
    return jnp.maximum(courant, 0.0) * (values - before) + jnp.minimum(courant, 0.0) * (after - values)


def column_update(state, forcing, factor):
    padded = jnp.pad(state, 1)
    middle = padded[1:-1, 1:-1, 1:-1]
    lateral = padded[1:-1, 2:, 1:-1] + padded[1:-1, :-2, 1:-1] + padded[1:-1, 1:-1, 2:] + padded[1:-1, 1:-1, :-2] - 4.0 * middle
    upright = padded[2:, 1:-1, 1:-1] + padded[:-2, 1:-1, 1:-1] - 2.0 * middle
    return middle + 0.1 * lateral + 0.1 * upright + factor * forcing


def reference(spectrum, courant_x, courant_y, growth, quartet, coupler, atmosphere, ocean_state, sea_mask):
    highest = lax.Precision.HIGHEST
    weights = quartet.astype(jnp.float32)
    couple_full = coupler.astype(jnp.float32)
    shift_x = courant_x[:, None, None]
    shift_y = courant_y[:, None, None]
    sea_float = sea_mask.astype(jnp.float32).reshape(1, GRID_Y * GRID_X)
    energy = spectrum
    for counter in range(NSTEP):
        surface_wind = atmosphere[0] - ocean_state[0]
        wind_input = (surface_wind * surface_wind).reshape(1, GRID_Y * GRID_X)
        values = energy.astype(jnp.float32)
        moved = values - upwind(values, shift_x, jnp.roll(values, 1, axis=2), jnp.roll(values, -1, axis=2))
        moved = moved - upwind(values, shift_y, jnp.roll(values, 1, axis=1), jnp.roll(values, -1, axis=1))
        advected = lax.optimization_barrier(moved.astype(jnp.bfloat16)).astype(jnp.float32)
        advected = advected.reshape(COMPS, GRID_Y * GRID_X)
        paired = jnp.dot(weights, advected, precision=highest)
        squared = lax.optimization_barrier((advected * advected).astype(jnp.bfloat16)).astype(jnp.float32)
        quad_square = jnp.dot(weights, squared, precision=highest)
        fresh = (advected + 0.3 * (advected * paired - quad_square) + 0.1 * growth[:, None] * wind_input) / (1.0 + 0.1 * advected * advected)
        fresh = (fresh * sea_float).astype(jnp.bfloat16)
        fresh_float = lax.optimization_barrier(fresh).astype(jnp.float32)
        profile = jnp.dot(couple_full, fresh_float, precision=highest).reshape(2, LEVELS, GRID_Y, GRID_X)
        atmosphere = column_update(atmosphere, profile[0], -0.3)
        ocean_state = column_update(ocean_state, profile[1], 0.3)
        energy = fresh.reshape(COMPS, GRID_Y, GRID_X)
    return energy, atmosphere, ocean_state
```

```python
import functools

import jax
import jax.numpy as jnp
from jax import lax
from jax.experimental import pallas as pl
from jax.experimental.pallas import tpu as pltpu
from jax.sharding import PartitionSpec as P

NSTEP = 2
LANES = 128
F32 = jnp.float32
BF16 = jnp.bfloat16
VMEM = pltpu.VMEM


def from_root(block, axis, source):
    block = jnp.where(lax.axis_index(axis) == source, block, jnp.zeros_like(block))
    return lax.psum(block, axis)


def extended_2(block, sides, width, periodic):
    for axis, dim in sides:
        count = lax.axis_size(axis)
        forward = [(i, i + 1) for i in range(count - 1)]
        if periodic:
            forward.append((count - 1, 0))
        backward = [(target, source) for source, target in forward]
        low = lax.ppermute(
            lax.slice_in_dim(block, block.shape[dim] - width, None, axis=dim), axis, forward
        )
        high = lax.ppermute(lax.slice_in_dim(block, 0, width, axis=dim), axis, backward)
        block = jnp.concatenate([low, block, high], axis=dim)
    return block


def upwind(values, courant, before, after):
    return jnp.maximum(courant, 0.0) * (values - before) + jnp.minimum(courant, 0.0) * (
        after - values
    )


def any_shape(
    spectrum, courant_x, courant_y, growth, quartet, coupler, atmosphere, ocean_state, sea_mask
):
    cell_tiles = lax.axis_size("cells")
    lev_parts = lax.axis_size("lev")
    blocks = cell_tiles * lev_parts
    comps_own, rows_all, row_width = spectrum.shape
    total_comps = comps_own * blocks
    cell_rows = rows_all // blocks
    level_count = coupler.shape[0] // 2
    row_start = lax.axis_index("lev") * cell_rows
    shift_x = courant_x[:, None, None]
    shift_y = courant_y[:, None, None]
    sea_rows = (
        lax.dynamic_slice_in_dim(sea_mask, row_start, cell_rows, 0)
        .astype(jnp.float32)
        .reshape(1, cell_rows * row_width)
    )
    growth_column = growth[:, None]
    forcing_sign = jnp.array([-0.3, 0.3], jnp.float32)[:, None, None, None]
    state = jnp.stack([atmosphere, ocean_state])
    energy = spectrum
    for counter in range(NSTEP):
        surface = from_root(state[:, 0], "lev", 0)
        surface_wind = surface[0] - surface[1]
        wind_rows = lax.dynamic_slice_in_dim(
            surface_wind * surface_wind, row_start, cell_rows, 0
        ).reshape(1, cell_rows * row_width)
        padded = extended_2(energy, (("sect", 2),), 1, True)
        values = padded[:, :, 1:-1].astype(jnp.float32)
        west_side = padded[:, :, :-2].astype(jnp.float32)
        east_side = padded[:, :, 2:].astype(jnp.float32)
        moved = values - upwind(values, shift_x, west_side, east_side)
        moved = moved - upwind(
            values, shift_y, jnp.roll(values, 1, axis=1), jnp.roll(values, -1, axis=1)
        )
        advected = moved.astype(jnp.bfloat16)
        pieces = advected.reshape(1, comps_own, blocks, cell_rows, row_width)
        on_cells = lax.all_to_all(pieces, ("cells", "lev"), split_axis=2, concat_axis=0, tiled=True)
        on_cells = on_cells.reshape(total_comps, cell_rows * row_width)
        cell_values = on_cells.astype(jnp.float32)
        paired = jnp.dot(quartet, on_cells, preferred_element_type=jnp.float32)
        squared = (cell_values * cell_values).astype(jnp.bfloat16)
        quad_square = jnp.dot(quartet, squared, preferred_element_type=jnp.float32)
        fresh = (
            cell_values
            + 0.3 * (cell_values * paired - quad_square)
            + 0.1 * growth_column * wind_rows
        ) / (1.0 + 0.1 * cell_values * cell_values)
        fresh = (fresh * sea_rows).astype(jnp.bfloat16)
        profile = jnp.dot(coupler, fresh, preferred_element_type=jnp.float32).reshape(
            2, level_count, cell_rows, row_width
        )
        forcing = lax.all_to_all(profile, "lev", split_axis=1, concat_axis=2, tiled=True)
        returned = fresh.reshape(blocks, comps_own, 1, cell_rows, row_width)
        returned = lax.all_to_all(
            returned, ("cells", "lev"), split_axis=0, concat_axis=2, tiled=True
        )
        energy = returned.reshape(comps_own, rows_all, row_width)
        extended = extended_2(state, (("lev", 1), ("cells", 2), ("sect", 3)), 1, False)
        state = relaxed(extended, 1) + forcing_sign * forcing
    return (energy, state[0], state[1])


def relaxed(extended, first):
    centre = (slice(None),) * first + (slice(1, -1),) * 3
    middle = extended[centre]

    def moved(dim, start):
        where = list(centre)
        where[first + dim] = slice(start, extended.shape[first + dim] - 2 + start)
        return extended[tuple(where)]

    lateral = moved(1, 2) + moved(1, 0) + moved(2, 2) + moved(2, 0) - 4.0 * middle
    upright = moved(0, 2) + moved(0, 0) - 2.0 * middle
    return middle + 0.1 * lateral + 0.1 * upright


def lane_of(shape):
    return lax.broadcasted_iota(jnp.int32, shape, len(shape) - 1)


def rolled(values, shift):
    shift = shift % LANES
    return values if shift == 0 else pltpu.roll(values, shift, 1)


def swapped_blocks(values, unit):
    values = list(values)
    lane = lane_of(values[0].shape)
    step = 1
    while step < len(values):
        upper = (lane // (unit * step)) % 2 == 1
        for low in range(len(values)):
            if low & step:
                continue
            a, b = values[low], values[low | step]
            values[low] = jnp.where(upper, rolled(b, unit * step), a)
            values[low | step] = jnp.where(upper, b, rolled(a, -unit * step))
        step *= 2
    return values


def row_before(values, rows, periodic):
    lane = lane_of(values.shape) % rows
    wrap = rolled(values, 1 - rows) if periodic else 0.0
    return jnp.where(lane == 0, wrap, rolled(values, 1))


def row_after(values, rows, periodic):
    lane = lane_of(values.shape) % rows
    wrap = rolled(values, rows - 1) if periodic else 0.0
    return jnp.where(lane == rows - 1, wrap, rolled(values, -1))


def column_neighbours(first, second, outer, rows):
    lane = lane_of(first.shape)
    low, high = lane < rows, lane >= LANES - rows
    first_up, second_up = rolled(first, rows), rolled(second, rows)
    first_down, second_down = rolled(first, -rows), rolled(second, -rows)
    west = (jnp.where(low, outer, first_up), jnp.where(low, first_up, second_up))
    east = (jnp.where(high, second_down, first_down), jnp.where(high, outer, second_down))
    return west, east


def to_column_major(cells, rows, width):
    source = lax.broadcasted_iota(jnp.int32, (cells, cells), 0)
    target = lax.broadcasted_iota(jnp.int32, (cells, cells), 1)
    return ((target % rows) * width + target // rows == source).astype(BF16)


def to_row_major(cells, rows, width):
    source = lax.broadcasted_iota(jnp.int32, (cells, cells), 0)
    target = lax.broadcasted_iota(jnp.int32, (cells, cells), 1)
    return ((target % width) * rows + target // width == source).astype(BF16)


def edges_kernel(x_ref, by_row_ref, edge_ref, wide):
    comps, rows, columns = x_ref.shape
    wide[...] = x_ref[...].astype(F32).reshape(comps * rows, columns)
    column = lax.broadcasted_iota(jnp.int32, (columns, LANES), 0)
    lane = lax.broadcasted_iota(jnp.int32, (columns, LANES), 1)
    block = (lane // rows) % 4
    wanted = jnp.where(block < 2, columns - 2 + block, block - 2)
    total = jnp.zeros((comps, LANES), F32)
    for row in range(rows):
        values = wide[pl.ds(row, comps, stride=rows), :].astype(BF16)
        by_row_ref[row] = values
        pick = ((wanted == column) & (lane % rows == row)).astype(BF16)
        total += jnp.dot(values, pick, preferred_element_type=F32)
    edge_ref[...] = total.astype(BF16)


def advect_kernel(groups, count, where_ref, by_row_ref, edge_ref, halo_ref, cx_ref, cy_ref, *refs):
    out_refs, (packed, cell_major) = refs[:count], refs[count:]
    rows, comps, columns = by_row_ref.shape
    width = columns // count
    part = 16

    @pl.loop(0, comps // part)
    def _(step):
        start = pl.multiple_of(step * part, part)
        values = [by_row_ref[row, pl.ds(start, part), :].astype(F32) for row in range(rows)]
        cx = jnp.broadcast_to(cx_ref[pl.ds(start, part), :], (part, columns))
        cy = jnp.broadcast_to(cy_ref[pl.ds(start, part), :], (part, columns))
        moved = []
        for row in range(rows):
            here = values[row]
            along = upwind(here, cx, rolled(here, 1), rolled(here, -1))
            across = upwind(here, cy, values[row - 1], values[(row + 1) % rows])
            moved.append(here - along - across)
        for tile in range(rows // count):
            pieces = swapped_blocks(moved[tile * count : (tile + 1) * count], width)
            for target in range(count):
                cell_major[
                    pl.ds(pl.multiple_of(target * comps + start, part), part),
                    tile * LANES : (tile + 1) * LANES,
                ] = pieces[target].astype(BF16)

    change = to_column_major(rows * width, rows, width)
    lane = lane_of((comps, LANES))
    block = lane // rows
    halo = halo_ref[...].astype(F32)
    edge = edge_ref[...].astype(F32)
    near = jnp.where((block < 2) | (block >= 6), halo, edge)
    cx = jnp.broadcast_to(cx_ref[...], (comps, LANES))
    cy = jnp.broadcast_to(cy_ref[...], (comps, LANES))
    near = (
        near
        - upwind(near, cx, rolled(near, rows), rolled(near, -rows))
        - upwind(near, cy, row_before(near, rows, True), row_after(near, rows, True))
    )
    tiles = []
    for target in range(count):
        both = jnp.dot(
            cell_major[target * comps : (target + 1) * comps, :],
            change,
            preferred_element_type=F32,
        )
        tiles.append([both[:, :LANES], both[:, LANES:]])
    tiles[0][0] = jnp.where(block == 0, rolled(near, -2 * rows), tiles[0][0])
    tiles[-1][1] = jnp.where(block == 7, rolled(near, 2 * rows), tiles[-1][1])
    size = comps // groups
    me = where_ref[0]
    for target in range(count):
        west = rolled(tiles[target - 1][1], rows) if target else rolled(near, -rows)
        east = rolled(tiles[target + 1][0], -rows) if target < count - 1 else rolled(near, rows)
        outer = jnp.where(block == 0, west, east)
        shared = outer[:size]
        for group in range(1, groups):
            other = rolled(outer[group * size : (group + 1) * size], 2 * group * rows)
            own = lane_of(other.shape) // rows
            shared = jnp.where((own == 2 * group) | (own == 2 * group - 1), other, shared)
        slot = lax.rem(target - me + count, count)
        packed[slot, :comps, :] = tiles[target][0].astype(BF16)
        packed[slot, comps : 2 * comps, :] = tiles[target][1].astype(BF16)
        packed[slot, 2 * comps :, :] = shared.astype(BF16)
    for slot in range(count):
        out_refs[slot][...] = packed[slot]


def steps_kernel(groups, count, where_ref, quartet_ref, coupler_ref, growth_ref, surface_ref, *refs):
    in_refs, refs = refs[:count], refs[count:]
    out_refs, (first_in, fresh, second_in, last, ordered, shares) = refs[:count], refs[count:]
    total = quartet_ref.shape[0]
    comps = total // count
    size = comps // groups
    rows = surface_ref.shape[0] // 3
    grid_columns = surface_ref.shape[1]
    cells = 2 * LANES
    wide = 3 * LANES
    width = cells // rows
    levels = coupler_ref.shape[0] // 2
    me = where_ref[0]
    base = where_ref[1]

    for slot in range(count):
        source = lax.rem(me - slot + count, count)
        start = pl.multiple_of(source * comps, 16)
        first_in[pl.ds(start, comps), :LANES] = in_refs[slot][:comps]
        first_in[pl.ds(start, comps), LANES:cells] = in_refs[slot][comps : 2 * comps]
        shared = in_refs[slot][2 * comps :].astype(F32)
        for group in range(groups):
            first_in[pl.ds(start + group * size, size), cells:wide] = rolled(
                shared, -2 * group * rows
            ).astype(BF16)

    lane = lane_of((grid_columns, wide))
    offset = jnp.where(lane < cells, lane // rows, jnp.where(lane < cells + rows, -1, width))
    wanted = lax.rem(base + offset + grid_columns, grid_columns)
    pick = (lax.broadcasted_iota(jnp.int32, (grid_columns, wide), 0) == wanted).astype(BF16)
    rest = surface_ref[...]
    spread = jnp.zeros((3 * rows, wide), F32)
    for _ in range(3):
        head = rest.astype(BF16)
        rest = rest - head.astype(F32)
        spread += jnp.dot(head, pick, preferred_element_type=F32)
    row = lax.broadcasted_iota(jnp.int32, (rows, wide), 0)
    lane = lane_of((rows, wide))
    used = (lane < cells + rows) | (lane >= wide - rows)
    keep = (row == lane % rows) & used

    def field(index):
        values = jnp.where(keep, spread[index * rows : (index + 1) * rows], 0.0)
        return jnp.sum(values, axis=0, keepdims=True)

    surface, below, sea = field(0), field(1), field(2)
    wind = 0.1 * surface * surface

    def renew(values, products, growth, wind, sea):
        half = values.shape[1]
        paired, quad_square = products[:, :half], products[:, half:]
        return (
            (values + 0.3 * (values * paired - quad_square) + growth * wind)
            / (1.0 + 0.1 * values * values)
        ) * sea

    part = total // 3
    for step in range(3):
        span = slice(step * part, (step + 1) * part)
        values = first_in[span, :wide].astype(F32)
        first_in[span, wide:] = (values * values).astype(BF16)

    @pl.loop(0, 3)
    def _(step):
        span = pl.ds(pl.multiple_of(step * part, part), part)
        products = jnp.dot(quartet_ref[span, :], first_in[...], preferred_element_type=F32)
        values = first_in[span, :wide].astype(F32)
        fresh[span, :] = renew(values, products, growth_ref[span, :1], wind, sea).astype(BF16)

    level = lax.broadcasted_iota(jnp.int32, (2 * levels, wide), 0)
    forced = jnp.dot(coupler_ref[...], fresh[...], preferred_element_type=F32)
    forced = jnp.where(level < levels, -0.3, 0.3) * forced

    def beside(values):
        first, second = values[:, :LANES], values[:, LANES:cells]
        west, east = column_neighbours(first, second, values[:, cells:], rows)
        lane = lane_of(first.shape)
        west_edge = (base == 0) & (lane < rows)
        east_edge = (base + width == grid_columns) & (lane >= LANES - rows)
        west = (jnp.where(west_edge, 0.0, west[0]), west[1])
        east = (east[0], jnp.where(east_edge, 0.0, east[1]))
        sums = [
            row_before(here, rows, False) + row_after(here, rows, False) + west[i] + east[i]
            for i, here in enumerate((first, second))
        ]
        return jnp.concatenate(sums, axis=1) - 4.0 * values[:, :cells]

    eight = jnp.broadcast_to(surface, (8, wide))
    calm = surface[:, :cells] + 0.1 * beside(eight)[:1]
    calm = calm + 0.1 * (below[:, :cells] - 2.0 * surface[:, :cells])
    later = calm + forced[:1, :cells] - forced[levels : levels + 1, :cells]
    later = 0.1 * later * later
    middle = forced[:, :cells]
    level = level[:, :cells] % levels
    above = jnp.where(level == 0, 0.0, pltpu.roll(middle, 1, 0))
    under = jnp.where(level == levels - 1, 0.0, pltpu.roll(middle, 2 * levels - 1, 0))
    carried = middle + 0.1 * beside(forced) + 0.1 * (above + under - 2.0 * middle)


    @pl.loop(0, total // 32)
    def _(step):
        span = pl.ds(pl.multiple_of(step * 32, 32), 32)
        first = fresh[span, :LANES].astype(F32)
        second = fresh[span, LANES:cells].astype(F32)
        west, east = column_neighbours(first, second, fresh[span, cells:].astype(F32), rows)
        cx = jnp.broadcast_to(growth_ref[span, 1:2], first.shape)
        cy = jnp.broadcast_to(growth_ref[span, 2:3], first.shape)
        for i, here in enumerate((first, second)):
            moved = here - upwind(here, cx, west[i], east[i])
            moved = moved - upwind(
                here, cy, row_before(here, rows, True), row_after(here, rows, True)
            )
            moved = moved.astype(BF16)
            second_in[span, i * LANES : (i + 1) * LANES] = moved
            moved = moved.astype(F32)
            second_in[span, cells + i * LANES : cells + (i + 1) * LANES] = (moved * moved).astype(
                BF16
            )

    back = to_row_major(cells, rows, width)

    @pl.loop(0, 3)
    def _(step):
        span = pl.ds(pl.multiple_of(step * part, part), part)
        products = jnp.dot(quartet_ref[span, :], second_in[...], preferred_element_type=F32)
        values = second_in[span, :cells].astype(F32)
        done = renew(values, products, growth_ref[span, :1], later, sea[:, :cells]).astype(BF16)
        last[span, :] = done
        ordered[span, :] = jnp.dot(done, back, preferred_element_type=F32).astype(BF16)

    forced = jnp.dot(coupler_ref[...], last[...], preferred_element_type=F32)
    carried = carried + jnp.where(level_sign(levels, cells), -0.3, 0.3) * forced
    carried = jnp.dot(carried.astype(BF16), back, preferred_element_type=F32)
    half = shares.shape[1]
    lev_parts = levels // half
    low = lane_of((half, LANES)) < LANES // 2
    for target in range(count):
        cell_tile, lev_part = target // lev_parts, target % lev_parts
        columns = slice((cell_tile // 2) * LANES, (cell_tile // 2 + 1) * LANES)
        air = carried[lev_part * half : (lev_part + 1) * half, columns]
        sea_part = carried[levels + lev_part * half : levels + (lev_part + 1) * half, columns]
        if cell_tile % 2:
            air = rolled(air, LANES // 2)
        else:
            sea_part = rolled(sea_part, LANES // 2)
        shares[target] = jnp.where(low, air, sea_part).astype(BF16)
    for slot in range(count):
        target = lax.rem(me + slot, count)
        span = pl.ds(pl.multiple_of(target * comps, 16), comps)
        out_refs[slot][:comps] = ordered[span, :LANES]
        out_refs[slot][comps : 2 * comps] = ordered[span, LANES:]
        out_refs[slot][2 * comps :] = shares[target]


def level_sign(levels, cells):
    return lax.broadcasted_iota(jnp.int32, (2 * levels, cells), 0) < levels


def finish_kernel(count, where_ref, calm_ref, *refs):
    in_refs, refs = refs[:count], refs[count:]
    energy_ref, air_ref, ocean_ref, pieces, wide, narrow = refs
    comps, rows, columns = energy_ref.shape
    levels, tile_rows, _ = air_ref.shape
    unit = columns // count
    me = where_ref[0]
    part = 16
    for slot in range(count):
        pieces[lax.rem(me - slot + count, count)] = in_refs[slot][...]

    @pl.loop(0, comps // part)
    def _(step):
        start = pl.multiple_of(step * part, part)
        for tile in range(rows // count):
            values = [
                pieces[source, pl.ds(tile * comps + start, part), :].astype(F32)
                for source in range(count)
            ]
            for row, value in enumerate(swapped_blocks(values, unit)):
                wide[pl.ds(start * rows + tile * count + row, part, stride=rows), :] = value
        span = pl.ds(pl.multiple_of(start * rows, part * rows), part * rows)
        energy_ref[pl.ds(start, part)] = (
            wide[span, :].reshape(part, rows, columns).astype(energy_ref.dtype)
        )

    for step in range(levels // part):
        values = [
            pieces[source, 2 * comps + step * part : 2 * comps + (step + 1) * part, :].astype(F32)
            for source in range(count)
        ]
        for index, value in enumerate(swapped_blocks(values, unit)):
            kind, row = divmod(index, tile_rows)
            start = (kind * levels + step * part) * tile_rows + row
            narrow[pl.ds(start, part, stride=tile_rows), :] = value
    size = levels * tile_rows
    air_ref[...] = calm_ref[0] + narrow[:size, :].reshape(air_ref.shape)
    ocean_ref[...] = calm_ref[1] + narrow[size:, :].reshape(ocean_ref.shape)


def beside_ends(block, axis, dim, width):
    count = lax.axis_size(axis)
    if count != 2:
        return extended_2(block, ((axis, dim),), width, False)
    low_end = lax.axis_index(axis) == 0
    head = lax.slice_in_dim(block, 0, width, axis=dim)
    tail = lax.slice_in_dim(block, block.shape[dim] - width, None, axis=dim)
    other = lax.ppermute(jnp.where(low_end, tail, head), axis, [(0, 1), (1, 0)])
    low = jnp.where(low_end, 0.0, other)
    high = jnp.where(low_end, other, 0.0)
    return jnp.concatenate([low, block, high], axis=dim)


def twice_relaxed(state):
    for axis, dim in (("lev", 1), ("cells", 2), ("sect", 3)):
        state = beside_ends(state, axis, dim, 2)
    state = relaxed(state, 1)
    for axis, dim in (("lev", 1), ("cells", 2), ("sect", 3)):
        place = lax.broadcasted_iota(jnp.int32, state.shape, dim)
        index = lax.axis_index(axis)
        outside = (index == 0) & (place == 0)
        outside |= (index == lax.axis_size(axis) - 1) & (place == state.shape[dim] - 1)
        state = jnp.where(outside, 0.0, state)
    return relaxed(state, 1)


def spread_out(pieces, axes, count):
    received = [pieces[0]]
    for shift in range(1, count):
        pairs = [(index, (index + shift) % count) for index in range(count)]
        received.append(lax.ppermute(pieces[shift], axes, pairs))
    return received


def by_columns(
    spectrum, courant_x, courant_y, growth, quartet, coupler, atmosphere, ocean_state, sea_mask
):
    axes = ("cells", "lev")
    count = lax.axis_size("cells") * lax.axis_size("lev")
    sects = lax.axis_size("sect")
    comps, rows, columns = spectrum.shape
    total = comps * count
    width = columns // count
    cells = rows * width
    levels_own, tile_rows, _ = atmosphere.shape
    groups = max(n for n in range(1, 5) if comps % (16 * n) == 0)
    me = lax.axis_index(axes)
    sect = lax.axis_index("sect")
    where = jnp.stack([me, sect * columns + me * width]).astype(jnp.int32)
    params = pltpu.CompilerParams(vmem_limit_bytes=40 * 1024 * 1024)
    whole = pl.BlockSpec(memory_space=VMEM)
    scalars = pl.BlockSpec(memory_space=pltpu.SMEM)

    surface = jnp.stack(
        [atmosphere[0] - ocean_state[0], atmosphere[1] - ocean_state[1], sea_mask.astype(F32)]
    )
    surface = lax.all_gather(surface, ("sect",) + axes)
    surface = surface.reshape(sects, lax.axis_size("cells"), lax.axis_size("lev"), 3, tile_rows, columns)
    surface = surface[:, :, 0].transpose(2, 1, 3, 0, 4).reshape(3 * rows, sects * columns)

    by_row, edge = pl.pallas_call(
        edges_kernel,
        out_shape=(
            jax.ShapeDtypeStruct((rows, comps, columns), BF16),
            jax.ShapeDtypeStruct((comps, LANES), BF16),
        ),
        in_specs=[whole],
        out_specs=(whole, whole),
        scratch_shapes=[VMEM((comps * rows, columns), F32)],
        compiler_params=params,
        name="edges",
    )(spectrum)
    forward = [(i, (i + 1) % sects) for i in range(sects)]
    backward = [(target, source) for source, target in forward]
    if sects == 2:
        halo = lax.ppermute(edge, "sect", forward)
    else:
        low = lax.ppermute(edge, "sect", forward)
        high = lax.ppermute(edge, "sect", backward)
        halo = jnp.concatenate([low[:, : LANES // 2], high[:, LANES // 2 :]], axis=1)

    column_x, column_y = courant_x[:, None], courant_y[:, None]
    piece = jax.ShapeDtypeStruct((2 * comps + comps // groups, LANES), BF16)
    pieces = pl.pallas_call(
        functools.partial(advect_kernel, groups, count),
        out_shape=(piece,) * count,
        in_specs=[scalars] + [whole] * 5,
        out_specs=(whole,) * count,
        scratch_shapes=[VMEM((count,) + piece.shape, BF16), VMEM((total, cells), BF16)],
        compiler_params=params,
        name="advect",
    )(where, by_row, edge, halo, column_x, column_y)
    received = spread_out(pieces, axes, count)

    factors = jnp.stack([growth, lax.all_gather(courant_x, axes, tiled=True), lax.all_gather(courant_y, axes, tiled=True)], axis=1)
    result = jax.ShapeDtypeStruct((2 * comps + levels_own, LANES), BF16)
    results = pl.pallas_call(
        functools.partial(steps_kernel, groups, count),
        out_shape=(result,) * count,
        in_specs=[scalars] + [whole] * (4 + count),
        out_specs=(whole,) * count,
        scratch_shapes=[
            VMEM((total, 6 * LANES), BF16),
            VMEM((total, 3 * LANES), BF16),
            VMEM((total, 4 * LANES), BF16),
            VMEM((total, cells), BF16),
            VMEM((total, cells), BF16),
            VMEM((count, levels_own, LANES), BF16),
        ],
        compiler_params=params,
        name="steps",
    )(where, quartet, coupler, factors, surface, *received)
    returned = spread_out(results, axes, count)

    state = jnp.stack([atmosphere, ocean_state])
    calm = twice_relaxed(state)
    return pl.pallas_call(
        functools.partial(finish_kernel, count),
        out_shape=(
            jax.ShapeDtypeStruct(spectrum.shape, spectrum.dtype),
            jax.ShapeDtypeStruct(atmosphere.shape, F32),
            jax.ShapeDtypeStruct(ocean_state.shape, F32),
        ),
        in_specs=[scalars] + [whole] * (1 + count),
        out_specs=(whole,) * 3,
        scratch_shapes=[
            VMEM((count,) + result.shape, BF16),
            VMEM((comps * rows, columns), F32),
            VMEM((2 * levels_own * tile_rows, columns), F32),
        ],
        compiler_params=params,
        name="finish",
    )(where, calm, *returned)


def on_device(spectrum, *rest):
    atmosphere = rest[5]
    blocks = lax.axis_size("cells") * lax.axis_size("lev")
    comps, rows, columns = spectrum.shape
    fits = (
        columns == LANES
        and blocks == 8
        and rows * (columns // blocks) == 2 * LANES
        and atmosphere.shape[1] * (columns // blocks) * 2 == LANES
        and comps % 16 == 0
        and atmosphere.shape[0] % 16 == 0
        and NSTEP == 2
    )
    return (by_columns if fits else any_shape)(spectrum, *rest)


def solution(mesh):
    in_specs = (
        P(("cells", "lev"), "groups", "sect"),
        P(("cells", "lev")),
        P(("cells", "lev")),
        P(),
        P(),
        P(),
        P("lev", ("groups", "cells"), "sect"),
        P("lev", ("groups", "cells"), "sect"),
        P(("groups", "cells"), "sect"),
    )
    out_specs = (
        P(("cells", "lev"), "groups", "sect"),
        P("lev", ("groups", "cells"), "sect"),
        P("lev", ("groups", "cells"), "sect"),
    )
    return jax.shard_map(
        on_device, mesh=mesh, in_specs=in_specs, out_specs=out_specs, check_vma=False
    )
```

```python
import functools

import jax
import jax.numpy as jnp
from jax import lax
from jax.experimental import pallas as pl
from jax.experimental.pallas import tpu as pltpu
from jax.sharding import PartitionSpec as P

NSTEP = 2
LANES = 128
F32 = jnp.float32
BF16 = jnp.bfloat16
VMEM = pltpu.VMEM


def from_root(block, axis, source):
    block = jnp.where(lax.axis_index(axis) == source, block, jnp.zeros_like(block))
    return lax.psum(block, axis)


def extended_2(block, sides, width, periodic):
    for axis, dim in sides:
        count = lax.axis_size(axis)
        forward = [(i, i + 1) for i in range(count - 1)]
        if periodic:
            forward.append((count - 1, 0))
        backward = [(target, source) for source, target in forward]
        low = lax.ppermute(
            lax.slice_in_dim(block, block.shape[dim] - width, None, axis=dim), axis, forward
        )
        high = lax.ppermute(lax.slice_in_dim(block, 0, width, axis=dim), axis, backward)
        block = jnp.concatenate([low, block, high], axis=dim)
    return block


def upwind(values, courant, before, after):
    return jnp.maximum(courant, 0.0) * (values - before) + jnp.minimum(courant, 0.0) * (
        after - values
    )


def any_shape(
    spectrum, courant_x, courant_y, growth, quartet, coupler, atmosphere, ocean_state, sea_mask
):
    cell_tiles = lax.axis_size("cells")
    lev_parts = lax.axis_size("lev")
    blocks = cell_tiles * lev_parts
    comps_own, rows_all, row_width = spectrum.shape
    total_comps = comps_own * blocks
    cell_rows = rows_all // blocks
    level_count = coupler.shape[0] // 2
    row_start = lax.axis_index("lev") * cell_rows
    shift_x = courant_x[:, None, None]
    shift_y = courant_y[:, None, None]
    sea_rows = (
        lax.dynamic_slice_in_dim(sea_mask, row_start, cell_rows, 0)
        .astype(jnp.float32)
        .reshape(1, cell_rows * row_width)
    )
    growth_column = growth[:, None]
    forcing_sign = jnp.array([-0.3, 0.3], jnp.float32)[:, None, None, None]
    state = jnp.stack([atmosphere, ocean_state])
    energy = spectrum
    for counter in range(NSTEP):
        surface = from_root(state[:, 0], "lev", 0)
        surface_wind = surface[0] - surface[1]
        wind_rows = lax.dynamic_slice_in_dim(
            surface_wind * surface_wind, row_start, cell_rows, 0
        ).reshape(1, cell_rows * row_width)
        padded = extended_2(energy, (("sect", 2),), 1, True)
        values = padded[:, :, 1:-1].astype(jnp.float32)
        west_side = padded[:, :, :-2].astype(jnp.float32)
        east_side = padded[:, :, 2:].astype(jnp.float32)
        moved = values - upwind(values, shift_x, west_side, east_side)
        moved = moved - upwind(
            values, shift_y, jnp.roll(values, 1, axis=1), jnp.roll(values, -1, axis=1)
        )
        advected = moved.astype(jnp.bfloat16)
        pieces = advected.reshape(1, comps_own, blocks, cell_rows, row_width)
        on_cells = lax.all_to_all(pieces, ("cells", "lev"), split_axis=2, concat_axis=0, tiled=True)
        on_cells = on_cells.reshape(total_comps, cell_rows * row_width)
        cell_values = on_cells.astype(jnp.float32)
        paired = jnp.dot(quartet, on_cells, preferred_element_type=jnp.float32)
        squared = (cell_values * cell_values).astype(jnp.bfloat16)
        quad_square = jnp.dot(quartet, squared, preferred_element_type=jnp.float32)
        fresh = (
            cell_values
            + 0.3 * (cell_values * paired - quad_square)
            + 0.1 * growth_column * wind_rows
        ) / (1.0 + 0.1 * cell_values * cell_values)
        fresh = (fresh * sea_rows).astype(jnp.bfloat16)
        profile = jnp.dot(coupler, fresh, preferred_element_type=jnp.float32).reshape(
            2, level_count, cell_rows, row_width
        )
        forcing = lax.all_to_all(profile, "lev", split_axis=1, concat_axis=2, tiled=True)
        returned = fresh.reshape(blocks, comps_own, 1, cell_rows, row_width)
        returned = lax.all_to_all(
            returned, ("cells", "lev"), split_axis=0, concat_axis=2, tiled=True
        )
        energy = returned.reshape(comps_own, rows_all, row_width)
        extended = extended_2(state, (("lev", 1), ("cells", 2), ("sect", 3)), 1, False)
        state = relaxed(extended, 1) + forcing_sign * forcing
    return (energy, state[0], state[1])


def relaxed(extended, first):
    centre = (slice(None),) * first + (slice(1, -1),) * 3
    middle = extended[centre]

    def moved(dim, start):
        where = list(centre)
        where[first + dim] = slice(start, extended.shape[first + dim] - 2 + start)
        return extended[tuple(where)]

    lateral = moved(1, 2) + moved(1, 0) + moved(2, 2) + moved(2, 0) - 4.0 * middle
    upright = moved(0, 2) + moved(0, 0) - 2.0 * middle
    return middle + 0.1 * lateral + 0.1 * upright


def lane_of(shape):
    return lax.broadcasted_iota(jnp.int32, shape, len(shape) - 1)


def rolled(values, shift):
    shift = shift % LANES
    return values if shift == 0 else pltpu.roll(values, shift, 1)


def swapped_blocks(values, unit):
    values = list(values)
    lane = lane_of(values[0].shape)
    step = 1
    while step < len(values):
        upper = (lane // (unit * step)) % 2 == 1
        for low in range(len(values)):
            if low & step:
                continue
            a, b = values[low], values[low | step]
            values[low] = jnp.where(upper, rolled(b, unit * step), a)
            values[low | step] = jnp.where(upper, b, rolled(a, -unit * step))
        step *= 2
    return values


def row_before(values, rows, periodic):
    lane = lane_of(values.shape) % rows
    wrap = rolled(values, 1 - rows) if periodic else 0.0
    return jnp.where(lane == 0, wrap, rolled(values, 1))


def row_after(values, rows, periodic):
    lane = lane_of(values.shape) % rows
    wrap = rolled(values, rows - 1) if periodic else 0.0
    return jnp.where(lane == rows - 1, wrap, rolled(values, -1))


def column_neighbours(first, second, outer, rows):
    lane = lane_of(first.shape)
    low, high = lane < rows, lane >= LANES - rows
    first_up, second_up = rolled(first, rows), rolled(second, rows)
    first_down, second_down = rolled(first, -rows), rolled(second, -rows)
    west = (jnp.where(low, outer, first_up), jnp.where(low, first_up, second_up))
    east = (jnp.where(high, second_down, first_down), jnp.where(high, outer, second_down))
    return west, east


def to_column_major(cells, rows, width):
    source = lax.broadcasted_iota(jnp.int32, (cells, cells), 0)
    target = lax.broadcasted_iota(jnp.int32, (cells, cells), 1)
    return ((target % rows) * width + target // rows == source).astype(BF16)


def to_row_major(cells, rows, width):
    source = lax.broadcasted_iota(jnp.int32, (cells, cells), 0)
    target = lax.broadcasted_iota(jnp.int32, (cells, cells), 1)
    return ((target % width) * rows + target // width == source).astype(BF16)


def split(values):
    head = values.astype(BF16).astype(F32)
    return head, values - head


def column_of(row, lanes):
    return jnp.transpose(jnp.broadcast_to(row, (lanes, row.shape[1])))


def edges_kernel(x_ref, air_ref, ocean_ref, sea_ref, by_row_ref, edge_ref, below_ref, wide):
    comps, rows, columns = x_ref.shape
    tile_rows = sea_ref.shape[0]
    wide[...] = x_ref[...].astype(F32).reshape(comps * rows, columns)
    column = lax.broadcasted_iota(jnp.int32, (columns, LANES), 0)
    lane = lax.broadcasted_iota(jnp.int32, (columns, LANES), 1)
    block = (lane // rows) % 4
    wanted = jnp.where(block < 2, columns - 2 + block, block - 2)
    total = jnp.zeros((comps, LANES), F32)
    for row in range(rows):
        values = wide[pl.ds(row, comps, stride=rows), :].astype(BF16)
        by_row_ref[row] = values
        pick = ((wanted == column) & (lane % rows == row)).astype(BF16)
        total += jnp.dot(values, pick, preferred_element_type=F32)
    edge_ref[:comps] = total.astype(BF16)
    owner = jnp.where(lax.axis_index("lev") == 0, 1.0, 0.0)
    head, tail = split((air_ref[0] - ocean_ref[0]) * owner)
    sea = sea_ref[...].astype(F32) * owner
    none = jnp.zeros_like(sea)
    edge_ref[comps:] = jnp.concatenate([head, tail, sea, none], axis=0).astype(BF16)
    head, tail = split((air_ref[1] - ocean_ref[1]) * owner)
    below_ref[...] = jnp.concatenate([head, tail, none, none], axis=0).astype(BF16)


def advect_kernel(
    groups, count, by_row_ref, edge_ref, below_ref, halo_ref, courant_x_ref, courant_y_ref, *refs
):
    out_refs, (packed, cell_major, cx_ref, cy_ref) = refs[:count], refs[count:]
    rows, comps, columns = by_row_ref.shape
    width = columns // count
    part = 16
    cx_ref[...] = column_of(courant_x_ref[...], LANES)
    cy_ref[...] = column_of(courant_y_ref[...], LANES)

    @pl.loop(0, comps // part)
    def _(step):
        start = pl.multiple_of(step * part, part)
        values = [by_row_ref[row, pl.ds(start, part), :].astype(F32) for row in range(rows)]
        cx = cx_ref[pl.ds(start, part), :]
        cy = cy_ref[pl.ds(start, part), :]
        moved = []
        for row in range(rows):
            here = values[row]
            along = upwind(here, cx, rolled(here, 1), rolled(here, -1))
            across = upwind(here, cy, values[row - 1], values[(row + 1) % rows])
            moved.append(here - along - across)
        for tile in range(rows // count):
            pieces = swapped_blocks(moved[tile * count : (tile + 1) * count], width)
            for target in range(count):
                cell_major[
                    pl.ds(pl.multiple_of(target * comps + start, part), part),
                    tile * LANES : (tile + 1) * LANES,
                ] = pieces[target].astype(BF16)

    change = to_column_major(rows * width, rows, width)
    lane = lane_of((comps, LANES))
    block = lane // rows
    halo = halo_ref[:comps].astype(F32)
    edge = edge_ref[:comps].astype(F32)
    near = jnp.where((block < 2) | (block >= 6), halo, edge)
    cx = cx_ref[...]
    cy = cy_ref[...]
    near = (
        near
        - upwind(near, cx, rolled(near, rows), rolled(near, -rows))
        - upwind(near, cy, row_before(near, rows, True), row_after(near, rows, True))
    )
    tiles = []
    for target in range(count):
        both = jnp.dot(
            cell_major[target * comps : (target + 1) * comps, :],
            change,
            preferred_element_type=F32,
        )
        tiles.append([both[:, :LANES], both[:, LANES:]])
    tiles[0][0] = jnp.where(block == 0, rolled(near, -2 * rows), tiles[0][0])
    tiles[-1][1] = jnp.where(block == 7, rolled(near, 2 * rows), tiles[-1][1])
    size = comps // groups
    me = lax.axis_index(("cells", "lev"))

    own = lane_of((size, LANES))
    riders = jnp.zeros((size, LANES), F32)
    for group in range(groups):
        span = slice(group * size, (group + 1) * size)
        for index, term in enumerate(split(cx[span]) + split(cy[span])):
            riders = jnp.where(own == 5 * rows + 4 * group + index, term, riders)

    tile_rows = 4
    cells = rows * width
    values = jnp.concatenate([edge_ref[comps:], below_ref[...]], axis=0)
    spot = lax.broadcasted_iota(jnp.int32, (columns, count * cells), 0)
    lanes = lax.broadcasted_iota(jnp.int32, (columns, count * cells), 1)
    repeat = (lanes // rows == spot).astype(BF16)
    inland = jnp.dot(values, repeat, preferred_element_type=F32)
    spot = lax.broadcasted_iota(jnp.int32, (columns, LANES), 0)
    lanes = lax.broadcasted_iota(jnp.int32, (columns, LANES), 1)
    repeat = ((lanes < rows) & (spot == columns - 1)) | ((lanes >= LANES - rows) & (spot == 0))
    coast = jnp.dot(halo_ref[comps:], repeat.astype(BF16), preferred_element_type=F32)
    coast = jnp.concatenate([coast, jnp.zeros_like(coast)], axis=0)
    first_row = lax.axis_index("cells") * tile_rows

    def gathered(values):
        place = lax.broadcasted_iota(jnp.int32, values.shape, 0)
        lanes = lane_of(values.shape)
        kept = jnp.where(lanes % rows == first_row + place % tile_rows, values, 0.0).astype(BF16)
        target = lax.broadcasted_iota(jnp.int32, (8, values.shape[0]), 0)
        source = lax.broadcasted_iota(jnp.int32, (8, values.shape[0]), 1) // tile_rows
        source = jnp.where(source < 3, source, jnp.where(source < 4, 7, source - 1))
        adds = (target == jnp.where(source < 5, source, 7)).astype(BF16)
        return jnp.dot(adds, kept, preferred_element_type=F32)

    inland, coast = gathered(inland), gathered(coast)
    place = lax.broadcasted_iota(jnp.int32, (8, LANES), 0)
    for target in range(count):
        tile = 2 * target
        winds = [inland[:, (tile + i) * LANES : (tile + i + 1) * LANES] for i in range(2)]
        before = coast
        if target:
            before = rolled(inland[:, (tile - 1) * LANES : tile * LANES], rows)
        after = coast
        if target < count - 1:
            after = rolled(inland[:, (tile + 2) * LANES : (tile + 3) * LANES], -rows)
        ends = jnp.where(lane_of(before.shape) < rows, before, after)
        winds[0] = jnp.where(place < 5, winds[0], pltpu.roll(ends, 5, 0))
        slot = lax.rem(target - me + count, count)
        packed[slot, 2 * comps + size :, :] = jnp.concatenate(winds, axis=0).astype(BF16)

    for target in range(count):
        west = rolled(tiles[target - 1][1], rows) if target else rolled(near, -rows)
        east = rolled(tiles[target + 1][0], -rows) if target < count - 1 else rolled(near, rows)
        outer = jnp.where(block == 0, west, east)
        shared = outer[:size]
        for group in range(1, groups):
            other = rolled(outer[group * size : (group + 1) * size], 2 * group * rows)
            own = lane_of(other.shape) // rows
            shared = jnp.where((own == 2 * group) | (own == 2 * group - 1), other, shared)
        own = lane_of(shared.shape) // rows
        shared = jnp.where((own == 5) | (own == 6), riders, shared)
        slot = lax.rem(target - me + count, count)
        packed[slot, :comps, :] = tiles[target][0].astype(BF16)
        packed[slot, comps : 2 * comps, :] = tiles[target][1].astype(BF16)
        packed[slot, 2 * comps : 2 * comps + size, :] = shared.astype(BF16)
    for slot in range(count):
        out_refs[slot][...] = packed[slot]


def steps_kernel(groups, count, rows, quartet_ref, coupler_ref, growth_ref, *refs):
    in_refs, refs = refs[:count], refs[count:]
    out_refs, refs = refs[:count], refs[count:]
    first_in, fresh, second_in, last, ordered, shares, factors = refs
    total = quartet_ref.shape[0]
    comps = total // count
    size = comps // groups
    cells = 2 * LANES
    wide = 3 * LANES
    width = cells // rows
    levels = coupler_ref.shape[0] // 2
    me = lax.axis_index(("cells", "lev"))
    west_end = (me == 0) & (lax.axis_index("sect") == 0)
    east_end = (me == count - 1) & (lax.axis_index("sect") == lax.axis_size("sect") - 1)
    factors[:, 8:16] = column_of(0.1 * growth_ref[...], 8)

    winds = jnp.zeros((16, LANES), F32)
    for slot in range(count):
        source = lax.rem(me - slot + count, count)
        start = pl.multiple_of(source * comps, 16)
        first_in[pl.ds(start, comps), :LANES] = in_refs[slot][:comps]
        first_in[pl.ds(start, comps), LANES:cells] = in_refs[slot][comps : 2 * comps]
        shared = in_refs[slot][2 * comps : 2 * comps + size].astype(F32)
        courant = shared + rolled(shared, -1)
        for group in range(groups):
            span = pl.ds(pl.multiple_of(start + group * size, 16), size)
            first_in[span, cells:wide] = rolled(shared, -2 * group * rows).astype(BF16)
            factors[span, :8] = rolled(courant, -5 * rows - 4 * group)[:, :8]
        winds += in_refs[slot][2 * comps + size :].astype(F32)

    first, second = winds[:8], winds[8:]
    outer = pltpu.roll(first, 3, 0)

    def joined(tile):
        return tile[:1] + tile[1:2]

    surface = jnp.concatenate([joined(first), joined(second), joined(outer)], axis=1)
    sea = jnp.concatenate([first[2:3], second[2:3], outer[2:3]], axis=1)
    below = jnp.concatenate([joined(first[3:5]), joined(second[3:5])], axis=1)
    wind = surface * surface

    def renew(values, products, growth, wind, sea):
        half = values.shape[1]
        paired, quad_square = products[:, :half], products[:, half:]
        below = 1.0 + 0.1 * values * values
        inverse = pl.reciprocal(below, approx=True)
        inverse = inverse * (2.0 - below * inverse)
        return (values + 0.3 * (values * paired - quad_square) + growth * wind) * inverse * sea

    part = total // 3
    for step in range(3):
        span = slice(step * part, (step + 1) * part)
        values = first_in[span, :wide].astype(F32)
        first_in[span, wide:] = (values * values).astype(BF16)

    @pl.loop(0, 3)
    def _(step):
        span = pl.ds(pl.multiple_of(step * part, part), part)
        products = jnp.dot(quartet_ref[span, :], first_in[...], preferred_element_type=F32)
        values = first_in[span, :wide].astype(F32)
        fresh[span, :] = renew(values, products, factors[span, 8:9], wind, sea).astype(BF16)

    level = lax.broadcasted_iota(jnp.int32, (2 * levels, wide), 0)
    forced = jnp.dot(coupler_ref[...], fresh[...], preferred_element_type=F32)
    forced = jnp.where(level < levels, -0.3, 0.3) * forced

    def beside(values):
        first, second = values[:, :LANES], values[:, LANES:cells]
        west, east = column_neighbours(first, second, values[:, cells:], rows)
        lane = lane_of(first.shape)
        west_edge = west_end & (lane < rows)
        east_edge = east_end & (lane >= LANES - rows)
        west = (jnp.where(west_edge, 0.0, west[0]), west[1])
        east = (east[0], jnp.where(east_edge, 0.0, east[1]))
        sums = [
            row_before(here, rows, False) + row_after(here, rows, False) + west[i] + east[i]
            for i, here in enumerate((first, second))
        ]
        return jnp.concatenate(sums, axis=1) - 4.0 * values[:, :cells]

    eight = jnp.broadcast_to(surface, (8, wide))
    calm = surface[:, :cells] + 0.1 * beside(eight)[:1]
    calm = calm + 0.1 * (below - 2.0 * surface[:, :cells])
    later = calm + forced[:1, :cells] - forced[levels : levels + 1, :cells]
    later = later * later
    middle = forced[:, :cells]
    level = level[:, :cells] % levels
    above = jnp.where(level == 0, 0.0, pltpu.roll(middle, 1, 0))
    under = jnp.where(level == levels - 1, 0.0, pltpu.roll(middle, 2 * levels - 1, 0))
    carried = middle + 0.1 * beside(forced) + 0.1 * (above + under - 2.0 * middle)


    @pl.loop(0, total // 32)
    def _(step):
        span = pl.ds(pl.multiple_of(step * 32, 32), 32)
        first = fresh[span, :LANES].astype(F32)
        second = fresh[span, LANES:cells].astype(F32)
        west, east = column_neighbours(first, second, fresh[span, cells:].astype(F32), rows)
        cx = jnp.broadcast_to(factors[span, 0:1], first.shape)
        cy = jnp.broadcast_to(factors[span, 2:3], first.shape)
        for i, here in enumerate((first, second)):
            moved = here - upwind(here, cx, west[i], east[i])
            moved = moved - upwind(
                here, cy, row_before(here, rows, True), row_after(here, rows, True)
            )
            moved = moved.astype(BF16)
            second_in[span, i * LANES : (i + 1) * LANES] = moved
            moved = moved.astype(F32)
            second_in[span, cells + i * LANES : cells + (i + 1) * LANES] = (moved * moved).astype(
                BF16
            )

    back = to_row_major(cells, rows, width)

    @pl.loop(0, 3)
    def _(step):
        span = pl.ds(pl.multiple_of(step * part, part), part)
        products = jnp.dot(quartet_ref[span, :], second_in[...], preferred_element_type=F32)
        values = second_in[span, :cells].astype(F32)
        done = renew(values, products, factors[span, 8:9], later, sea[:, :cells]).astype(BF16)
        last[span, :] = done
        ordered[span, :] = jnp.dot(done, back, preferred_element_type=F32).astype(BF16)

    forced = jnp.dot(coupler_ref[...], last[...], preferred_element_type=F32)
    carried = carried + jnp.where(level_sign(levels, cells), -0.3, 0.3) * forced
    carried = jnp.dot(carried.astype(BF16), back, preferred_element_type=F32)
    half = shares.shape[1]
    lev_parts = levels // half
    low = lane_of((half, LANES)) < LANES // 2
    for target in range(count):
        cell_tile, lev_part = target // lev_parts, target % lev_parts
        columns = slice((cell_tile // 2) * LANES, (cell_tile // 2 + 1) * LANES)
        air = carried[lev_part * half : (lev_part + 1) * half, columns]
        sea_part = carried[levels + lev_part * half : levels + (lev_part + 1) * half, columns]
        if cell_tile % 2:
            air = rolled(air, LANES // 2)
        else:
            sea_part = rolled(sea_part, LANES // 2)
        shares[target] = jnp.where(low, air, sea_part).astype(BF16)
    for slot in range(count):
        target = lax.rem(me + slot, count)
        span = pl.ds(pl.multiple_of(target * comps, 16), comps)
        out_refs[slot][:comps] = ordered[span, :LANES]
        out_refs[slot][comps : 2 * comps] = ordered[span, LANES:]
        out_refs[slot][2 * comps :] = shares[target]


def level_sign(levels, cells):
    return lax.broadcasted_iota(jnp.int32, (2 * levels, cells), 0) < levels


def finish_kernel(count, calm_ref, *refs):
    in_refs, refs = refs[:count], refs[count:]
    energy_ref, air_ref, ocean_ref, pieces, wide, narrow = refs
    comps, rows, columns = energy_ref.shape
    levels, tile_rows, _ = air_ref.shape
    unit = columns // count
    me = lax.axis_index(("cells", "lev"))
    part = 16
    for slot in range(count):
        pieces[lax.rem(me - slot + count, count)] = in_refs[slot][...]

    @pl.loop(0, comps // part)
    def _(step):
        start = pl.multiple_of(step * part, part)
        for tile in range(rows // count):
            values = [
                pieces[source, pl.ds(tile * comps + start, part), :].astype(F32)
                for source in range(count)
            ]
            for row, value in enumerate(swapped_blocks(values, unit)):
                wide[pl.ds(start * rows + tile * count + row, part, stride=rows), :] = value
        span = pl.ds(pl.multiple_of(start * rows, part * rows), part * rows)
        energy_ref[pl.ds(start, part)] = (
            wide[span, :].reshape(part, rows, columns).astype(energy_ref.dtype)
        )

    for step in range(levels // part):
        values = [
            pieces[source, 2 * comps + step * part : 2 * comps + (step + 1) * part, :].astype(F32)
            for source in range(count)
        ]
        for index, value in enumerate(swapped_blocks(values, unit)):
            kind, row = divmod(index, tile_rows)
            start = (kind * levels + step * part) * tile_rows + row
            narrow[pl.ds(start, part, stride=tile_rows), :] = value
    size = levels * tile_rows
    air_ref[...] = calm_ref[0] + narrow[:size, :].reshape(air_ref.shape)
    ocean_ref[...] = calm_ref[1] + narrow[size:, :].reshape(ocean_ref.shape)


def beside_ends(block, axis, dim, width):
    count = lax.axis_size(axis)
    if count != 2:
        return extended_2(block, ((axis, dim),), width, False)
    low_end = lax.axis_index(axis) == 0
    head = lax.slice_in_dim(block, 0, width, axis=dim)
    tail = lax.slice_in_dim(block, block.shape[dim] - width, None, axis=dim)
    other = lax.ppermute(jnp.where(low_end, tail, head), axis, [(0, 1), (1, 0)])
    low = jnp.where(low_end, 0.0, other)
    high = jnp.where(low_end, other, 0.0)
    return jnp.concatenate([low, block, high], axis=dim)


def twice_relaxed(state):
    for axis, dim in (("lev", 1), ("cells", 2), ("sect", 3)):
        state = beside_ends(state, axis, dim, 2)
    state = relaxed(state, 1)
    for axis, dim in (("lev", 1), ("cells", 2), ("sect", 3)):
        place = lax.broadcasted_iota(jnp.int32, state.shape, dim)
        index = lax.axis_index(axis)
        outside = (index == 0) & (place == 0)
        outside |= (index == lax.axis_size(axis) - 1) & (place == state.shape[dim] - 1)
        state = jnp.where(outside, 0.0, state)
    return relaxed(state, 1)


def spread_out(pieces, axes, count):
    received = [pieces[0]]
    for shift in range(1, count):
        pairs = [(index, (index + shift) % count) for index in range(count)]
        received.append(lax.ppermute(pieces[shift], axes, pairs))
    return received


def by_columns(
    spectrum, courant_x, courant_y, growth, quartet, coupler, atmosphere, ocean_state, sea_mask
):
    axes = ("cells", "lev")
    count = lax.axis_size("cells") * lax.axis_size("lev")
    sects = lax.axis_size("sect")
    comps, rows, columns = spectrum.shape
    total = comps * count
    width = columns // count
    cells = rows * width
    levels_own, tile_rows, _ = atmosphere.shape
    groups = 3 if comps % 48 == 0 else 2
    params = pltpu.CompilerParams(vmem_limit_bytes=40 * 1024 * 1024)
    whole = pl.BlockSpec(memory_space=VMEM)

    edge = jax.ShapeDtypeStruct((comps + 16, LANES), BF16)
    by_row, edge, below = pl.pallas_call(
        edges_kernel,
        out_shape=(
            jax.ShapeDtypeStruct((rows, comps, columns), BF16),
            edge,
            jax.ShapeDtypeStruct((16, LANES), BF16),
        ),
        in_specs=[whole] * 4,
        out_specs=(whole,) * 3,
        scratch_shapes=[VMEM((comps * rows, columns), F32)],
        compiler_params=params,
        name="edges",
    )(spectrum, atmosphere, ocean_state, sea_mask)
    halo = lax.ppermute(edge, "sect", [(0, 1), (1, 0)])

    piece = jax.ShapeDtypeStruct((2 * comps + comps // groups + 16, LANES), BF16)
    pieces = pl.pallas_call(
        functools.partial(advect_kernel, groups, count),
        out_shape=(piece,) * count,
        in_specs=[whole] * 6,
        out_specs=(whole,) * count,
        scratch_shapes=[
            VMEM((count,) + piece.shape, BF16),
            VMEM((total, cells), BF16),
            VMEM((comps, LANES), F32),
            VMEM((comps, LANES), F32),
        ],
        compiler_params=params,
        name="advect",
    )(by_row, edge, below, halo, courant_x[None], courant_y[None])
    received = spread_out(pieces, axes, count)

    result = jax.ShapeDtypeStruct((2 * comps + levels_own, LANES), BF16)
    results = pl.pallas_call(
        functools.partial(steps_kernel, groups, count, rows),
        out_shape=(result,) * count,
        in_specs=[whole] * (3 + count),
        out_specs=(whole,) * count,
        scratch_shapes=[
            VMEM((total, 6 * LANES), BF16),
            VMEM((total, 3 * LANES), BF16),
            VMEM((total, 4 * LANES), BF16),
            VMEM((total, cells), BF16),
            VMEM((total, cells), BF16),
            VMEM((count, levels_own, LANES), BF16),
            VMEM((total, LANES), F32),
        ],
        compiler_params=params,
        name="steps",
    )(quartet, coupler, growth[None], *received)
    returned = spread_out(results, axes, count)

    atmosphere, ocean_state, _ = lax.optimization_barrier((atmosphere, ocean_state, pieces[0]))
    calm = twice_relaxed(jnp.stack([atmosphere, ocean_state]))
    return pl.pallas_call(
        functools.partial(finish_kernel, count),
        out_shape=(
            jax.ShapeDtypeStruct(spectrum.shape, spectrum.dtype),
            jax.ShapeDtypeStruct(atmosphere.shape, F32),
            jax.ShapeDtypeStruct(ocean_state.shape, F32),
        ),
        in_specs=[whole] * (1 + count),
        out_specs=(whole,) * 3,
        scratch_shapes=[
            VMEM((count,) + result.shape, BF16),
            VMEM((comps * rows, columns), F32),
            VMEM((2 * levels_own * tile_rows, columns), F32),
        ],
        compiler_params=params,
        name="finish",
    )(calm, *returned)


def on_device(spectrum, *rest):
    atmosphere = rest[5]
    blocks = lax.axis_size("cells") * lax.axis_size("lev")
    comps, rows, columns = spectrum.shape
    fits = (
        columns == LANES
        and blocks == 8
        and lax.axis_size("sect") == 2
        and rows * (columns // blocks) == 2 * LANES
        and atmosphere.shape[1] * (columns // blocks) * 2 == LANES
        and any(comps % (16 * groups) == 0 for groups in (3, 2))
        and atmosphere.shape[0] % 16 == 0
        and NSTEP == 2
    )
    return (by_columns if fits else any_shape)(spectrum, *rest)


def solution(mesh):
    in_specs = (
        P(("cells", "lev"), "groups", "sect"),
        P(("cells", "lev")),
        P(("cells", "lev")),
        P(),
        P(),
        P(),
        P("lev", ("groups", "cells"), "sect"),
        P("lev", ("groups", "cells"), "sect"),
        P(("groups", "cells"), "sect"),
    )
    out_specs = (
        P(("cells", "lev"), "groups", "sect"),
        P("lev", ("groups", "cells"), "sect"),
        P("lev", ("groups", "cells"), "sect"),
    )
    return jax.shard_map(
        on_device, mesh=mesh, in_specs=in_specs, out_specs=out_specs, check_vma=False
    )
```

```python
import functools

import jax
import jax.numpy as jnp
from jax import lax
from jax.experimental import pallas as pl
from jax.experimental.pallas import tpu as pltpu
from jax.sharding import PartitionSpec as P

NSTEP = 2
LANES = 128
F32 = jnp.float32
BF16 = jnp.bfloat16
VMEM = pltpu.VMEM


def from_root(block, axis, source):
    block = jnp.where(lax.axis_index(axis) == source, block, jnp.zeros_like(block))
    return lax.psum(block, axis)


def extended_2(block, sides, width, periodic):
    for axis, dim in sides:
        count = lax.axis_size(axis)
        forward = [(i, i + 1) for i in range(count - 1)]
        if periodic:
            forward.append((count - 1, 0))
        backward = [(target, source) for source, target in forward]
        low = lax.ppermute(
            lax.slice_in_dim(block, block.shape[dim] - width, None, axis=dim), axis, forward
        )
        high = lax.ppermute(lax.slice_in_dim(block, 0, width, axis=dim), axis, backward)
        block = jnp.concatenate([low, block, high], axis=dim)
    return block


def upwind(values, courant, before, after):
    return jnp.maximum(courant, 0.0) * (values - before) + jnp.minimum(courant, 0.0) * (
        after - values
    )


def any_shape(
    spectrum, courant_x, courant_y, growth, quartet, coupler, atmosphere, ocean_state, sea_mask
):
    cell_tiles = lax.axis_size("cells")
    lev_parts = lax.axis_size("lev")
    blocks = cell_tiles * lev_parts
    comps_own, rows_all, row_width = spectrum.shape
    total_comps = comps_own * blocks
    cell_rows = rows_all // blocks
    level_count = coupler.shape[0] // 2
    row_start = lax.axis_index("lev") * cell_rows
    shift_x = courant_x[:, None, None]
    shift_y = courant_y[:, None, None]
    sea_rows = (
        lax.dynamic_slice_in_dim(sea_mask, row_start, cell_rows, 0)
        .astype(jnp.float32)
        .reshape(1, cell_rows * row_width)
    )
    growth_column = growth[:, None]
    forcing_sign = jnp.array([-0.3, 0.3], jnp.float32)[:, None, None, None]
    state = jnp.stack([atmosphere, ocean_state])
    energy = spectrum
    for counter in range(NSTEP):
        surface = from_root(state[:, 0], "lev", 0)
        surface_wind = surface[0] - surface[1]
        wind_rows = lax.dynamic_slice_in_dim(
            surface_wind * surface_wind, row_start, cell_rows, 0
        ).reshape(1, cell_rows * row_width)
        padded = extended_2(energy, (("sect", 2),), 1, True)
        values = padded[:, :, 1:-1].astype(jnp.float32)
        west_side = padded[:, :, :-2].astype(jnp.float32)
        east_side = padded[:, :, 2:].astype(jnp.float32)
        moved = values - upwind(values, shift_x, west_side, east_side)
        moved = moved - upwind(
            values, shift_y, jnp.roll(values, 1, axis=1), jnp.roll(values, -1, axis=1)
        )
        advected = moved.astype(jnp.bfloat16)
        pieces = advected.reshape(1, comps_own, blocks, cell_rows, row_width)
        on_cells = lax.all_to_all(pieces, ("cells", "lev"), split_axis=2, concat_axis=0, tiled=True)
        on_cells = on_cells.reshape(total_comps, cell_rows * row_width)
        cell_values = on_cells.astype(jnp.float32)
        paired = jnp.dot(quartet, on_cells, preferred_element_type=jnp.float32)
        squared = (cell_values * cell_values).astype(jnp.bfloat16)
        quad_square = jnp.dot(quartet, squared, preferred_element_type=jnp.float32)
        fresh = (
            cell_values
            + 0.3 * (cell_values * paired - quad_square)
            + 0.1 * growth_column * wind_rows
        ) / (1.0 + 0.1 * cell_values * cell_values)
        fresh = (fresh * sea_rows).astype(jnp.bfloat16)
        profile = jnp.dot(coupler, fresh, preferred_element_type=jnp.float32).reshape(
            2, level_count, cell_rows, row_width
        )
        forcing = lax.all_to_all(profile, "lev", split_axis=1, concat_axis=2, tiled=True)
        returned = fresh.reshape(blocks, comps_own, 1, cell_rows, row_width)
        returned = lax.all_to_all(
            returned, ("cells", "lev"), split_axis=0, concat_axis=2, tiled=True
        )
        energy = returned.reshape(comps_own, rows_all, row_width)
        extended = extended_2(state, (("lev", 1), ("cells", 2), ("sect", 3)), 1, False)
        state = relaxed(extended, 1) + forcing_sign * forcing
    return (energy, state[0], state[1])


def relaxed(extended, first):
    centre = (slice(None),) * first + (slice(1, -1),) * 3
    middle = extended[centre]

    def moved(dim, start):
        where = list(centre)
        where[first + dim] = slice(start, extended.shape[first + dim] - 2 + start)
        return extended[tuple(where)]

    lateral = moved(1, 2) + moved(1, 0) + moved(2, 2) + moved(2, 0) - 4.0 * middle
    upright = moved(0, 2) + moved(0, 0) - 2.0 * middle
    return middle + 0.1 * lateral + 0.1 * upright


def lane_of(shape):
    return lax.broadcasted_iota(jnp.int32, shape, len(shape) - 1)


def rolled(values, shift):
    shift = shift % LANES
    return values if shift == 0 else pltpu.roll(values, shift, 1)


def swapped_blocks(values, unit):
    values = list(values)
    lane = lane_of(values[0].shape)
    step = 1
    while step < len(values):
        upper = (lane // (unit * step)) % 2 == 1
        for low in range(len(values)):
            if low & step:
                continue
            a, b = values[low], values[low | step]
            values[low] = jnp.where(upper, rolled(b, unit * step), a)
            values[low | step] = jnp.where(upper, b, rolled(a, -unit * step))
        step *= 2
    return values


def row_before(values, rows, periodic):
    lane = lane_of(values.shape) % rows
    wrap = rolled(values, 1 - rows) if periodic else 0.0
    return jnp.where(lane == 0, wrap, rolled(values, 1))


def row_after(values, rows, periodic):
    lane = lane_of(values.shape) % rows
    wrap = rolled(values, rows - 1) if periodic else 0.0
    return jnp.where(lane == rows - 1, wrap, rolled(values, -1))


def column_neighbours(first, second, outer, rows):
    lane = lane_of(first.shape)
    low, high = lane < rows, lane >= LANES - rows
    first_up, second_up = rolled(first, rows), rolled(second, rows)
    first_down, second_down = rolled(first, -rows), rolled(second, -rows)
    west = (jnp.where(low, outer, first_up), jnp.where(low, first_up, second_up))
    east = (jnp.where(high, second_down, first_down), jnp.where(high, outer, second_down))
    return west, east


def to_column_major(cells, rows, width):
    source = lax.broadcasted_iota(jnp.int32, (cells, cells), 0)
    target = lax.broadcasted_iota(jnp.int32, (cells, cells), 1)
    return ((target % rows) * width + target // rows == source).astype(BF16)


def to_row_major(cells, rows, width):
    source = lax.broadcasted_iota(jnp.int32, (cells, cells), 0)
    target = lax.broadcasted_iota(jnp.int32, (cells, cells), 1)
    return ((target % width) * rows + target // width == source).astype(BF16)


def split(values):
    head = values.astype(BF16).astype(F32)
    return head, values - head


def column_of(row, lanes):
    return jnp.transpose(jnp.broadcast_to(row, (lanes, row.shape[1])))


def edges_kernel(
    x_hbm, air_hbm, ocean_hbm, sea_hbm, courant_x_hbm, courant_y_hbm,
    by_row_ref, edge_ref, below_ref, state_ref, courant_x_ref, courant_y_ref,
    x_ref, air_ref, ocean_ref, sea_ref, wide, sems,
):
    comps, rows, columns = x_ref.shape
    levels, tile_rows, _ = air_ref.shape
    copies = [
        pltpu.make_async_copy(source, target, sems.at[index])
        for index, (source, target) in enumerate(
            (
                (x_hbm, x_ref),
                (air_hbm, air_ref),
                (ocean_hbm, ocean_ref),
                (sea_hbm, sea_ref),
                (courant_x_hbm, courant_x_ref),
                (courant_y_hbm, courant_y_ref),
            )
        )
    ]
    for copy in copies:
        copy.start()
    column = lax.broadcasted_iota(jnp.int32, (columns, LANES), 0)
    lane = lax.broadcasted_iota(jnp.int32, (columns, LANES), 1)
    block = (lane // rows) % 4
    wanted = jnp.where(block < 2, columns - 2 + block, block - 2)
    total = jnp.zeros((comps, LANES), F32)
    copies[0].wait()
    wide[...] = x_ref[...].astype(F32).reshape(comps * rows, columns)
    for row in range(rows):
        values = wide[pl.ds(row, comps, stride=rows), :].astype(BF16)
        by_row_ref[row] = values
        pick = ((wanted == column) & (lane % rows == row)).astype(BF16)
        total += jnp.dot(values, pick, preferred_element_type=F32)
    edge_ref[:comps] = total.astype(BF16)
    for copy in copies[1:]:
        copy.wait()
    owner = jnp.where(lax.axis_index("lev") == 0, 1.0, 0.0)
    head, tail = split((air_ref[0] - ocean_ref[0]) * owner)
    sea = sea_ref[...].astype(F32) * owner
    none = jnp.zeros_like(sea)
    edge_ref[comps : comps + 16] = jnp.concatenate([head, tail, sea, none], axis=0).astype(BF16)
    head, tail = split((air_ref[1] - ocean_ref[1]) * owner)
    below_ref[...] = jnp.concatenate([head, tail, none, none], axis=0).astype(BF16)
    values = [ref[:, row, :] for ref in (air_ref, ocean_ref) for row in range(tile_rows)]
    unit = columns // len(values)
    values = swapped_blocks(values, unit)
    for target, value in enumerate(values):
        state_ref[target] = value.astype(BF16)
    inner = lane_of(values[0].shape) % unit
    ends = jnp.where(inner < 2, rolled(values[-1], 2 - unit), rolled(values[0], 2))
    edge_ref[comps + 16 :] = ends.astype(BF16)


def surface_rows(values, rows, tile_rows):
    first_row = lax.axis_index("cells") * tile_rows
    place = lax.broadcasted_iota(jnp.int32, values.shape, 0)
    kept = lane_of(values.shape) % rows == first_row + place % tile_rows
    kept = jnp.where(kept, values, 0.0).astype(BF16)
    target = lax.broadcasted_iota(jnp.int32, (8, values.shape[0]), 0)
    source = lax.broadcasted_iota(jnp.int32, (8, values.shape[0]), 1) // tile_rows
    source = jnp.where(source < 3, source, jnp.where(source < 4, 7, source - 1))
    adds = (target == jnp.where(source < 5, source, 7)).astype(BF16)
    return jnp.dot(adds, kept, preferred_element_type=F32)


def advect_kernel(
    groups, count, by_row_ref, edge_ref, below_ref, state_ref, courant_x_ref, courant_y_ref,
    packed_ref, cx_ref, cy_ref, cell_major,
):
    rows, comps, columns = by_row_ref.shape
    levels = state_ref.shape[1]
    width = columns // count
    part = 16
    cx_ref[...] = column_of(courant_x_ref[...], LANES)
    cy_ref[...] = column_of(courant_y_ref[...], LANES)

    @pl.loop(0, comps // part)
    def _(step):
        start = pl.multiple_of(step * part, part)
        values = [by_row_ref[row, pl.ds(start, part), :].astype(F32) for row in range(rows)]
        cx = cx_ref[pl.ds(start, part), :]
        cy = cy_ref[pl.ds(start, part), :]
        moved = []
        for row in range(rows):
            here = values[row]
            along = upwind(here, cx, rolled(here, 1), rolled(here, -1))
            across = upwind(here, cy, values[row - 1], values[(row + 1) % rows])
            moved.append(here - along - across)
        for tile in range(rows // count):
            pieces = swapped_blocks(moved[tile * count : (tile + 1) * count], width)
            for target in range(count):
                cell_major[
                    pl.ds(pl.multiple_of(target * comps + start, part), part),
                    tile * LANES : (tile + 1) * LANES,
                ] = pieces[target].astype(BF16)

    change = to_column_major(rows * width, rows, width)
    tiles = []
    for target in range(count):
        both = jnp.dot(
            cell_major[target * comps : (target + 1) * comps, :],
            change,
            preferred_element_type=F32,
        )
        tiles.append([both[:, :LANES], both[:, LANES:]])
    size = comps // groups
    block = lane_of((size, LANES)) // rows

    own = lane_of((size, LANES))
    riders = jnp.zeros((size, LANES), F32)
    for group in range(groups):
        span = slice(group * size, (group + 1) * size)
        for index, term in enumerate(split(cx_ref[span]) + split(cy_ref[span])):
            riders = jnp.where(own == 5 * rows + 4 * group + index, term, riders)

    cells = rows * width
    values = jnp.concatenate([edge_ref[comps : comps + 16], below_ref[...]], axis=0)
    spot = lax.broadcasted_iota(jnp.int32, (columns, count * cells), 0)
    lanes = lax.broadcasted_iota(jnp.int32, (columns, count * cells), 1)
    repeat = (lanes // rows == spot).astype(BF16)
    inland = jnp.dot(values, repeat, preferred_element_type=F32)
    inland = surface_rows(inland, rows, 4)
    place = lax.broadcasted_iota(jnp.int32, (8, LANES), 0)
    inner = lane_of((levels, LANES)) % width
    for target in range(count):
        left, right = max(target - 1, 0), min(target + 1, count - 1)
        packed_ref[target, :comps, :] = tiles[target][0].astype(BF16)
        packed_ref[target, comps : 2 * comps, :] = tiles[target][1].astype(BF16)

        west, east = tiles[left][1], tiles[right][0]
        shared = riders
        for group in range(groups):
            span = slice(group * size, (group + 1) * size)
            shared = jnp.where(
                block == 2 * group, rolled(west[span], (2 * group + 1) * rows), shared
            )
            shared = jnp.where(
                block == (2 * group - 1) % 8, rolled(east[span], (2 * group - 1) * rows), shared
            )
        packed_ref[target, 2 * comps : 2 * comps + size, :] = shared.astype(BF16)

        tile = 2 * target
        winds = [inland[:, (tile + i) * LANES : (tile + i + 1) * LANES] for i in range(2)]
        before = rolled(inland[:, (2 * left + 1) * LANES : (2 * left + 2) * LANES], rows)
        after = rolled(inland[:, 2 * right * LANES : (2 * right + 1) * LANES], -rows)
        ends = jnp.where(lane_of(before.shape) < rows, before, after)
        winds[0] = jnp.where(place < 5, winds[0], pltpu.roll(ends, 5, 0))
        start = 2 * comps + size
        packed_ref[target, start : start + 16, :] = jnp.concatenate(winds, axis=0).astype(BF16)

        start += 16
        packed_ref[target, start : start + levels, :] = state_ref[target]
        start += levels
        west, east = state_ref[left].astype(F32), state_ref[right].astype(F32)
        ends = jnp.where(inner < 2, rolled(west, 2 - width), rolled(east, 2))
        half = levels // 2
        ends = jnp.where(inner[:half] < 8, ends[:half], rolled(ends[half:], 8))
        packed_ref[target, start : start + half, :] = ends.astype(BF16)


def coast_kernel(groups, count, packed_ref, edge_ref, halo_ref, cx_ref, cy_ref, *refs):
    out_refs = refs
    comps = cx_ref.shape[0]
    size = comps // groups
    levels = halo_ref.shape[0] - comps - 16
    rows = 16
    unit = 16
    lane = lane_of((comps, LANES))
    block = lane // rows
    halo = halo_ref[:comps].astype(F32)
    edge = edge_ref[:comps].astype(F32)
    near = jnp.where((block < 2) | (block >= 6), halo, edge)
    cx, cy = cx_ref[...], cy_ref[...]
    near = (
        near
        - upwind(near, cx, rolled(near, rows), rolled(near, -rows))
        - upwind(near, cy, row_before(near, rows, True), row_after(near, rows, True))
    )
    spot = lax.broadcasted_iota(jnp.int32, (LANES, LANES), 0)
    lanes = lax.broadcasted_iota(jnp.int32, (LANES, LANES), 1)
    repeat = ((lanes < rows) & (spot == LANES - 1)) | ((lanes >= LANES - rows) & (spot == 0))
    values = halo_ref[comps : comps + 16]
    coast = jnp.dot(values, repeat.astype(BF16), preferred_element_type=F32)
    coast = surface_rows(jnp.concatenate([coast, jnp.zeros_like(coast)], axis=0), rows, 4)
    coast = pltpu.roll(coast, 5, 0)
    coast = jnp.concatenate([coast, jnp.zeros_like(coast)], axis=0)
    state = halo_ref[comps + 16 :].astype(F32)
    half = levels // 2
    inner = lane_of((half, LANES)) % unit
    state = jnp.where(inner < 8, state[:half], rolled(state[half:], 8))
    me = lax.axis_index(("cells", "lev"))
    for slot in range(count):
        target = lax.rem(me + slot, count)
        out_refs[slot][...] = packed_ref[target]
        place = lax.broadcasted_iota(jnp.int32, (16, LANES), 0)
        lane = lane_of((16, LANES))
        outer = (place >= 5) & (place < 8)

        def patch(start, stop, where, values):
            old = out_refs[slot][start:stop].astype(F32)
            out_refs[slot][start:stop] = jnp.where(where, values, old).astype(BF16)

        def patch_ends(first, shift, side, surface, own):
            own_block = lane_of((size, LANES)) // rows
            patch(first * comps, (first + 1) * comps, block == 7 * first, rolled(near, shift))
            shared = out_refs[slot][2 * comps : 2 * comps + size].astype(F32)
            for group in range(groups):
                there = (2 * group - first) % 8
                values = rolled(near[group * size : (group + 1) * size], (there - side) * rows)
                shared = jnp.where(own_block == there, values, shared)
            out_refs[slot][2 * comps : 2 * comps + size] = shared.astype(BF16)
            start = 2 * comps + size
            patch(start, start + 16, outer & surface, coast)
            start += 16 + levels
            patch(start, start + half, own, state)

        @pl.when(target == 0)
        def _():
            patch_ends(0, -2 * rows, 1, lane < rows, inner % 8 < 2)

        @pl.when(target == count - 1)
        def _():
            patch_ends(1, 2 * rows, 6, lane >= LANES - rows, inner % 8 >= 2)


def steps_kernel(groups, count, rows, quartet_ref, coupler_ref, growth_ref, *refs):
    in_refs, refs = refs[:count], refs[count:]
    out_refs, refs = refs[:count], refs[count:]
    first_in, fresh, second_in, last, ordered, shares, factors, state, ends = refs
    total = quartet_ref.shape[0]
    comps = total // count
    size = comps // groups
    cells = 2 * LANES
    wide = 3 * LANES
    width = cells // rows
    levels = coupler_ref.shape[0] // 2
    me = lax.axis_index(("cells", "lev"))
    west_end = (me == 0) & (lax.axis_index("sect") == 0)
    east_end = (me == count - 1) & (lax.axis_index("sect") == lax.axis_size("sect") - 1)
    factors[:, 8:16] = column_of(0.1 * growth_ref[...], 8)

    winds = jnp.zeros((16, LANES), F32)
    for slot in range(count):
        source = lax.rem(me - slot + count, count)
        start = pl.multiple_of(source * comps, 16)
        first_in[pl.ds(start, comps), :LANES] = in_refs[slot][:comps]
        first_in[pl.ds(start, comps), LANES:cells] = in_refs[slot][comps : 2 * comps]
        shared = in_refs[slot][2 * comps : 2 * comps + size].astype(F32)
        courant = shared + rolled(shared, -1)
        for group in range(groups):
            span = pl.ds(pl.multiple_of(start + group * size, 16), size)
            first_in[span, cells:wide] = rolled(shared, -2 * group * rows).astype(BF16)
            factors[span, :8] = rolled(courant, -5 * rows - 4 * group)[:, :8]
        place = 2 * comps + size
        winds += in_refs[slot][place : place + 16].astype(F32)
        place += 16
        half = shares.shape[1]
        state[source] = in_refs[slot][place : place + half]
        beside_state = in_refs[slot][place + half :].astype(F32)
        ends[source, : half // 2] = beside_state.astype(BF16)
        ends[source, half // 2 :] = rolled(beside_state, -8).astype(BF16)

    first, second = winds[:8], winds[8:]
    outer = pltpu.roll(first, 3, 0)

    def joined(tile):
        return tile[:1] + tile[1:2]

    surface = jnp.concatenate([joined(first), joined(second), joined(outer)], axis=1)
    sea = jnp.concatenate([first[2:3], second[2:3], outer[2:3]], axis=1)
    below = jnp.concatenate([joined(first[3:5]), joined(second[3:5])], axis=1)
    wind = surface * surface

    def renew(values, products, growth, wind, sea):
        half = values.shape[1]
        paired, quad_square = products[:, :half], products[:, half:]
        below = 1.0 + 0.1 * values * values
        inverse = pl.reciprocal(below, approx=True)
        inverse = inverse * (2.0 - below * inverse)
        return (values + 0.3 * (values * paired - quad_square) + growth * wind) * inverse * sea

    part = total // 3
    for step in range(3):
        span = slice(step * part, (step + 1) * part)
        values = first_in[span, :wide].astype(F32)
        first_in[span, wide:] = (values * values).astype(BF16)

    @pl.loop(0, 3)
    def _(step):
        span = pl.ds(pl.multiple_of(step * part, part), part)
        products = jnp.dot(quartet_ref[span, :], first_in[...], preferred_element_type=F32)
        values = first_in[span, :wide].astype(F32)
        fresh[span, :] = renew(values, products, factors[span, 8:9], wind, sea).astype(BF16)

    lev_parts = levels // half
    low = lane_of((half, LANES)) < LANES // 2

    def collected(source_ref):
        fields = []
        for kind in range(2):
            for part in range(lev_parts):
                tiles = []
                for pair in range(count // lev_parts // 2):
                    left = source_ref[2 * pair * lev_parts + part].astype(F32)
                    right = source_ref[(2 * pair + 1) * lev_parts + part].astype(F32)
                    if kind == 0:
                        right = rolled(right, LANES // 2)
                    else:
                        left = rolled(left, LANES // 2)
                    tiles.append(jnp.where(low, left, right))
                fields.append(jnp.concatenate(tiles, axis=1))
        return jnp.concatenate(fields, axis=0).astype(BF16)

    inner = jnp.dot(
        collected(state), to_column_major(cells, rows, width), preferred_element_type=F32
    )
    source = lax.broadcasted_iota(jnp.int32, (cells, cells), 0)
    target = lax.broadcasted_iota(jnp.int32, (cells, cells), 1)
    order = jnp.where(
        target < LANES,
        jnp.where(target < rows, 1, 2),
        jnp.where(target < LANES + rows, 0, 3),
    )
    blocks = (target % LANES) // rows
    spread = (source == (target % rows) * width + order) & ((blocks == 0) | (blocks == 7))
    outer = jnp.dot(collected(ends), spread.astype(BF16), preferred_element_type=F32)
    lane = lane_of((2 * levels, LANES))
    outside = (west_end & (lane < rows)) | (east_end & (lane >= LANES - rows))
    fields = [inner[:, :LANES], inner[:, LANES:], outer[:, :LANES], outer[:, LANES:]]
    fields[2:] = [jnp.where(outside, 0.0, field) for field in fields[2:]]
    level = lax.broadcasted_iota(jnp.int32, (2 * levels, LANES), 0) % levels

    def relaxed_tile(here, west, east):
        lateral = row_before(here, rows, False) + row_after(here, rows, False)
        lateral = lateral + west + east - 4.0 * here
        above = jnp.where(level == 0, 0.0, pltpu.roll(here, 1, 0))
        under = jnp.where(level == levels - 1, 0.0, pltpu.roll(here, 2 * levels - 1, 0))
        return here + 0.1 * lateral + 0.1 * (above + under - 2.0 * here)

    sign = jnp.where(
        lax.broadcasted_iota(jnp.int32, (2 * levels, LANES), 0) < levels, -0.3, 0.3
    )
    forced = jnp.dot(coupler_ref[...], fresh[...], preferred_element_type=F32)
    forced = [forced[:, i * LANES : (i + 1) * LANES] * sign for i in range(3)]
    west, east = column_neighbours(fields[0], fields[1], fields[2], rows)
    block = lane // rows
    later_fields = [relaxed_tile(fields[i], west[i], east[i]) + forced[i] for i in range(2)]
    beyond = relaxed_tile(
        fields[2],
        jnp.where(block == 7, fields[1], fields[3]),
        jnp.where(block == 0, fields[0], fields[3]),
    )
    beyond = jnp.where(outside, 0.0, beyond + forced[2])
    west, east = column_neighbours(later_fields[0], later_fields[1], beyond, rows)
    fields = [relaxed_tile(later_fields[i], west[i], east[i]) for i in range(2)]

    def beside(values):
        first, second, outer = values
        west, east = column_neighbours(first, second, outer, rows)
        lane = lane_of(first.shape)
        west = (jnp.where(west_end & (lane < rows), 0.0, west[0]), west[1])
        east = (east[0], jnp.where(east_end & (lane >= LANES - rows), 0.0, east[1]))
        sums = [
            row_before(here, rows, False)
            + row_after(here, rows, False)
            + west[i]
            + east[i]
            - 4.0 * here
            for i, here in enumerate((first, second))
        ]
        return jnp.concatenate(sums, axis=1)

    eight = [
        jnp.broadcast_to(surface[:, i * LANES : (i + 1) * LANES], (8, LANES)) for i in range(3)
    ]
    calm = surface[:, :cells] + 0.1 * beside(eight)[:1]
    calm = calm + 0.1 * (below - 2.0 * surface[:, :cells])
    later = [
        calm[:, i * LANES : (i + 1) * LANES] + forced[i][:1] - forced[i][levels : levels + 1]
        for i in range(2)
    ]
    later = jnp.concatenate([values * values for values in later], axis=1)


    @pl.loop(0, total // 32)
    def _(step):
        span = pl.ds(pl.multiple_of(step * 32, 32), 32)
        first = fresh[span, :LANES].astype(F32)
        second = fresh[span, LANES:cells].astype(F32)
        west, east = column_neighbours(first, second, fresh[span, cells:].astype(F32), rows)
        cx = jnp.broadcast_to(factors[span, 0:1], first.shape)
        cy = jnp.broadcast_to(factors[span, 2:3], first.shape)
        for i, here in enumerate((first, second)):
            moved = here - upwind(here, cx, west[i], east[i])
            moved = moved - upwind(
                here, cy, row_before(here, rows, True), row_after(here, rows, True)
            )
            moved = moved.astype(BF16)
            second_in[span, i * LANES : (i + 1) * LANES] = moved
            moved = moved.astype(F32)
            second_in[span, cells + i * LANES : cells + (i + 1) * LANES] = (moved * moved).astype(
                BF16
            )

    back = to_row_major(cells, rows, width)

    @pl.loop(0, 3)
    def _(step):
        span = pl.ds(pl.multiple_of(step * part, part), part)
        products = jnp.dot(quartet_ref[span, :], second_in[...], preferred_element_type=F32)
        values = second_in[span, :cells].astype(F32)
        done = renew(values, products, factors[span, 8:9], later, sea[:, :cells]).astype(BF16)
        last[span, :] = done
        ordered[span, :] = jnp.dot(done, back, preferred_element_type=F32).astype(BF16)

    forced = jnp.dot(coupler_ref[...], last[...], preferred_element_type=F32)
    carried = jnp.concatenate(
        [fields[i] + sign * forced[:, i * LANES : (i + 1) * LANES] for i in range(2)], axis=1
    )
    carried = jnp.dot(carried.astype(BF16), back, preferred_element_type=F32)
    for target in range(count):
        cell_tile, lev_part = target // lev_parts, target % lev_parts
        columns = slice((cell_tile // 2) * LANES, (cell_tile // 2 + 1) * LANES)
        air = carried[lev_part * half : (lev_part + 1) * half, columns]
        sea_part = carried[levels + lev_part * half : levels + (lev_part + 1) * half, columns]
        if cell_tile % 2:
            air = rolled(air, LANES // 2)
        else:
            sea_part = rolled(sea_part, LANES // 2)
        shares[target] = jnp.where(low, air, sea_part).astype(BF16)
    for slot in range(count):
        target = lax.rem(me + slot, count)
        span = pl.ds(pl.multiple_of(target * comps, 16), comps)
        out_refs[slot][:comps] = ordered[span, :LANES]
        out_refs[slot][comps : 2 * comps] = ordered[span, LANES:]
        out_refs[slot][2 * comps :] = shares[target]


def finish_kernel(count, *refs):
    in_refs, refs = refs[:count], refs[count:]
    energy_ref, air_ref, ocean_ref, pieces, wide, narrow = refs
    comps, rows, columns = energy_ref.shape
    levels, tile_rows, _ = air_ref.shape
    unit = columns // count
    me = lax.axis_index(("cells", "lev"))
    part = 16
    for slot in range(count):
        pieces[lax.rem(me - slot + count, count)] = in_refs[slot][...]

    @pl.loop(0, comps // part)
    def _(step):
        start = pl.multiple_of(step * part, part)
        for tile in range(rows // count):
            values = [
                pieces[source, pl.ds(tile * comps + start, part), :].astype(F32)
                for source in range(count)
            ]
            for row, value in enumerate(swapped_blocks(values, unit)):
                wide[pl.ds(start * rows + tile * count + row, part, stride=rows), :] = value
        span = pl.ds(pl.multiple_of(start * rows, part * rows), part * rows)
        energy_ref[pl.ds(start, part)] = (
            wide[span, :].reshape(part, rows, columns).astype(energy_ref.dtype)
        )

    for step in range(levels // part):
        values = [
            pieces[source, 2 * comps + step * part : 2 * comps + (step + 1) * part, :].astype(F32)
            for source in range(count)
        ]
        for index, value in enumerate(swapped_blocks(values, unit)):
            kind, row = divmod(index, tile_rows)
            start = (kind * levels + step * part) * tile_rows + row
            narrow[pl.ds(start, part, stride=tile_rows), :] = value
    size = levels * tile_rows
    air_ref[...] = narrow[:size, :].reshape(air_ref.shape)
    ocean_ref[...] = narrow[size:, :].reshape(ocean_ref.shape)


def spread_out(pieces, axes, count):
    received = [pieces[0]]
    for shift in range(1, count):
        pairs = [(index, (index + shift) % count) for index in range(count)]
        received.append(lax.ppermute(pieces[shift], axes, pairs))
    return received


def by_columns(
    spectrum, courant_x, courant_y, growth, quartet, coupler, atmosphere, ocean_state, sea_mask
):
    axes = ("cells", "lev")
    count = lax.axis_size("cells") * lax.axis_size("lev")
    sects = lax.axis_size("sect")
    comps, rows, columns = spectrum.shape
    total = comps * count
    width = columns // count
    cells = rows * width
    levels_own, tile_rows, _ = atmosphere.shape
    groups = 3 if comps % 48 == 0 else 2
    whole = pl.BlockSpec(memory_space=VMEM)
    far = pl.BlockSpec(memory_space=pltpu.HBM)

    def shape(*dims, kind=BF16):
        return jax.ShapeDtypeStruct(dims, kind)

    def call(kernel, outs, *args, kept=(), specs=None, flops=0, mega=16):
        return pl.pallas_call(
            kernel,
            out_shape=outs,
            in_specs=specs or [whole] * len(args),
            out_specs=jax.tree.map(lambda _: whole, outs),
            scratch_shapes=list(kept),
            compiler_params=pltpu.CompilerParams(vmem_limit_bytes=mega * 1024 * 1024),
            cost_estimate=pl.CostEstimate(flops=flops, bytes_accessed=4000000, transcendentals=0),
        )(*args)

    row = shape(1, comps, kind=F32)
    by_row, edge, below, state, row_x, row_y = call(
        edges_kernel,
        (
            shape(rows, comps, columns),
            shape(comps + 16 + levels_own, LANES),
            shape(16, LANES),
            shape(count, levels_own, LANES),
            row,
            row,
        ),
        spectrum,
        atmosphere,
        ocean_state,
        sea_mask,
        courant_x[None],
        courant_y[None],
        specs=[far] * 6,
        kept=[
            VMEM(spectrum.shape, BF16),
            VMEM(atmosphere.shape, F32),
            VMEM(ocean_state.shape, F32),
            VMEM(sea_mask.shape, sea_mask.dtype),
            VMEM((comps * rows, columns), F32),
            pltpu.SemaphoreType.DMA((6,)),
        ],
    )
    halo = lax.ppermute(edge, "sect", [(0, 1), (1, 0)])

    size = 2 * comps + comps // groups + 16 + levels_own + levels_own // 2
    factor = shape(comps, LANES, kind=F32)
    packed, factor_x, factor_y = call(
        functools.partial(advect_kernel, groups, count),
        (shape(count, size, LANES), factor, factor),
        by_row,
        edge,
        below,
        state,
        row_x,
        row_y,
        kept=[VMEM((total, cells), BF16)],
        flops=2000000000,
    )
    pieces = call(
        functools.partial(coast_kernel, groups, count),
        (shape(size, LANES),) * count,
        packed,
        edge,
        halo,
        factor_x,
        factor_y,
    )
    received = spread_out(pieces, axes, count)

    results = call(
        functools.partial(steps_kernel, groups, count, rows),
        (shape(2 * comps + levels_own, LANES),) * count,
        quartet,
        coupler,
        growth[None],
        *received,
        kept=[
            VMEM((total, 6 * LANES), BF16),
            VMEM((total, 3 * LANES), BF16),
            VMEM((total, 4 * LANES), BF16),
            VMEM((total, cells), BF16),
            VMEM((total, cells), BF16),
            VMEM((count, levels_own, LANES), BF16),
            VMEM((total, LANES), F32),
            VMEM((count, levels_own, LANES), BF16),
            VMEM((count, levels_own, LANES), BF16),
        ],
        mega=32,
    )
    returned = spread_out(results, axes, count)

    return call(
        functools.partial(finish_kernel, count),
        (
            shape(*spectrum.shape),
            shape(*atmosphere.shape, kind=F32),
            shape(*ocean_state.shape, kind=F32),
        ),
        *returned,
        kept=[
            VMEM((count, 2 * comps + levels_own, LANES), BF16),
            VMEM((comps * rows, columns), F32),
            VMEM((2 * levels_own * tile_rows, columns), F32),
        ],
    )


def on_device(spectrum, *rest):
    atmosphere = rest[5]
    blocks = lax.axis_size("cells") * lax.axis_size("lev")
    comps, rows, columns = spectrum.shape
    fits = (
        columns == LANES
        and blocks == 8
        and lax.axis_size("sect") == 2
        and rows * (columns // blocks) == 2 * LANES
        and atmosphere.shape[1] * (columns // blocks) * 2 == LANES
        and any(comps % (16 * groups) == 0 for groups in (3, 2))
        and atmosphere.shape[0] % 16 == 0
        and NSTEP == 2
    )
    return (by_columns if fits else any_shape)(spectrum, *rest)


def solution(mesh):
    in_specs = (
        P(("cells", "lev"), "groups", "sect"),
        P(("cells", "lev")),
        P(("cells", "lev")),
        P(),
        P(),
        P(),
        P("lev", ("groups", "cells"), "sect"),
        P("lev", ("groups", "cells"), "sect"),
        P(("groups", "cells"), "sect"),
    )
    out_specs = (
        P(("cells", "lev"), "groups", "sect"),
        P("lev", ("groups", "cells"), "sect"),
        P("lev", ("groups", "cells"), "sect"),
    )
    return jax.shard_map(
        on_device, mesh=mesh, in_specs=in_specs, out_specs=out_specs, check_vma=False
    )
```

```python
import functools

import jax
import jax.numpy as jnp
import numpy as np
from jax import lax
from jax.experimental import pallas as pl
from jax.experimental.pallas import tpu as pltpu
from jax.sharding import PartitionSpec as P

NSTEP = 2
LANES = 128
F32 = jnp.float32
BF16 = jnp.bfloat16
VMEM = pltpu.VMEM


def from_root(block, axis, source):
    block = jnp.where(lax.axis_index(axis) == source, block, jnp.zeros_like(block))
    return lax.psum(block, axis)


def extended_2(block, sides, width, periodic):
    for axis, dim in sides:
        count = lax.axis_size(axis)
        forward = [(i, i + 1) for i in range(count - 1)]
        if periodic:
            forward.append((count - 1, 0))
        backward = [(target, source) for source, target in forward]
        low = lax.ppermute(
            lax.slice_in_dim(block, block.shape[dim] - width, None, axis=dim), axis, forward
        )
        high = lax.ppermute(lax.slice_in_dim(block, 0, width, axis=dim), axis, backward)
        block = jnp.concatenate([low, block, high], axis=dim)
    return block


def upwind(values, courant, before, after):
    return jnp.maximum(courant, 0.0) * (values - before) + jnp.minimum(courant, 0.0) * (
        after - values
    )


def any_shape(
    spectrum, courant_x, courant_y, growth, quartet, coupler, atmosphere, ocean_state, sea_mask
):
    cell_tiles = lax.axis_size("cells")
    lev_parts = lax.axis_size("lev")
    blocks = cell_tiles * lev_parts
    comps_own, rows_all, row_width = spectrum.shape
    total_comps = comps_own * blocks
    cell_rows = rows_all // blocks
    level_count = coupler.shape[0] // 2
    row_start = lax.axis_index("lev") * cell_rows
    shift_x = courant_x[:, None, None]
    shift_y = courant_y[:, None, None]
    sea_rows = (
        lax.dynamic_slice_in_dim(sea_mask, row_start, cell_rows, 0)
        .astype(jnp.float32)
        .reshape(1, cell_rows * row_width)
    )
    growth_column = growth[:, None]
    forcing_sign = jnp.array([-0.3, 0.3], jnp.float32)[:, None, None, None]
    state = jnp.stack([atmosphere, ocean_state])
    energy = spectrum
    for counter in range(NSTEP):
        surface = from_root(state[:, 0], "lev", 0)
        surface_wind = surface[0] - surface[1]
        wind_rows = lax.dynamic_slice_in_dim(
            surface_wind * surface_wind, row_start, cell_rows, 0
        ).reshape(1, cell_rows * row_width)
        padded = extended_2(energy, (("sect", 2),), 1, True)
        values = padded[:, :, 1:-1].astype(jnp.float32)
        west_side = padded[:, :, :-2].astype(jnp.float32)
        east_side = padded[:, :, 2:].astype(jnp.float32)
        moved = values - upwind(values, shift_x, west_side, east_side)
        moved = moved - upwind(
            values, shift_y, jnp.roll(values, 1, axis=1), jnp.roll(values, -1, axis=1)
        )
        advected = moved.astype(jnp.bfloat16)
        pieces = advected.reshape(1, comps_own, blocks, cell_rows, row_width)
        on_cells = lax.all_to_all(pieces, ("cells", "lev"), split_axis=2, concat_axis=0, tiled=True)
        on_cells = on_cells.reshape(total_comps, cell_rows * row_width)
        cell_values = on_cells.astype(jnp.float32)
        paired = jnp.dot(quartet, on_cells, preferred_element_type=jnp.float32)
        squared = (cell_values * cell_values).astype(jnp.bfloat16)
        quad_square = jnp.dot(quartet, squared, preferred_element_type=jnp.float32)
        fresh = (
            cell_values
            + 0.3 * (cell_values * paired - quad_square)
            + 0.1 * growth_column * wind_rows
        ) / (1.0 + 0.1 * cell_values * cell_values)
        fresh = (fresh * sea_rows).astype(jnp.bfloat16)
        profile = jnp.dot(coupler, fresh, preferred_element_type=jnp.float32).reshape(
            2, level_count, cell_rows, row_width
        )
        forcing = lax.all_to_all(profile, "lev", split_axis=1, concat_axis=2, tiled=True)
        returned = fresh.reshape(blocks, comps_own, 1, cell_rows, row_width)
        returned = lax.all_to_all(
            returned, ("cells", "lev"), split_axis=0, concat_axis=2, tiled=True
        )
        energy = returned.reshape(comps_own, rows_all, row_width)
        extended = extended_2(state, (("lev", 1), ("cells", 2), ("sect", 3)), 1, False)
        state = relaxed(extended, 1) + forcing_sign * forcing
    return (energy, state[0], state[1])


def relaxed(extended, first):
    centre = (slice(None),) * first + (slice(1, -1),) * 3
    middle = extended[centre]

    def moved(dim, start):
        where = list(centre)
        where[first + dim] = slice(start, extended.shape[first + dim] - 2 + start)
        return extended[tuple(where)]

    lateral = moved(1, 2) + moved(1, 0) + moved(2, 2) + moved(2, 0) - 4.0 * middle
    upright = moved(0, 2) + moved(0, 0) - 2.0 * middle
    return middle + 0.1 * lateral + 0.1 * upright


def iota(shape, dim):
    return lax.broadcasted_iota(jnp.int32, shape, dim)


def over(values, unit):
    return values >> (unit.bit_length() - 1)


def within(values, unit):
    return values & (unit - 1)


def moved(values, matrix):
    return jnp.dot(values.astype(BF16), matrix, preferred_element_type=F32)


def split(values):
    head = values.astype(BF16).astype(F32)
    return head, values - head


def column_of(row, lanes):
    return jnp.transpose(jnp.broadcast_to(row, (lanes, row.shape[1])))


def swap_matrix(count, unit):
    index = np.arange(count * count * unit)
    a, b, i = index // (count * unit), index // unit % count, index % unit
    return index[:, None] == ((b * count + a) * unit + i)[None, :]


def neighbour_matrices(rows, width):
    cells = rows * width
    row, column = np.divmod(np.arange(cells), width)
    west = np.where(column > 0, row * width + column - 1, cells + row)
    east = np.where(
        column < width - 1, row * width + column + 1, cells + LANES - rows + row
    )
    north = (row - 1) % rows * width + column
    south = (row + 1) % rows * width + column
    source = np.arange(cells + LANES)[:, None]
    return np.concatenate([source == move[None, :] for move in (west, east, north, south)], axis=1)


def lateral_matrix(rows, width):
    cells = rows * width
    far_west, west, east, far_east = cells + LANES, cells, cells + LANES - rows, cells + 2 * LANES - rows
    place = {}
    for row in range(rows):
        for column in range(width):
            place[row, column] = row * width + column
        for column, start in ((-2, far_west), (-1, west), (width, east), (width + 1, far_east)):
            place[row, column] = start + row
    matrix = np.zeros((cells + 2 * LANES, cells + LANES), bool)
    for (row, column), target in place.items():
        if not -1 <= column <= width:
            continue
        for near in ((row - 1, column), (row + 1, column), (row, column - 1), (row, column + 1)):
            if near in place:
                matrix[place[near], target] = True
    return matrix


def edges_kernel(
    x_hbm, air_hbm, ocean_hbm, sea_hbm, courant_x_hbm, courant_y_hbm,
    by_row_ref, edge_ref, below_ref, state_ref, courant_x_ref, courant_y_ref,
    x_ref, air_ref, ocean_ref, sea_ref, wide, sems,
):
    comps, rows, columns = x_ref.shape
    levels, tile_rows, _ = air_ref.shape
    copies = [
        pltpu.make_async_copy(source, target, sems.at[index])
        for index, (source, target) in enumerate(
            (
                (x_hbm, x_ref),
                (air_hbm, air_ref),
                (ocean_hbm, ocean_ref),
                (sea_hbm, sea_ref),
                (courant_x_hbm, courant_x_ref),
                (courant_y_hbm, courant_y_ref),
            )
        )
    ]
    for copy in copies:
        copy.start()
    column, lane = iota((columns, LANES), 0), iota((columns, LANES), 1)

    block = within(over(lane, rows), 4)
    wanted = jnp.where(block < 2, columns - 2 + block, block - 2) == column
    row_of_lane = within(lane, rows)
    total = jnp.zeros((comps, LANES), F32)
    copies[0].wait()
    wide[...] = x_ref[...].astype(F32).reshape(comps * rows, columns)
    for row in range(rows):
        values = wide[pl.ds(row, comps, stride=rows), :].astype(BF16)
        by_row_ref[row] = values
        total += moved(values, (wanted & (row_of_lane == row)).astype(BF16))
    edge_ref[:comps] = total.astype(BF16)
    for copy in copies[1:]:
        copy.wait()
    owner = jnp.where(lax.axis_index("lev") == 0, 1.0, 0.0)
    head, tail = split((air_ref[0] - ocean_ref[0]) * owner)
    sea = sea_ref[...].astype(F32) * owner
    none = jnp.zeros_like(sea)
    edge_ref[comps : comps + 16] = jnp.concatenate([head, tail, sea, none], axis=0).astype(BF16)
    head, tail = split((air_ref[1] - ocean_ref[1]) * owner)
    below_ref[...] = jnp.concatenate([head, tail, none, none], axis=0).astype(BF16)

    values = [ref[:, row, :] for ref in (air_ref, ocean_ref) for row in range(tile_rows)]
    unit = columns // len(values)
    inner = within(lane, unit)
    wanted = (jnp.where(inner < 2, columns - 2 + inner, inner - 2) == column) & (inner < 4)
    total = jnp.zeros((levels, LANES), F32)
    for index, value in enumerate(values):
        value = value.astype(BF16)
        state_ref[:, index * columns : (index + 1) * columns] = value
        total += moved(value, (wanted & (over(lane, unit) == index)).astype(BF16))
    edge_ref[comps + 16 :] = total.astype(BF16)


def surface_rows(values, row_of_lane, tile_rows):
    first_row = lax.axis_index("cells") * tile_rows
    kept = row_of_lane == first_row + within(iota(values.shape, 0), tile_rows)
    kept = jnp.where(kept, values, 0.0).astype(BF16)
    target = iota((8, values.shape[0]), 0)
    source = over(iota((8, values.shape[0]), 1), tile_rows)
    source = jnp.where(source < 3, source, jnp.where(source < 4, 7, source - 1))
    adds = (target == jnp.where(source < 5, source, 7)).astype(BF16)
    return jnp.dot(adds, kept, preferred_element_type=F32)


def advect_kernel(
    groups, count, by_row_ref, edge_ref, below_ref, state_ref, courant_x_ref, courant_y_ref, swap_ref,
    packed_ref, cx_ref, cy_ref, gathered,
):
    rows, comps, columns = by_row_ref.shape
    levels = state_ref.shape[0]
    width = columns // count
    cells = rows * width
    cx_ref[...] = column_of(courant_x_ref[...], LANES)
    cy_ref[...] = column_of(courant_y_ref[...], LANES)
    source, target = iota((columns, 2 * columns), 0), iota((columns, 2 * columns), 1)
    step = jnp.where(target < columns, -1, 1)
    sides = (source == within(target + step, columns)).astype(BF16)
    for row in range(rows):
        here = by_row_ref[row].astype(F32)
        beside = moved(by_row_ref[row], sides)
        along = upwind(here, cx_ref[...], beside[:, :columns], beside[:, columns:])
        across = upwind(
            here,
            cy_ref[...],
            by_row_ref[row - 1 if row else rows - 1].astype(F32),
            by_row_ref[row + 1 if row < rows - 1 else 0].astype(F32),
        )
        tile, place = divmod(row, count)
        gathered[tile * comps : (tile + 1) * comps, place * columns : (place + 1) * columns] = (
            here - along - across
        ).astype(BF16)
    gathered[2 * comps :, :] = state_ref[...]
    for target in range(count // 2):
        lanes = slice(2 * target * LANES, 2 * (target + 1) * LANES)
        values = moved(gathered[...], swap_ref[:, lanes]).astype(BF16)
        for side in range(2):
            half = values[:, side * LANES : (side + 1) * LANES]
            packed_ref[2 * target + side, : 2 * comps, :] = half[: 2 * comps]
            start = 2 * comps + comps // groups + 16
            packed_ref[2 * target + side, start : start + levels, :] = half[2 * comps :]
    size = comps // groups

    own = iota((size, LANES), 1)
    riders = jnp.zeros((size, LANES), F32)
    for group in range(groups):
        span = slice(group * size, (group + 1) * size)
        for index, term in enumerate(split(cx_ref[span]) + split(cy_ref[span])):
            riders = jnp.where(own == 5 * rows + 4 * group + index, term, riders)

    values = jnp.concatenate([edge_ref[comps : comps + 16], below_ref[...]], axis=0)
    spot, lanes = iota((columns, count * cells), 0), iota((columns, count * cells), 1)
    repeat = spot == over(lanes, cells) * width + within(lanes, width)
    inland = moved(values, repeat.astype(BF16))
    inland = surface_rows(inland, over(within(iota(inland.shape, 1), cells), width), 4)
    spot, lanes = iota((columns, count * LANES), 0), iota((columns, count * LANES), 1)
    first = over(lanes, LANES) * width
    lanes = within(lanes, LANES)
    repeat = ((lanes < rows) & (spot == first - 1)) | (
        (lanes >= LANES - rows) & (spot == first + width)
    )
    shore = moved(values, repeat.astype(BF16))
    shore = surface_rows(shore, within(iota(shore.shape, 1), rows), 4)
    place = iota((8, LANES), 0)

    source, target_lane = iota((cells, 2 * LANES), 0), iota((cells, 2 * LANES), 1)
    block = over(within(target_lane, LANES), rows)
    row_start = within(target_lane, rows) * width
    ends = []
    for group in range(groups):
        west = (target_lane < LANES) & (block == 2 * group) & (source == row_start + width - 1)
        east = (target_lane >= LANES) & (block == (2 * group + 7) % 8) & (source == row_start)
        ends.append((west | east).astype(BF16))
    source, target_lane = iota((LANES, 2 * LANES), 0), iota((LANES, 2 * LANES), 1)
    inner = within(target_lane, width)
    back = (target_lane - inner) & (LANES - 1)
    shifts = []
    for start in (0, 8):
        west = (target_lane < LANES) & (inner >= start) & (inner < start + 2)
        west = west & (source == back + width - 2 + inner - start)
        east = (target_lane >= LANES) & (inner >= start + 2) & (inner < start + 4)
        east = east & (source == back + inner - start - 2)
        shifts.append((west | east).astype(BF16))
    beside, beside_state = [], []
    half = levels // 2
    for target in range(count):
        total = jnp.zeros((size, 2 * LANES), F32)
        for group in range(groups):
            for tile in range(2):
                span = slice(tile * comps + group * size, tile * comps + (group + 1) * size)
                rows_of = slice(tile * LANES, (tile + 1) * LANES)
                total += moved(packed_ref[target, span, :], ends[group][rows_of])
        beside.append(total)
        start = 2 * comps + size + 16
        low = moved(packed_ref[target, start : start + half, :], shifts[0])
        high = moved(packed_ref[target, start + half : start + levels, :], shifts[1])
        beside_state.append(low + high)
    for target in range(count):
        left, right = max(target - 1, 0), min(target + 1, count - 1)
        shared = riders + beside[left][:, :LANES] + beside[right][:, LANES:]
        packed_ref[target, 2 * comps : 2 * comps + size, :] = shared.astype(BF16)
        winds = [inland[:, (2 * target + i) * LANES : (2 * target + i + 1) * LANES] for i in range(2)]
        outer = pltpu.roll(shore[:, target * LANES : (target + 1) * LANES], 5, 0)
        winds[0] = jnp.where(place < 5, winds[0], outer)
        start = 2 * comps + size
        packed_ref[target, start : start + 16, :] = jnp.concatenate(winds, axis=0).astype(BF16)
        start += 16 + levels
        outer = beside_state[left][:, :LANES] + beside_state[right][:, LANES:]
        packed_ref[target, start : start + half, :] = outer.astype(BF16)


def coast_kernel(groups, count, rows, packed_ref, edge_ref, halo_ref, cx_ref, cy_ref, *out_refs):
    comps = cx_ref.shape[0]
    size = comps // groups
    levels = halo_ref.shape[0] - comps - 16
    cells = 2 * LANES
    width = cells // rows
    half = levels // 2
    block = over(iota((comps, LANES), 1), rows)
    near = jnp.where((block < 2) | (block >= 6), halo_ref[:comps], edge_ref[:comps])
    source, target = iota((LANES, 4 * LANES), 0), iota((LANES, 4 * LANES), 1)
    lane = within(target, LANES)
    row = within(lane, rows)
    kind = over(target, LANES)
    shift = jnp.where(
        kind == 0,
        within(lane - rows, LANES),
        jnp.where(
            kind == 1,
            within(lane + rows, LANES),
            lane - row + within(row + jnp.where(kind == 2, -1, 1), rows),
        ),
    )
    four = moved(near, (source == shift).astype(BF16))
    near = near.astype(F32)
    near = (
        near
        - upwind(near, cx_ref[...], four[:, :LANES], four[:, LANES : 2 * LANES])
        - upwind(near, cy_ref[...], four[:, 2 * LANES : 3 * LANES], four[:, 3 * LANES :])
    )
    source, target = iota((LANES, cells), 0), iota((LANES, cells), 1)
    column, row = within(target, width), over(target, width)
    spread = ((column == 0) & (source == 2 * rows + row)) | (
        (column == width - 1) & (source == 5 * rows + row)
    )
    ends = moved(near, spread.astype(BF16))
    shared = jnp.zeros((size, LANES), F32)
    source, target = iota((LANES, LANES), 0), iota((LANES, LANES), 1)
    for group in range(groups):
        there = over(target, rows)
        from_block = jnp.where(
            there == 2 * group, 1, jnp.where(there == (2 * group + 7) % 8, 6, LANES)
        )
        spread = source == from_block * rows + within(target, rows)
        shared += moved(near[group * size : (group + 1) * size], spread.astype(BF16))
    repeat = ((target < rows) & (source == LANES - 1)) | ((target >= LANES - rows) & (source == 0))
    coast = moved(halo_ref[comps : comps + 16], repeat.astype(BF16))
    coast = jnp.concatenate([coast, jnp.zeros_like(coast)], axis=0)
    coast = surface_rows(coast, within(iota(coast.shape, 1), rows), 4)
    coast = pltpu.roll(coast, 5, 0)
    coast = jnp.concatenate([coast, jnp.zeros_like(coast)], axis=0)
    inner = within(target, width)
    low = (source == target) & (inner < 4)
    high = (source == target - 8) & (inner >= 8) & (inner < 12)
    state = moved(halo_ref[comps + 16 : comps + 16 + half], low.astype(BF16))
    state += moved(halo_ref[comps + 16 + half :], high.astype(BF16))
    me = lax.axis_index(("cells", "lev"))
    for slot in range(count):
        target = lax.rem(me + slot, count)
        out_refs[slot][...] = packed_ref[target]
        place, lane = iota((16, LANES), 0), iota((16, LANES), 1)
        outer = (place >= 5) & (place < 8)

        def patch(start, stop, where, values):
            old = out_refs[slot][start:stop].astype(F32)
            out_refs[slot][start:stop] = jnp.where(where, values, old).astype(BF16)

        def patch_ends(east):
            column = within(iota((comps, LANES), 1), width)
            for tile in range(2):
                values = ends[:, tile * LANES : (tile + 1) * LANES]
                where = column == (width - 1 if east else 0)
                patch(tile * comps, (tile + 1) * comps, where, values)
            own = over(iota((size, LANES), 1), rows)
            where = own < 0
            for group in range(groups):
                where = where | (own == ((2 * group + 7) % 8 if east else 2 * group))
            patch(2 * comps, 2 * comps + size, where, shared)
            start = 2 * comps + size
            side = lane >= LANES - rows if east else lane < rows
            patch(start, start + 16, outer & side, coast)
            start += 16 + levels
            inner = within(iota((half, LANES), 1), 8)
            patch(start, start + half, (inner >= 2) == east, state)

        @pl.when(target == 0)
        def _():
            patch_ends(False)

        @pl.when(target == count - 1)
        def _():
            patch_ends(True)


def steps_kernel(
    groups, count, rows, quartet_ref, coupler_ref, growth_ref, beside_ref, lateral_ref, *refs
):
    in_refs, refs = refs[:count], refs[count:]
    out_refs, refs = refs[:count], refs[count:]
    first_in, fresh, second_in, last, shares, factors, state, ends = refs
    total = quartet_ref.shape[0]
    comps = total // count
    size = comps // groups
    cells = 2 * LANES
    wide = 3 * LANES
    width = cells // rows
    levels = coupler_ref.shape[0] // 2
    half = shares.shape[1]
    me = lax.axis_index(("cells", "lev"))
    west_end = (me == 0) & (lax.axis_index("sect") == 0)
    east_end = (me == count - 1) & (lax.axis_index("sect") == lax.axis_size("sect") - 1)
    factors[:, 8:16] = column_of(0.1 * growth_ref[...], 8)

    source, target = iota((LANES, 2 * LANES), 0), iota((LANES, 2 * LANES), 1)
    block = over(target, rows)
    opened = []
    for group in range(groups):
        from_block = jnp.where(
            block == 0, 2 * group, jnp.where(block == 7, (2 * group + 7) % 8, LANES)
        )
        column = source == from_block * rows + within(target, rows)
        rider = source - (5 * rows + 4 * group)
        rider = (rider >= 0) & (rider < 4) & (over(rider, 2) == target - LANES)
        opened.append((column | rider).astype(BF16))
    winds = jnp.zeros((16, LANES), F32)
    for slot in range(count):
        source = lax.rem(me - slot + count, count)
        start = pl.multiple_of(source * comps, 16)
        span = pl.ds(start, comps)
        for tile in range(2):
            values = in_refs[slot][tile * comps : (tile + 1) * comps]
            first_in[span, tile * LANES : (tile + 1) * LANES] = values
            values = values.astype(F32)
            first_in[span, wide + tile * LANES : wide + (tile + 1) * LANES] = (
                values * values
            ).astype(BF16)
        for group in range(groups):
            span = pl.ds(pl.multiple_of(start + group * size, 16), size)
            values = moved(in_refs[slot][2 * comps : 2 * comps + size], opened[group])
            first_in[span, cells:wide] = values[:, :LANES].astype(BF16)
            values_8 = values[:, LANES : LANES + 8]
            values = values[:, :LANES]
            first_in[span, wide + cells :] = (values * values).astype(BF16)
            factors[span, :8] = values_8
        place = 2 * comps + size
        winds += in_refs[slot][place : place + 16].astype(F32)
        place += 16
        state[source] = in_refs[slot][place : place + half]
        ends[source] = in_refs[slot][place + half :]

    first, second = winds[:8], winds[8:]
    outer = pltpu.roll(first, 3, 0)

    def joined(tile):
        return tile[:1] + tile[1:2]

    surface = jnp.concatenate([joined(first), joined(second), joined(outer)], axis=1)
    terms = jnp.concatenate([first, second, outer], axis=1)
    sea = terms[2:3]
    below = jnp.concatenate([joined(first[3:5]), joined(second[3:5])], axis=1)
    wind = surface * surface

    def renew(values, products, growth, wind, sea):
        half = values.shape[1]
        paired, quad_square = products[:, :half], products[:, half:]
        below = 1.0 + 0.1 * values * values
        inverse = pl.reciprocal(below, approx=True)
        inverse = inverse * (2.0 - below * inverse)
        return (values + 0.3 * (values * paired - quad_square) + growth * wind) * inverse * sea

    part = total // 2
    for step in range(2):
        span = slice(step * part, (step + 1) * part)
        products = jnp.dot(quartet_ref[span, :], first_in[...], preferred_element_type=F32)
        values = first_in[span, :wide].astype(F32)
        fresh[span, :] = renew(values, products, factors[span, 8:9], wind, sea).astype(BF16)
    part = total // 8
    for step in range(8):
        span = slice(step * part, (step + 1) * part)
        beside = jnp.dot(fresh[span, :], beside_ref[...], preferred_element_type=F32)
        here = fresh[span, :cells].astype(F32)
        cx = jnp.broadcast_to(factors[span, 0:1], here.shape)
        cy = jnp.broadcast_to(factors[span, 1:2], here.shape)
        values = (
            here
            - upwind(here, cx, beside[:, :cells], beside[:, cells : 2 * cells])
            - upwind(here, cy, beside[:, 2 * cells : 3 * cells], beside[:, 3 * cells :])
        ).astype(BF16)
        second_in[span, :cells] = values
        values = values.astype(F32)
        second_in[span, cells:] = (values * values).astype(BF16)

    lev_parts = levels // half
    halves = iota((half, LANES), 1) < LANES // 2

    def collected(values):
        fields = []
        for kind in range(2):
            for part in range(lev_parts):
                tiles = []
                for pair in range(count // lev_parts // 2):
                    left = values[2 * pair * lev_parts + part].astype(F32)
                    right = values[(2 * pair + 1) * lev_parts + part].astype(F32)
                    if kind == 0:
                        right = pltpu.roll(right, LANES // 2, 1)
                    else:
                        left = pltpu.roll(left, LANES // 2, 1)
                    tiles.append(jnp.where(halves[: left.shape[0]], left, right))
                fields.append(jnp.concatenate(tiles, axis=1))
        return fields

    inner = jnp.concatenate(collected(state), axis=0)
    source, target = iota((cells, cells), 0), iota((cells, cells), 1)
    far = over(target, LANES)
    block = over(within(target, LANES), rows)
    order = jnp.where(block == 0, jnp.where(far == 0, 1, 0), jnp.where(far == 0, 2, 3))
    used = (block == 0) | (block == 7)
    spread = [
        ((source == within(target, rows) * width + order + 8 * high) & used).astype(BF16)
        for high in range(2)
    ]
    outer = []
    for field in collected(ends):
        outer += [moved(field, spread[0]), moved(field, spread[1])]
    outer = jnp.concatenate(outer, axis=0)

    def bounded(values):
        lane = iota(values.shape, 1)
        outside = (west_end & (lane < rows)) | (east_end & (lane >= LANES - rows))
        return jnp.where(outside, 0.0, values)

    outer = [bounded(outer[:, :LANES]), bounded(outer[:, LANES:])]

    def relaxed_once(here, lateral):
        level = within(iota(here.shape, 0), levels)
        lateral = lateral - 4.0 * here
        above = jnp.where(level == 0, 0.0, pltpu.roll(here, 1, 0))
        under = jnp.where(level == levels - 1, 0.0, pltpu.roll(here, 2 * levels - 1, 0))
        return here + 0.1 * lateral + 0.1 * (above + under - 2.0 * here)

    sign = jnp.where(iota((2 * levels, 1), 0) < levels, -0.3, 0.3)
    forced = jnp.dot(coupler_ref[...], fresh[...], preferred_element_type=F32) * sign
    here = jnp.concatenate([inner] + outer, axis=1)
    fields = relaxed_once(here[:, :wide], moved(here, lateral_ref[...])) + forced
    fields = jnp.concatenate([fields[:, :cells], bounded(fields[:, cells:])], axis=1)
    near = lateral_ref[:wide, :cells]
    head, tail = split(fields)
    fields = relaxed_once(fields[:, :cells], moved(head, near) + moved(tail, near))

    terms = jnp.concatenate([terms[:, :cells], bounded(terms[:, cells:])], axis=1)
    lateral = joined(moved(terms, near))
    calm = surface[:, :cells]
    calm = calm + 0.1 * (lateral - 4.0 * calm) + 0.1 * (below - 2.0 * calm)
    later = calm + forced[:1, :cells] - forced[levels : levels + 1, :cells]
    later = later * later

    part = total // 2
    for step in range(2):
        span = slice(step * part, (step + 1) * part)
        products = jnp.dot(quartet_ref[span, :], second_in[...], preferred_element_type=F32)
        values = second_in[span, :cells].astype(F32)
        done = renew(values, products, factors[span, 8:9], later, sea[:, :cells])
        last[span, :] = done.astype(BF16)

    forced = jnp.dot(coupler_ref[...], last[...], preferred_element_type=F32)
    carried = fields + sign * forced
    for target in range(count):
        cell_tile, lev_part = target // lev_parts, target % lev_parts
        columns = slice((cell_tile // 2) * LANES, (cell_tile // 2 + 1) * LANES)
        air = carried[lev_part * half : (lev_part + 1) * half, columns]
        sea_part = carried[levels + lev_part * half : levels + (lev_part + 1) * half, columns]
        if cell_tile % 2:
            air = pltpu.roll(air, LANES // 2, 1)
        else:
            sea_part = pltpu.roll(sea_part, LANES // 2, 1)
        shares[target] = jnp.where(halves, air, sea_part).astype(BF16)
    for slot in range(count):
        target = lax.rem(me + slot, count)
        span = pl.ds(pl.multiple_of(target * comps, 16), comps)
        out_refs[slot][:comps] = last[span, :LANES]
        out_refs[slot][comps : 2 * comps] = last[span, LANES:]
        out_refs[slot][2 * comps :] = shares[target]


def finish_kernel(count, swap_ref, *refs):
    in_refs, refs = refs[:count], refs[count:]
    energy_ref, air_ref, ocean_ref, gathered, wide, narrow = refs
    comps, rows, columns = energy_ref.shape
    levels, tile_rows, _ = air_ref.shape
    me = lax.axis_index(("cells", "lev"))
    for slot in range(count):
        source = lax.rem(me - slot + count, count)
        gathered[:, pl.ds(pl.multiple_of(source * columns, columns), columns)] = in_refs[slot][...]
    for pair in range(count // 2):
        lanes = slice(2 * pair * columns, 2 * (pair + 1) * columns)
        values = moved(gathered[...], swap_ref[:, lanes])
        for side in range(2):
            index = 2 * pair + side
            part = values[:, side * columns : (side + 1) * columns]
            for tile in range(rows // count):
                wide[pl.ds(tile * count + index, comps, stride=rows), :] = part[
                    tile * comps : (tile + 1) * comps
                ]
            kind, row = divmod(index, tile_rows)
            narrow[pl.ds(kind * levels * tile_rows + row, levels, stride=tile_rows), :] = part[
                2 * comps :
            ]
    energy_ref[...] = wide[...].reshape(comps, rows, columns).astype(energy_ref.dtype)
    size = levels * tile_rows
    air_ref[...] = narrow[:size, :].reshape(air_ref.shape)
    ocean_ref[...] = narrow[size:, :].reshape(ocean_ref.shape)


def spread_out(pieces, axes, count):
    received = [pieces[0]]
    for shift in range(1, count):
        pairs = [(index, (index + shift) % count) for index in range(count)]
        received.append(lax.ppermute(pieces[shift], axes, pairs))
    return received


def by_columns(
    spectrum, courant_x, courant_y, growth, quartet, coupler, atmosphere, ocean_state, sea_mask
):
    axes = ("cells", "lev")
    count = lax.axis_size("cells") * lax.axis_size("lev")
    sects = lax.axis_size("sect")
    comps, rows, columns = spectrum.shape
    total = comps * count
    width = columns // count
    cells = rows * width
    levels_own, tile_rows, _ = atmosphere.shape
    groups = 3 if comps % 48 == 0 else 2
    whole = pl.BlockSpec(memory_space=VMEM)
    far = pl.BlockSpec(memory_space=pltpu.HBM)

    def shape(*dims, kind=BF16):
        return jax.ShapeDtypeStruct(dims, kind)

    def call(kernel, outs, *args, kept=(), specs=None, flops=0, mega=16):
        return pl.pallas_call(
            kernel,
            out_shape=outs,
            in_specs=specs or [whole] * len(args),
            out_specs=jax.tree.map(lambda _: whole, outs),
            scratch_shapes=list(kept),
            compiler_params=pltpu.CompilerParams(vmem_limit_bytes=mega * 1024 * 1024),
            cost_estimate=pl.CostEstimate(flops=flops, bytes_accessed=4000000, transcendentals=0),
        )(*args)

    swap = jnp.asarray(swap_matrix(count, width), BF16)
    row = shape(1, comps, kind=F32)
    by_row, edge, below, state, row_x, row_y = call(
        edges_kernel,
        (
            shape(rows, comps, columns),
            shape(comps + 16 + levels_own, LANES),
            shape(16, LANES),
            shape(levels_own, count * columns),
            row,
            row,
        ),
        spectrum,
        atmosphere,
        ocean_state,
        sea_mask,
        courant_x[None],
        courant_y[None],
        specs=[far] * 6,
        kept=[
            VMEM(spectrum.shape, BF16),
            VMEM(atmosphere.shape, F32),
            VMEM(ocean_state.shape, F32),
            VMEM(sea_mask.shape, sea_mask.dtype),
            VMEM((comps * rows, columns), F32),
            pltpu.SemaphoreType.DMA((6,)),
        ],
    )
    halo = lax.ppermute(edge, "sect", [(0, 1), (1, 0)])

    size = 2 * comps + comps // groups + 16 + levels_own + levels_own // 2
    factor = shape(comps, LANES, kind=F32)
    packed, factor_x, factor_y = call(
        functools.partial(advect_kernel, groups, count),
        (shape(count, size, LANES), factor, factor),
        by_row,
        edge,
        below,
        state,
        row_x,
        row_y,
        swap,
        kept=[VMEM((2 * comps + levels_own, count * columns), BF16)],
        flops=2000000000,
    )
    pieces = call(
        functools.partial(coast_kernel, groups, count, rows),
        (shape(size, LANES),) * count,
        packed,
        edge,
        halo,
        factor_x,
        factor_y,
    )
    received = spread_out(pieces, axes, count)

    results = call(
        functools.partial(steps_kernel, groups, count, rows),
        (shape(2 * comps + levels_own, LANES),) * count,
        quartet,
        coupler,
        growth[None],
        jnp.asarray(neighbour_matrices(rows, width), BF16),
        jnp.asarray(lateral_matrix(rows, width), BF16),
        *received,
        kept=[
            VMEM((total, 6 * LANES), BF16),
            VMEM((total, 3 * LANES), BF16),
            VMEM((total, 4 * LANES), BF16),
            VMEM((total, cells), BF16),
            VMEM((count, levels_own, LANES), BF16),
            VMEM((total, LANES), F32),
            VMEM((count, levels_own, LANES), BF16),
            VMEM((count, levels_own // 2, LANES), BF16),
        ],
        mega=32,
    )
    returned = spread_out(results, axes, count)

    return call(
        functools.partial(finish_kernel, count),
        (
            shape(*spectrum.shape),
            shape(*atmosphere.shape, kind=F32),
            shape(*ocean_state.shape, kind=F32),
        ),
        swap,
        *returned,
        kept=[
            VMEM((2 * comps + levels_own, count * columns), BF16),
            VMEM((comps * rows, columns), F32),
            VMEM((2 * levels_own * tile_rows, columns), F32),
        ],
    )


def on_device(spectrum, *rest):
    atmosphere = rest[5]
    blocks = lax.axis_size("cells") * lax.axis_size("lev")
    comps, rows, columns = spectrum.shape
    fits = (
        columns == LANES
        and blocks == 8
        and lax.axis_size("sect") == 2
        and rows * (columns // blocks) == 2 * LANES
        and atmosphere.shape[1] * (columns // blocks) * 2 == LANES
        and any(comps % (16 * groups) == 0 for groups in (3, 2))
        and atmosphere.shape[0] % 16 == 0
        and NSTEP == 2
    )
    return (by_columns if fits else any_shape)(spectrum, *rest)


def solution(mesh):
    in_specs = (
        P(("cells", "lev"), "groups", "sect"),
        P(("cells", "lev")),
        P(("cells", "lev")),
        P(),
        P(),
        P(),
        P("lev", ("groups", "cells"), "sect"),
        P("lev", ("groups", "cells"), "sect"),
        P(("groups", "cells"), "sect"),
    )
    out_specs = (
        P(("cells", "lev"), "groups", "sect"),
        P("lev", ("groups", "cells"), "sect"),
        P("lev", ("groups", "cells"), "sect"),
    )
    return jax.shard_map(
        on_device, mesh=mesh, in_specs=in_specs, out_specs=out_specs, check_vma=False
    )
```

```python
import functools

import jax
import jax.numpy as jnp
import numpy as np
from jax import lax
from jax.experimental import pallas as pl
from jax.experimental.pallas import tpu as pltpu
from jax.sharding import PartitionSpec as P

NSTEP = 2
LANES = 128
F32 = jnp.float32
BF16 = jnp.bfloat16
VMEM = pltpu.VMEM


def from_root(block, axis, source):
    block = jnp.where(lax.axis_index(axis) == source, block, jnp.zeros_like(block))
    return lax.psum(block, axis)


def extended_2(block, sides, width, periodic):
    for axis, dim in sides:
        count = lax.axis_size(axis)
        forward = [(i, i + 1) for i in range(count - 1)]
        if periodic:
            forward.append((count - 1, 0))
        backward = [(target, source) for source, target in forward]
        low = lax.ppermute(
            lax.slice_in_dim(block, block.shape[dim] - width, None, axis=dim), axis, forward
        )
        high = lax.ppermute(lax.slice_in_dim(block, 0, width, axis=dim), axis, backward)
        block = jnp.concatenate([low, block, high], axis=dim)
    return block


def upwind(values, courant, before, after):
    return jnp.maximum(courant, 0.0) * (values - before) + jnp.minimum(courant, 0.0) * (
        after - values
    )


def any_shape(
    spectrum, courant_x, courant_y, growth, quartet, coupler, atmosphere, ocean_state, sea_mask
):
    cell_tiles = lax.axis_size("cells")
    lev_parts = lax.axis_size("lev")
    blocks = cell_tiles * lev_parts
    comps_own, rows_all, row_width = spectrum.shape
    total_comps = comps_own * blocks
    cell_rows = rows_all // blocks
    level_count = coupler.shape[0] // 2
    row_start = lax.axis_index("lev") * cell_rows
    shift_x = courant_x[:, None, None]
    shift_y = courant_y[:, None, None]
    sea_rows = (
        lax.dynamic_slice_in_dim(sea_mask, row_start, cell_rows, 0)
        .astype(jnp.float32)
        .reshape(1, cell_rows * row_width)
    )
    growth_column = growth[:, None]
    forcing_sign = jnp.array([-0.3, 0.3], jnp.float32)[:, None, None, None]
    state = jnp.stack([atmosphere, ocean_state])
    energy = spectrum
    for counter in range(NSTEP):
        surface = from_root(state[:, 0], "lev", 0)
        surface_wind = surface[0] - surface[1]
        wind_rows = lax.dynamic_slice_in_dim(
            surface_wind * surface_wind, row_start, cell_rows, 0
        ).reshape(1, cell_rows * row_width)
        padded = extended_2(energy, (("sect", 2),), 1, True)
        values = padded[:, :, 1:-1].astype(jnp.float32)
        west_side = padded[:, :, :-2].astype(jnp.float32)
        east_side = padded[:, :, 2:].astype(jnp.float32)
        moved = values - upwind(values, shift_x, west_side, east_side)
        moved = moved - upwind(
            values, shift_y, jnp.roll(values, 1, axis=1), jnp.roll(values, -1, axis=1)
        )
        advected = moved.astype(jnp.bfloat16)
        pieces = advected.reshape(1, comps_own, blocks, cell_rows, row_width)
        on_cells = lax.all_to_all(pieces, ("cells", "lev"), split_axis=2, concat_axis=0, tiled=True)
        on_cells = on_cells.reshape(total_comps, cell_rows * row_width)
        cell_values = on_cells.astype(jnp.float32)
        paired = jnp.dot(quartet, on_cells, preferred_element_type=jnp.float32)
        squared = (cell_values * cell_values).astype(jnp.bfloat16)
        quad_square = jnp.dot(quartet, squared, preferred_element_type=jnp.float32)
        fresh = (
            cell_values
            + 0.3 * (cell_values * paired - quad_square)
            + 0.1 * growth_column * wind_rows
        ) / (1.0 + 0.1 * cell_values * cell_values)
        fresh = (fresh * sea_rows).astype(jnp.bfloat16)
        profile = jnp.dot(coupler, fresh, preferred_element_type=jnp.float32).reshape(
            2, level_count, cell_rows, row_width
        )
        forcing = lax.all_to_all(profile, "lev", split_axis=1, concat_axis=2, tiled=True)
        returned = fresh.reshape(blocks, comps_own, 1, cell_rows, row_width)
        returned = lax.all_to_all(
            returned, ("cells", "lev"), split_axis=0, concat_axis=2, tiled=True
        )
        energy = returned.reshape(comps_own, rows_all, row_width)
        extended = extended_2(state, (("lev", 1), ("cells", 2), ("sect", 3)), 1, False)
        state = relaxed(extended, 1) + forcing_sign * forcing
    return (energy, state[0], state[1])


def relaxed(extended, first):
    centre = (slice(None),) * first + (slice(1, -1),) * 3
    middle = extended[centre]

    def moved(dim, start):
        where = list(centre)
        where[first + dim] = slice(start, extended.shape[first + dim] - 2 + start)
        return extended[tuple(where)]

    lateral = moved(1, 2) + moved(1, 0) + moved(2, 2) + moved(2, 0) - 4.0 * middle
    upright = moved(0, 2) + moved(0, 0) - 2.0 * middle
    return middle + 0.1 * lateral + 0.1 * upright


def iota(shape, dim):
    return lax.broadcasted_iota(jnp.int32, shape, dim)


def over(values, unit):
    return values >> (unit.bit_length() - 1)


def within(values, unit):
    return values & (unit - 1)


def moved(values, matrix):
    return jnp.dot(values.astype(BF16), matrix, preferred_element_type=F32)


def split(values):
    head = values.astype(BF16).astype(F32)
    return head, values - head


def column_of(row, lanes):
    return jnp.transpose(jnp.broadcast_to(row, (lanes, row.shape[1])))


def swap_matrix(count, unit):
    index = np.arange(count * count * unit)
    a, b, i = index // (count * unit), index // unit % count, index % unit
    return index[:, None] == ((b * count + a) * unit + i)[None, :]


def neighbour_matrices(rows, width):
    cells = rows * width
    row, column = np.divmod(np.arange(cells), width)
    west = np.where(column > 0, row * width + column - 1, cells + row)
    east = np.where(
        column < width - 1, row * width + column + 1, cells + LANES - rows + row
    )
    north = (row - 1) % rows * width + column
    south = (row + 1) % rows * width + column
    source = np.arange(cells + LANES)[:, None]
    return np.concatenate([source == move[None, :] for move in (west, east, north, south)], axis=1)


def lateral_matrix(rows, width):
    cells = rows * width
    far_west, west, east, far_east = cells + LANES, cells, cells + LANES - rows, cells + 2 * LANES - rows
    place = {}
    for row in range(rows):
        for column in range(width):
            place[row, column] = row * width + column
        for column, start in ((-2, far_west), (-1, west), (width, east), (width + 1, far_east)):
            place[row, column] = start + row
    matrix = np.zeros((cells + 2 * LANES, cells + LANES), bool)
    for (row, column), target in place.items():
        if not -1 <= column <= width:
            continue
        for near in ((row - 1, column), (row + 1, column), (row, column - 1), (row, column + 1)):
            if near in place:
                matrix[place[near], target] = True
    return matrix


def started(pairs, sems):
    copies = [pltpu.make_async_copy(*pair, sems.at[i]) for i, pair in enumerate(pairs)]
    for copy in copies:
        copy.start()
    return copies


def edges_kernel(
    x_hbm, air_hbm, ocean_hbm, sea_hbm, courant_x_hbm, courant_y_hbm, all_hbm, edge_hbm,
    x_ref, air_ref, ocean_ref, sea_ref, courant_x_ref, courant_y_ref, all_ref, wide, sems,
):
    comps, rows, columns = x_ref.shape
    levels, tile_rows, _ = air_ref.shape
    copies = started(
        [
            (x_hbm, x_ref),
            (air_hbm, air_ref),
            (ocean_hbm, ocean_ref),
            (sea_hbm, sea_ref),
            (courant_x_hbm, courant_x_ref),
            (courant_y_hbm, courant_y_ref),
        ],
        sems.at[pl.ds(0, 6)],
    )
    edges = comps + 16 + levels
    start = edges
    column, lane = iota((columns, LANES), 0), iota((columns, LANES), 1)

    block = within(over(lane, rows), 4)
    wanted = jnp.where(block < 2, columns - 2 + block, block - 2) == column
    row_of_lane = within(lane, rows)
    total = jnp.zeros((comps, LANES), F32)
    copies[0].wait()
    wide[...] = x_ref[...].astype(F32).reshape(comps * rows, columns)
    for row in range(rows):
        values = wide[pl.ds(row, comps, stride=rows), :].astype(BF16)
        all_ref[start : start + comps] = values
        start += comps
        total += moved(values, (wanted & (row_of_lane == row)).astype(BF16))
    all_ref[:comps] = total.astype(BF16)
    leaving = started(
        [(all_ref.at[edges:start], all_hbm.at[edges:start])], sems.at[pl.ds(6, 1)]
    )
    for copy in copies[1:]:
        copy.wait()
    owner = jnp.where(lax.axis_index("lev") == 0, 1.0, 0.0)
    head, tail = split((air_ref[0] - ocean_ref[0]) * owner)
    sea = sea_ref[...].astype(F32) * owner
    none = jnp.zeros_like(sea)
    all_ref[comps : comps + 16] = jnp.concatenate([head, tail, sea, none], axis=0).astype(BF16)
    head, tail = split((air_ref[1] - ocean_ref[1]) * owner)
    later = start
    below = jnp.concatenate([head, tail, none, none], axis=0)
    all_ref[start : start + 16] = below.astype(BF16)
    start += 16
    terms = []
    for ref in (courant_x_ref, courant_y_ref):
        for term in split(ref[...]):
            rest = jnp.zeros((1, 2 * columns - comps), F32)
            terms += [term[:, :columns], jnp.concatenate([term[:, columns:], rest], axis=1)]
    terms.append(jnp.zeros((8, columns), F32))
    all_ref[start : start + 16] = jnp.concatenate(terms, axis=0).astype(BF16)
    start += 16

    values = [ref[:, row, :] for ref in (air_ref, ocean_ref) for row in range(tile_rows)]
    unit = columns // len(values)
    inner = within(lane, unit)
    wanted = (jnp.where(inner < 2, columns - 2 + inner, inner - 2) == column) & (inner < 4)
    total = jnp.zeros((levels, LANES), F32)
    for index, value in enumerate(values):
        value = value.astype(BF16)
        all_ref[start : start + levels] = value
        start += levels
        total += moved(value, (wanted & (over(lane, unit) == index)).astype(BF16))
    all_ref[comps + 16 : edges] = total.astype(BF16)
    leaving += started(
        [
            (all_ref.at[:edges], edge_hbm),
            (all_ref.at[:edges], all_hbm.at[:edges]),
            (all_ref.at[later:], all_hbm.at[later:]),
        ],
        sems.at[pl.ds(7, 3)],
    )
    for copy in leaving:
        copy.wait()


def surface_rows(values, row_of_lane, tile_rows):
    first_row = lax.axis_index("cells") * tile_rows
    kept = row_of_lane == first_row + within(iota(values.shape, 0), tile_rows)
    kept = jnp.where(kept, values, 0.0).astype(BF16)
    target = iota((8, values.shape[0]), 0)
    source = over(iota((8, values.shape[0]), 1), tile_rows)
    source = jnp.where(source < 3, source, jnp.where(source < 4, 7, source - 1))
    adds = (target == jnp.where(source < 5, source, 7)).astype(BF16)
    return jnp.dot(adds, kept, preferred_element_type=F32)


def advect_kernel(
    groups, count, rows, levels, all_ref, packed_ref, cx_ref, cy_ref, edge_ref, gathered
):
    comps = cx_ref.shape[0]
    columns = LANES
    width = columns // count
    cells = rows * width
    first = comps + 16 + levels
    edge_ref[...] = all_ref[:comps]

    def by_row(row):
        row = (row + rows) % rows
        return all_ref[first + row * comps : first + (row + 1) * comps]

    below = first + rows * comps
    terms = all_ref[below + 16 : below + 32].astype(F32)
    for index, ref in enumerate((cx_ref, cy_ref)):
        own = terms[4 * index : 4 * index + 4]
        own = own[:2] + own[2:]
        ref[...] = column_of(jnp.concatenate([own[:1], own[1:, : comps - columns]], axis=1), LANES)
    source, target = iota((columns, 2 * columns), 0), iota((columns, 2 * columns), 1)
    step = jnp.where(target < columns, -1, 1)
    sides = (source == within(target + step, columns)).astype(BF16)
    for row in range(rows):
        here = by_row(row).astype(F32)
        beside = moved(by_row(row), sides)
        along = upwind(here, cx_ref[...], beside[:, :columns], beside[:, columns:])
        across = upwind(
            here,
            cy_ref[...],
            by_row(row - 1).astype(F32),
            by_row(row + 1).astype(F32),
        )
        tile, place = divmod(row, count)
        gathered[tile * comps : (tile + 1) * comps, place * columns : (place + 1) * columns] = (
            here - along - across
        ).astype(BF16)
    for index in range(count):
        start = below + 32 + index * levels
        gathered[2 * comps :, index * columns : (index + 1) * columns] = all_ref[
            start : start + levels
        ]
    source = iota((count * columns, 2 * LANES), 0)
    lane = iota((count * columns, 2 * LANES), 1)
    for target in range(count // 2):
        origin = over(within(lane, LANES), width) * columns + within(lane, width)
        origin = origin + (2 * target + over(lane, LANES)) * width
        swap = (source == origin).astype(BF16)
        values = moved(gathered[...], swap).astype(BF16)
        for side in range(2):
            half = values[:, side * LANES : (side + 1) * LANES]
            packed_ref[2 * target + side, : 2 * comps, :] = half[: 2 * comps]
            start = 2 * comps + comps // groups + 16
            packed_ref[2 * target + side, start : start + levels, :] = half[2 * comps :]
    size = comps // groups

    own = iota((size, LANES), 1)
    riders = jnp.zeros((size, LANES), F32)
    for group in range(groups):
        span = slice(group * size, (group + 1) * size)
        for index, term in enumerate(split(cx_ref[span]) + split(cy_ref[span])):
            riders = jnp.where(own == 5 * rows + 4 * group + index, term, riders)

    values = jnp.concatenate([all_ref[comps : comps + 16], all_ref[below : below + 16]], axis=0)
    spot, lanes = iota((columns, count * cells), 0), iota((columns, count * cells), 1)
    repeat = spot == over(lanes, cells) * width + within(lanes, width)
    inland = moved(values, repeat.astype(BF16))
    inland = surface_rows(inland, over(within(iota(inland.shape, 1), cells), width), 4)
    spot, lanes = iota((columns, count * LANES), 0), iota((columns, count * LANES), 1)
    first = over(lanes, LANES) * width
    lanes = within(lanes, LANES)
    repeat = ((lanes < rows) & (spot == first - 1)) | (
        (lanes >= LANES - rows) & (spot == first + width)
    )
    shore = moved(values, repeat.astype(BF16))
    shore = surface_rows(shore, within(iota(shore.shape, 1), rows), 4)
    place = iota((8, LANES), 0)

    source, target_lane = iota((cells, 2 * LANES), 0), iota((cells, 2 * LANES), 1)
    block = over(within(target_lane, LANES), rows)
    row_start = within(target_lane, rows) * width
    ends = []
    for group in range(groups):
        west = (target_lane < LANES) & (block == 2 * group) & (source == row_start + width - 1)
        east = (target_lane >= LANES) & (block == (2 * group + 7) % 8) & (source == row_start)
        ends.append((west | east).astype(BF16))
    source, target_lane = iota((LANES, 2 * LANES), 0), iota((LANES, 2 * LANES), 1)
    inner = within(target_lane, width)
    back = (target_lane - inner) & (LANES - 1)
    shifts = []
    for start in (0, 8):
        west = (target_lane < LANES) & (inner >= start) & (inner < start + 2)
        west = west & (source == back + width - 2 + inner - start)
        east = (target_lane >= LANES) & (inner >= start + 2) & (inner < start + 4)
        east = east & (source == back + inner - start - 2)
        shifts.append((west | east).astype(BF16))
    beside, beside_state = [], []
    half = levels // 2
    for target in range(count):
        total = jnp.zeros((size, 2 * LANES), F32)
        for group in range(groups):
            for tile in range(2):
                span = slice(tile * comps + group * size, tile * comps + (group + 1) * size)
                rows_of = slice(tile * LANES, (tile + 1) * LANES)
                total += moved(packed_ref[target, span, :], ends[group][rows_of])
        beside.append(total)
        start = 2 * comps + size + 16
        low = moved(packed_ref[target, start : start + half, :], shifts[0])
        high = moved(packed_ref[target, start + half : start + levels, :], shifts[1])
        beside_state.append(low + high)
    for target in range(count):
        left, right = max(target - 1, 0), min(target + 1, count - 1)
        shared = riders + beside[left][:, :LANES] + beside[right][:, LANES:]
        packed_ref[target, 2 * comps : 2 * comps + size, :] = shared.astype(BF16)
        winds = [inland[:, (2 * target + i) * LANES : (2 * target + i + 1) * LANES] for i in range(2)]
        outer = pltpu.roll(shore[:, target * LANES : (target + 1) * LANES], 5, 0)
        winds[0] = jnp.where(place < 5, winds[0], outer)
        start = 2 * comps + size
        packed_ref[target, start : start + 16, :] = jnp.concatenate(winds, axis=0).astype(BF16)
        start += 16 + levels
        outer = beside_state[left][:, :LANES] + beside_state[right][:, LANES:]
        packed_ref[target, start : start + half, :] = outer.astype(BF16)


def coast_kernel(groups, count, rows, packed_ref, edge_ref, halo_ref, cx_ref, cy_ref, *out_refs):
    comps = cx_ref.shape[0]
    size = comps // groups
    levels = halo_ref.shape[0] - comps - 16
    cells = 2 * LANES
    width = cells // rows
    half = levels // 2
    block = over(iota((comps, LANES), 1), rows)
    near = jnp.where((block < 2) | (block >= 6), halo_ref[:comps], edge_ref[...])
    source, target = iota((LANES, 4 * LANES), 0), iota((LANES, 4 * LANES), 1)
    lane = within(target, LANES)
    row = within(lane, rows)
    kind = over(target, LANES)
    shift = jnp.where(
        kind == 0,
        within(lane - rows, LANES),
        jnp.where(
            kind == 1,
            within(lane + rows, LANES),
            lane - row + within(row + jnp.where(kind == 2, -1, 1), rows),
        ),
    )
    four = moved(near, (source == shift).astype(BF16))
    near = near.astype(F32)
    near = (
        near
        - upwind(near, cx_ref[...], four[:, :LANES], four[:, LANES : 2 * LANES])
        - upwind(near, cy_ref[...], four[:, 2 * LANES : 3 * LANES], four[:, 3 * LANES :])
    )
    source, target = iota((LANES, cells), 0), iota((LANES, cells), 1)
    column, row = within(target, width), over(target, width)
    spread = ((column == 0) & (source == 2 * rows + row)) | (
        (column == width - 1) & (source == 5 * rows + row)
    )
    ends = moved(near, spread.astype(BF16))
    shared = jnp.zeros((size, LANES), F32)
    source, target = iota((LANES, LANES), 0), iota((LANES, LANES), 1)
    for group in range(groups):
        there = over(target, rows)
        from_block = jnp.where(
            there == 2 * group, 1, jnp.where(there == (2 * group + 7) % 8, 6, LANES)
        )
        spread = source == from_block * rows + within(target, rows)
        shared += moved(near[group * size : (group + 1) * size], spread.astype(BF16))
    repeat = ((target < rows) & (source == LANES - 1)) | ((target >= LANES - rows) & (source == 0))
    coast = moved(halo_ref[comps : comps + 16], repeat.astype(BF16))
    coast = jnp.concatenate([coast, jnp.zeros_like(coast)], axis=0)
    coast = surface_rows(coast, within(iota(coast.shape, 1), rows), 4)
    coast = pltpu.roll(coast, 5, 0)
    coast = jnp.concatenate([coast, jnp.zeros_like(coast)], axis=0)
    inner = within(target, width)
    low = (source == target) & (inner < 4)
    high = (source == target - 8) & (inner >= 8) & (inner < 12)
    state = moved(halo_ref[comps + 16 : comps + 16 + half], low.astype(BF16))
    state += moved(halo_ref[comps + 16 + half :], high.astype(BF16))
    me = lax.axis_index(("cells", "lev"))
    for slot in range(count):
        target = lax.rem(me + slot, count)
        out_refs[slot][...] = packed_ref[target]
        place, lane = iota((16, LANES), 0), iota((16, LANES), 1)
        outer = (place >= 5) & (place < 8)

        def patch(start, stop, where, values):
            old = out_refs[slot][start:stop].astype(F32)
            out_refs[slot][start:stop] = jnp.where(where, values, old).astype(BF16)

        def patch_ends(east):
            column = within(iota((comps, LANES), 1), width)
            for tile in range(2):
                values = ends[:, tile * LANES : (tile + 1) * LANES]
                where = column == (width - 1 if east else 0)
                patch(tile * comps, (tile + 1) * comps, where, values)
            own = over(iota((size, LANES), 1), rows)
            where = own < 0
            for group in range(groups):
                where = where | (own == ((2 * group + 7) % 8 if east else 2 * group))
            patch(2 * comps, 2 * comps + size, where, shared)
            start = 2 * comps + size
            side = lane >= LANES - rows if east else lane < rows
            patch(start, start + 16, outer & side, coast)
            start += 16 + levels
            inner = within(iota((half, LANES), 1), 8)
            patch(start, start + half, (inner >= 2) == east, state)

        @pl.when(target == 0)
        def _():
            patch_ends(False)

        @pl.when(target == count - 1)
        def _():
            patch_ends(True)


def steps_kernel(
    groups, count, rows, quartet_ref, coupler_ref, growth_ref, beside_ref, lateral_ref, *refs
):
    in_refs, refs = refs[:count], refs[count:]
    out_refs, refs = refs[:count], refs[count:]
    first_in, fresh, second_in, last, shares, factors, state, ends = refs
    total = quartet_ref.shape[0]
    comps = total // count
    size = comps // groups
    cells = 2 * LANES
    wide = 3 * LANES
    width = cells // rows
    levels = coupler_ref.shape[0] // 2
    half = shares.shape[1]
    me = lax.axis_index(("cells", "lev"))
    west_end = (me == 0) & (lax.axis_index("sect") == 0)
    east_end = (me == count - 1) & (lax.axis_index("sect") == lax.axis_size("sect") - 1)
    factors[:, 8:16] = column_of(0.1 * growth_ref[...], 8)

    source, target = iota((LANES, 2 * LANES), 0), iota((LANES, 2 * LANES), 1)
    block = over(target, rows)
    opened = []
    for group in range(groups):
        from_block = jnp.where(
            block == 0, 2 * group, jnp.where(block == 7, (2 * group + 7) % 8, LANES)
        )
        column = source == from_block * rows + within(target, rows)
        rider = source - (5 * rows + 4 * group)
        rider = (rider >= 0) & (rider < 4) & (over(rider, 2) == target - LANES)
        opened.append((column | rider).astype(BF16))
    winds = jnp.zeros((16, LANES), F32)
    for slot in range(count):
        source = lax.rem(me - slot + count, count)
        start = pl.multiple_of(source * comps, 16)
        span = pl.ds(start, comps)
        for tile in range(2):
            values = in_refs[slot][tile * comps : (tile + 1) * comps]
            first_in[span, tile * LANES : (tile + 1) * LANES] = values
            values = values.astype(F32)
            first_in[span, wide + tile * LANES : wide + (tile + 1) * LANES] = (
                values * values
            ).astype(BF16)
        for group in range(groups):
            span = pl.ds(pl.multiple_of(start + group * size, 16), size)
            values = moved(in_refs[slot][2 * comps : 2 * comps + size], opened[group])
            first_in[span, cells:wide] = values[:, :LANES].astype(BF16)
            values_8 = values[:, LANES : LANES + 8]
            values = values[:, :LANES]
            first_in[span, wide + cells :] = (values * values).astype(BF16)
            factors[span, :8] = values_8
        place = 2 * comps + size
        winds += in_refs[slot][place : place + 16].astype(F32)
        place += 16
        state[source] = in_refs[slot][place : place + half]
        ends[source] = in_refs[slot][place + half :]

    first, second = winds[:8], winds[8:]
    outer = pltpu.roll(first, 3, 0)

    def joined(tile):
        return tile[:1] + tile[1:2]

    surface = jnp.concatenate([joined(first), joined(second), joined(outer)], axis=1)
    terms = jnp.concatenate([first, second, outer], axis=1)
    sea = terms[2:3]
    below = jnp.concatenate([joined(first[3:5]), joined(second[3:5])], axis=1)
    wind = surface * surface

    def renew(values, products, growth, wind, sea):
        half = values.shape[1]
        paired, quad_square = products[:, :half], products[:, half:]
        below = 1.0 + 0.1 * values * values
        inverse = pl.reciprocal(below, approx=True)
        inverse = inverse * (2.0 - below * inverse)
        return (values + 0.3 * (values * paired - quad_square) + growth * wind) * inverse * sea

    part = total // 2
    for step in range(2):
        span = slice(step * part, (step + 1) * part)
        products = jnp.dot(quartet_ref[span, :], first_in[...], preferred_element_type=F32)
        values = first_in[span, :wide].astype(F32)
        fresh[span, :] = renew(values, products, factors[span, 8:9], wind, sea).astype(BF16)
    part = total // 8
    for step in range(8):
        span = slice(step * part, (step + 1) * part)
        beside = jnp.dot(fresh[span, :], beside_ref[...], preferred_element_type=F32)
        here = fresh[span, :cells].astype(F32)
        cx = jnp.broadcast_to(factors[span, 0:1], here.shape)
        cy = jnp.broadcast_to(factors[span, 1:2], here.shape)
        values = (
            here
            - upwind(here, cx, beside[:, :cells], beside[:, cells : 2 * cells])
            - upwind(here, cy, beside[:, 2 * cells : 3 * cells], beside[:, 3 * cells :])
        ).astype(BF16)
        second_in[span, :cells] = values
        values = values.astype(F32)
        second_in[span, cells:] = (values * values).astype(BF16)

    lev_parts = levels // half
    halves = iota((half, LANES), 1) < LANES // 2

    def collected(values):
        fields = []
        for kind in range(2):
            for part in range(lev_parts):
                tiles = []
                for pair in range(count // lev_parts // 2):
                    left = values[2 * pair * lev_parts + part].astype(F32)
                    right = values[(2 * pair + 1) * lev_parts + part].astype(F32)
                    if kind == 0:
                        right = pltpu.roll(right, LANES // 2, 1)
                    else:
                        left = pltpu.roll(left, LANES // 2, 1)
                    tiles.append(jnp.where(halves[: left.shape[0]], left, right))
                fields.append(jnp.concatenate(tiles, axis=1))
        return fields

    inner = jnp.concatenate(collected(state), axis=0)
    source, target = iota((cells, cells), 0), iota((cells, cells), 1)
    far = over(target, LANES)
    block = over(within(target, LANES), rows)
    order = jnp.where(block == 0, jnp.where(far == 0, 1, 0), jnp.where(far == 0, 2, 3))
    used = (block == 0) | (block == 7)
    spread = [
        ((source == within(target, rows) * width + order + 8 * high) & used).astype(BF16)
        for high in range(2)
    ]
    outer = []
    for field in collected(ends):
        outer += [moved(field, spread[0]), moved(field, spread[1])]
    outer = jnp.concatenate(outer, axis=0)

    def bounded(values):
        lane = iota(values.shape, 1)
        outside = (west_end & (lane < rows)) | (east_end & (lane >= LANES - rows))
        return jnp.where(outside, 0.0, values)

    outer = [bounded(outer[:, :LANES]), bounded(outer[:, LANES:])]

    def relaxed_once(here, lateral):
        level = within(iota(here.shape, 0), levels)
        lateral = lateral - 4.0 * here
        above = jnp.where(level == 0, 0.0, pltpu.roll(here, 1, 0))
        under = jnp.where(level == levels - 1, 0.0, pltpu.roll(here, 2 * levels - 1, 0))
        return here + 0.1 * lateral + 0.1 * (above + under - 2.0 * here)

    sign = jnp.where(iota((2 * levels, 1), 0) < levels, -0.3, 0.3)
    forced = jnp.dot(coupler_ref[...], fresh[...], preferred_element_type=F32) * sign
    here = jnp.concatenate([inner] + outer, axis=1)
    fields = relaxed_once(here[:, :wide], moved(here, lateral_ref[...])) + forced
    fields = jnp.concatenate([fields[:, :cells], bounded(fields[:, cells:])], axis=1)
    near = lateral_ref[:wide, :cells]
    head, tail = split(fields)
    fields = relaxed_once(fields[:, :cells], moved(head, near) + moved(tail, near))

    terms = jnp.concatenate([terms[:, :cells], bounded(terms[:, cells:])], axis=1)
    lateral = joined(moved(terms, near))
    calm = surface[:, :cells]
    calm = calm + 0.1 * (lateral - 4.0 * calm) + 0.1 * (below - 2.0 * calm)
    later = calm + forced[:1, :cells] - forced[levels : levels + 1, :cells]
    later = later * later

    part = total // 2
    for step in range(2):
        span = slice(step * part, (step + 1) * part)
        products = jnp.dot(quartet_ref[span, :], second_in[...], preferred_element_type=F32)
        values = second_in[span, :cells].astype(F32)
        done = renew(values, products, factors[span, 8:9], later, sea[:, :cells])
        last[span, :] = done.astype(BF16)

    forced = jnp.dot(coupler_ref[...], last[...], preferred_element_type=F32)
    carried = fields + sign * forced
    for target in range(count):
        cell_tile, lev_part = target // lev_parts, target % lev_parts
        columns = slice((cell_tile // 2) * LANES, (cell_tile // 2 + 1) * LANES)
        air = carried[lev_part * half : (lev_part + 1) * half, columns]
        sea_part = carried[levels + lev_part * half : levels + (lev_part + 1) * half, columns]
        if cell_tile % 2:
            air = pltpu.roll(air, LANES // 2, 1)
        else:
            sea_part = pltpu.roll(sea_part, LANES // 2, 1)
        shares[target] = jnp.where(halves, air, sea_part).astype(BF16)
    for slot in range(count):
        target = lax.rem(me + slot, count)
        span = pl.ds(pl.multiple_of(target * comps, 16), comps)
        out_refs[slot][:comps] = last[span, :LANES]
        out_refs[slot][comps : 2 * comps] = last[span, LANES:]
        out_refs[slot][2 * comps :] = shares[target]


def finish_kernel(count, swap_ref, *refs):
    in_refs, refs = refs[:count], refs[count:]
    energy_ref, air_ref, ocean_ref, gathered, wide, narrow = refs
    comps, rows, columns = energy_ref.shape
    levels, tile_rows, _ = air_ref.shape
    me = lax.axis_index(("cells", "lev"))
    for slot in range(count):
        source = lax.rem(me - slot + count, count)
        gathered[:, pl.ds(pl.multiple_of(source * columns, columns), columns)] = in_refs[slot][...]
    for pair in range(count // 2):
        lanes = slice(2 * pair * columns, 2 * (pair + 1) * columns)
        values = moved(gathered[...], swap_ref[:, lanes])
        for side in range(2):
            index = 2 * pair + side
            part = values[:, side * columns : (side + 1) * columns]
            for tile in range(rows // count):
                wide[pl.ds(tile * count + index, comps, stride=rows), :] = part[
                    tile * comps : (tile + 1) * comps
                ]
            kind, row = divmod(index, tile_rows)
            narrow[pl.ds(kind * levels * tile_rows + row, levels, stride=tile_rows), :] = part[
                2 * comps :
            ]
    energy_ref[...] = wide[...].reshape(comps, rows, columns).astype(energy_ref.dtype)
    size = levels * tile_rows
    air_ref[...] = narrow[:size, :].reshape(air_ref.shape)
    ocean_ref[...] = narrow[size:, :].reshape(ocean_ref.shape)


def spread_out(pieces, axes, count):
    received = [pieces[0]]
    for shift in range(1, count):
        pairs = [(index, (index + shift) % count) for index in range(count)]
        received.append(lax.ppermute(pieces[shift], axes, pairs))
    return received


def by_columns(
    spectrum, courant_x, courant_y, growth, quartet, coupler, atmosphere, ocean_state, sea_mask
):
    axes = ("cells", "lev")
    count = lax.axis_size("cells") * lax.axis_size("lev")
    sects = lax.axis_size("sect")
    comps, rows, columns = spectrum.shape
    total = comps * count
    width = columns // count
    cells = rows * width
    levels_own, tile_rows, _ = atmosphere.shape
    groups = 3 if comps % 48 == 0 else 2
    whole = pl.BlockSpec(memory_space=VMEM)
    far = pl.BlockSpec(memory_space=pltpu.HBM)

    def shape(*dims, kind=BF16):
        return jax.ShapeDtypeStruct(dims, kind)

    def call(kernel, outs, *args, kept=(), place=whole, flops=0, mega=16):
        return pl.pallas_call(
            kernel,
            out_shape=outs,
            in_specs=[place] * len(args),
            out_specs=jax.tree.map(lambda _: place, outs),
            scratch_shapes=list(kept),
            compiler_params=pltpu.CompilerParams(vmem_limit_bytes=mega * 1024 * 1024),
            cost_estimate=pl.CostEstimate(flops=flops, bytes_accessed=4000000, transcendentals=0),
        )(*args)

    swap = jnp.asarray(swap_matrix(count, width), BF16)
    edges = comps + 16 + levels_own
    fields = (spectrum, atmosphere, ocean_state, sea_mask, courant_x[None], courant_y[None])
    fetched = shape(edges + rows * comps + 32 + count * levels_own, LANES)
    fetched, edge = call(
        edges_kernel,
        (fetched, shape(edges, LANES)),
        *fields,
        kept=[VMEM(array.shape, array.dtype) for array in fields + (fetched,)]
        + [VMEM((comps * rows, columns), F32), pltpu.SemaphoreType.DMA((10,))],
        place=far,
        mega=63,
    )
    halo = lax.ppermute(edge, "sect", [(0, 1), (1, 0)])

    size = 2 * comps + comps // groups + 16 + levels_own + levels_own // 2
    factor = shape(comps, LANES, kind=F32)
    packed, factor_x, factor_y, edge = call(
        functools.partial(advect_kernel, groups, count, rows, levels_own),
        (shape(count, size, LANES), factor, factor, shape(comps, LANES)),
        fetched,
        kept=[VMEM((2 * comps + levels_own, count * columns), BF16)],
        flops=2000000000,
    )
    pieces = call(
        functools.partial(coast_kernel, groups, count, rows),
        (shape(size, LANES),) * count,
        packed,
        edge,
        halo,
        factor_x,
        factor_y,
    )
    received = spread_out(pieces, axes, count)

    results = call(
        functools.partial(steps_kernel, groups, count, rows),
        (shape(2 * comps + levels_own, LANES),) * count,
        quartet,
        coupler,
        growth[None],
        jnp.asarray(neighbour_matrices(rows, width), BF16),
        jnp.asarray(lateral_matrix(rows, width), BF16),
        *received,
        kept=[
            VMEM((total, 6 * LANES), BF16),
            VMEM((total, 3 * LANES), BF16),
            VMEM((total, 4 * LANES), BF16),
            VMEM((total, cells), BF16),
            VMEM((count, levels_own, LANES), BF16),
            VMEM((total, LANES), F32),
            VMEM((count, levels_own, LANES), BF16),
            VMEM((count, levels_own // 2, LANES), BF16),
        ],
        mega=32,
    )
    returned = spread_out(results, axes, count)

    return call(
        functools.partial(finish_kernel, count),
        (
            shape(*spectrum.shape),
            shape(*atmosphere.shape, kind=F32),
            shape(*ocean_state.shape, kind=F32),
        ),
        swap,
        *returned,
        kept=[
            VMEM((2 * comps + levels_own, count * columns), BF16),
            VMEM((comps * rows, columns), F32),
            VMEM((2 * levels_own * tile_rows, columns), F32),
        ],
    )


def on_device(spectrum, *rest):
    atmosphere = rest[5]
    blocks = lax.axis_size("cells") * lax.axis_size("lev")
    comps, rows, columns = spectrum.shape
    fits = (
        columns == LANES
        and blocks == 8
        and lax.axis_size("sect") == 2
        and rows * (columns // blocks) == 2 * LANES
        and atmosphere.shape[1] * (columns // blocks) * 2 == LANES
        and any(comps % (16 * groups) == 0 for groups in (3, 2))
        and atmosphere.shape[0] % 16 == 0
        and NSTEP == 2
    )
    return (by_columns if fits else any_shape)(spectrum, *rest)


def solution(mesh):
    in_specs = (
        P(("cells", "lev"), "groups", "sect"),
        P(("cells", "lev")),
        P(("cells", "lev")),
        P(),
        P(),
        P(),
        P("lev", ("groups", "cells"), "sect"),
        P("lev", ("groups", "cells"), "sect"),
        P(("groups", "cells"), "sect"),
    )
    out_specs = (
        P(("cells", "lev"), "groups", "sect"),
        P("lev", ("groups", "cells"), "sect"),
        P("lev", ("groups", "cells"), "sect"),
    )
    return jax.shard_map(
        on_device, mesh=mesh, in_specs=in_specs, out_specs=out_specs, check_vma=False
    )
```

```python
import functools

import jax
import jax.numpy as jnp
import numpy as np
from jax import lax
from jax.experimental import pallas as pl
from jax.experimental.pallas import tpu as pltpu
from jax.sharding import PartitionSpec as P

NSTEP = 2
LANES = 128
F32 = jnp.float32
BF16 = jnp.bfloat16
VMEM = pltpu.VMEM


def from_root(block, axis, source):
    block = jnp.where(lax.axis_index(axis) == source, block, jnp.zeros_like(block))
    return lax.psum(block, axis)


def extended_2(block, sides, width, periodic):
    for axis, dim in sides:
        count = lax.axis_size(axis)
        forward = [(i, i + 1) for i in range(count - 1)]
        if periodic:
            forward.append((count - 1, 0))
        backward = [(target, source) for source, target in forward]
        low = lax.ppermute(
            lax.slice_in_dim(block, block.shape[dim] - width, None, axis=dim), axis, forward
        )
        high = lax.ppermute(lax.slice_in_dim(block, 0, width, axis=dim), axis, backward)
        block = jnp.concatenate([low, block, high], axis=dim)
    return block


def upwind(values, courant, before, after):
    return jnp.maximum(courant, 0.0) * (values - before) + jnp.minimum(courant, 0.0) * (
        after - values
    )


def any_shape(
    spectrum, courant_x, courant_y, growth, quartet, coupler, atmosphere, ocean_state, sea_mask
):
    cell_tiles = lax.axis_size("cells")
    lev_parts = lax.axis_size("lev")
    blocks = cell_tiles * lev_parts
    comps_own, rows_all, row_width = spectrum.shape
    total_comps = comps_own * blocks
    cell_rows = rows_all // blocks
    level_count = coupler.shape[0] // 2
    row_start = lax.axis_index("lev") * cell_rows
    shift_x = courant_x[:, None, None]
    shift_y = courant_y[:, None, None]
    sea_rows = (
        lax.dynamic_slice_in_dim(sea_mask, row_start, cell_rows, 0)
        .astype(jnp.float32)
        .reshape(1, cell_rows * row_width)
    )
    growth_column = growth[:, None]
    forcing_sign = jnp.array([-0.3, 0.3], jnp.float32)[:, None, None, None]
    state = jnp.stack([atmosphere, ocean_state])
    energy = spectrum
    for counter in range(NSTEP):
        surface = from_root(state[:, 0], "lev", 0)
        surface_wind = surface[0] - surface[1]
        wind_rows = lax.dynamic_slice_in_dim(
            surface_wind * surface_wind, row_start, cell_rows, 0
        ).reshape(1, cell_rows * row_width)
        padded = extended_2(energy, (("sect", 2),), 1, True)
        values = padded[:, :, 1:-1].astype(jnp.float32)
        west_side = padded[:, :, :-2].astype(jnp.float32)
        east_side = padded[:, :, 2:].astype(jnp.float32)
        moved = values - upwind(values, shift_x, west_side, east_side)
        moved = moved - upwind(
            values, shift_y, jnp.roll(values, 1, axis=1), jnp.roll(values, -1, axis=1)
        )
        advected = moved.astype(jnp.bfloat16)
        pieces = advected.reshape(1, comps_own, blocks, cell_rows, row_width)
        on_cells = lax.all_to_all(pieces, ("cells", "lev"), split_axis=2, concat_axis=0, tiled=True)
        on_cells = on_cells.reshape(total_comps, cell_rows * row_width)
        cell_values = on_cells.astype(jnp.float32)
        paired = jnp.dot(quartet, on_cells, preferred_element_type=jnp.float32)
        squared = (cell_values * cell_values).astype(jnp.bfloat16)
        quad_square = jnp.dot(quartet, squared, preferred_element_type=jnp.float32)
        fresh = (
            cell_values
            + 0.3 * (cell_values * paired - quad_square)
            + 0.1 * growth_column * wind_rows
        ) / (1.0 + 0.1 * cell_values * cell_values)
        fresh = (fresh * sea_rows).astype(jnp.bfloat16)
        profile = jnp.dot(coupler, fresh, preferred_element_type=jnp.float32).reshape(
            2, level_count, cell_rows, row_width
        )
        forcing = lax.all_to_all(profile, "lev", split_axis=1, concat_axis=2, tiled=True)
        returned = fresh.reshape(blocks, comps_own, 1, cell_rows, row_width)
        returned = lax.all_to_all(
            returned, ("cells", "lev"), split_axis=0, concat_axis=2, tiled=True
        )
        energy = returned.reshape(comps_own, rows_all, row_width)
        extended = extended_2(state, (("lev", 1), ("cells", 2), ("sect", 3)), 1, False)
        state = relaxed(extended, 1) + forcing_sign * forcing
    return (energy, state[0], state[1])


def relaxed(extended, first):
    centre = (slice(None),) * first + (slice(1, -1),) * 3
    middle = extended[centre]

    def moved(dim, start):
        where = list(centre)
        where[first + dim] = slice(start, extended.shape[first + dim] - 2 + start)
        return extended[tuple(where)]

    lateral = moved(1, 2) + moved(1, 0) + moved(2, 2) + moved(2, 0) - 4.0 * middle
    upright = moved(0, 2) + moved(0, 0) - 2.0 * middle
    return middle + 0.1 * lateral + 0.1 * upright


def iota(shape, dim):
    return lax.broadcasted_iota(jnp.int32, shape, dim)


def over(values, unit):
    return values >> (unit.bit_length() - 1)


def within(values, unit):
    return values & (unit - 1)


def moved(values, matrix):
    return jnp.dot(values.astype(BF16), matrix, preferred_element_type=F32)


def split(values):
    head = values.astype(BF16).astype(F32)
    return head, values - head


def column_of(row, lanes):
    return jnp.transpose(jnp.broadcast_to(row, (lanes, row.shape[1])))


def swap_matrix(count, unit):
    index = np.arange(count * count * unit)
    a, b, i = index // (count * unit), index // unit % count, index % unit
    return index[:, None] == ((b * count + a) * unit + i)[None, :]


def neighbour_matrices(rows, width):
    cells = rows * width
    row, column = np.divmod(np.arange(cells), width)
    west = np.where(column > 0, row * width + column - 1, cells + row)
    east = np.where(
        column < width - 1, row * width + column + 1, cells + LANES - rows + row
    )
    north = (row - 1) % rows * width + column
    south = (row + 1) % rows * width + column
    source = np.arange(cells + LANES)[:, None]
    return np.concatenate([source == move[None, :] for move in (west, east, north, south)], axis=1)


def lateral_matrix(rows, width):
    cells = rows * width
    far_west, west, east, far_east = cells + LANES, cells, cells + LANES - rows, cells + 2 * LANES - rows
    place = {}
    for row in range(rows):
        for column in range(width):
            place[row, column] = row * width + column
        for column, start in ((-2, far_west), (-1, west), (width, east), (width + 1, far_east)):
            place[row, column] = start + row
    matrix = np.zeros((cells + 2 * LANES, cells + LANES), bool)
    for (row, column), target in place.items():
        if not -1 <= column <= width:
            continue
        for near in ((row - 1, column), (row + 1, column), (row, column - 1), (row, column + 1)):
            if near in place:
                matrix[place[near], target] = True
    return matrix


def started(pairs, sems):
    copies = [pltpu.make_async_copy(*pair, sems.at[i]) for i, pair in enumerate(pairs)]
    for copy in copies:
        copy.start()
    return copies


def edges_kernel(
    x_hbm, air_hbm, ocean_hbm, sea_hbm, courant_x_hbm, courant_y_hbm, all_hbm, edge_hbm,
    x_ref, air_ref, ocean_ref, sea_ref, courant_x_ref, courant_y_ref, all_ref, wide, sems,
):
    comps, rows, columns = x_ref.shape
    levels, tile_rows, _ = air_ref.shape
    copies = started(
        [
            (x_hbm, x_ref),
            (air_hbm, air_ref),
            (ocean_hbm, ocean_ref),
            (sea_hbm, sea_ref),
            (courant_x_hbm, courant_x_ref),
            (courant_y_hbm, courant_y_ref),
        ],
        sems.at[pl.ds(0, 6)],
    )
    edges = comps + 16 + levels
    start = edges
    column, lane = iota((columns, LANES), 0), iota((columns, LANES), 1)

    block = within(over(lane, rows), 4)
    wanted = jnp.where(block < 2, columns - 2 + block, block - 2) == column
    row_of_lane = within(lane, rows)
    total = jnp.zeros((comps, LANES), F32)
    copies[0].wait()
    wide[...] = x_ref[...].astype(F32).reshape(comps * rows, columns)
    for row in range(rows):
        values = wide[pl.ds(row, comps, stride=rows), :].astype(BF16)
        all_ref[start : start + comps] = values
        start += comps
        total += moved(values, (wanted & (row_of_lane == row)).astype(BF16))
    all_ref[:comps] = total.astype(BF16)
    leaving = started(
        [(all_ref.at[edges:start], all_hbm.at[edges:start])], sems.at[pl.ds(6, 1)]
    )
    for copy in copies[1:]:
        copy.wait()
    owner = jnp.where(lax.axis_index("lev") == 0, 1.0, 0.0)
    head, tail = split((air_ref[0] - ocean_ref[0]) * owner)
    sea = sea_ref[...].astype(F32) * owner
    none = jnp.zeros_like(sea)
    all_ref[comps : comps + 16] = jnp.concatenate([head, tail, sea, none], axis=0).astype(BF16)
    head, tail = split((air_ref[1] - ocean_ref[1]) * owner)
    later = start
    below = jnp.concatenate([head, tail, none, none], axis=0)
    all_ref[start : start + 16] = below.astype(BF16)
    start += 16
    terms = []
    for ref in (courant_x_ref, courant_y_ref):
        for term in split(ref[...]):
            rest = jnp.zeros((1, 2 * columns - comps), F32)
            terms += [term[:, :columns], jnp.concatenate([term[:, columns:], rest], axis=1)]
    terms.append(jnp.zeros((8, columns), F32))
    all_ref[start : start + 16] = jnp.concatenate(terms, axis=0).astype(BF16)
    start += 16

    values = [ref[:, row, :] for ref in (air_ref, ocean_ref) for row in range(tile_rows)]
    unit = columns // len(values)
    inner = within(lane, unit)
    wanted = (jnp.where(inner < 2, columns - 2 + inner, inner - 2) == column) & (inner < 4)
    total = jnp.zeros((levels, LANES), F32)
    for index, value in enumerate(values):
        value = value.astype(BF16)
        all_ref[start : start + levels] = value
        start += levels
        total += moved(value, (wanted & (over(lane, unit) == index)).astype(BF16))
    all_ref[comps + 16 : edges] = total.astype(BF16)
    leaving += started(
        [
            (all_ref.at[:edges], edge_hbm),
            (all_ref.at[:edges], all_hbm.at[:edges]),
            (all_ref.at[later:], all_hbm.at[later:]),
        ],
        sems.at[pl.ds(7, 3)],
    )
    for copy in leaving:
        copy.wait()


def advect_kernel(
    groups, count, rows, levels, all_ref, packed_ref, cx_ref, cy_ref, edge_ref, gathered
):
    comps = cx_ref.shape[0]
    columns = LANES
    width = columns // count
    cells = rows * width
    first = comps + 16 + levels
    edge_ref[...] = all_ref[:comps]

    def by_row(row):
        row = (row + rows) % rows
        return all_ref[first + row * comps : first + (row + 1) * comps]

    below = first + rows * comps
    terms = all_ref[below + 16 : below + 32].astype(F32)
    for index, ref in enumerate((cx_ref, cy_ref)):
        own = terms[4 * index : 4 * index + 4]
        own = own[:2] + own[2:]
        ref[...] = column_of(jnp.concatenate([own[:1], own[1:, : comps - columns]], axis=1), LANES)
    source, target = iota((columns, 2 * columns), 0), iota((columns, 2 * columns), 1)
    step = jnp.where(target < columns, -1, 1)
    sides = (source == within(target + step, columns)).astype(BF16)
    for row in range(rows):
        here = by_row(row).astype(F32)
        beside = moved(by_row(row), sides)
        along = upwind(here, cx_ref[...], beside[:, :columns], beside[:, columns:])
        across = upwind(
            here,
            cy_ref[...],
            by_row(row - 1).astype(F32),
            by_row(row + 1).astype(F32),
        )
        tile, place = divmod(row, count)
        gathered[tile * comps : (tile + 1) * comps, place * columns : (place + 1) * columns] = (
            here - along - across
        ).astype(BF16)
    for index in range(count):
        start = below + 32 + index * levels
        gathered[2 * comps :, index * columns : (index + 1) * columns] = all_ref[
            start : start + levels
        ]
    source = iota((count * columns, 2 * LANES), 0)
    lane = iota((count * columns, 2 * LANES), 1)
    for target in range(count // 2):
        origin = over(within(lane, LANES), width) * columns + within(lane, width)
        origin = origin + (2 * target + over(lane, LANES)) * width
        swap = (source == origin).astype(BF16)
        values = moved(gathered[...], swap).astype(BF16)
        for side in range(2):
            half = values[:, side * LANES : (side + 1) * LANES]
            packed_ref[2 * target + side, : 2 * comps, :] = half[: 2 * comps]
            start = 2 * comps + comps // groups
            packed_ref[2 * target + side, start : start + levels, :] = half[2 * comps :]
    size = comps // groups

    own = iota((size, LANES), 1)
    riders = jnp.zeros((size, LANES), F32)
    for group in range(groups):
        span = slice(group * size, (group + 1) * size)
        for index, term in enumerate(split(cx_ref[span]) + split(cy_ref[span])):
            riders = jnp.where(own == 5 * rows + 4 * group + index, term, riders)

    values = jnp.concatenate([all_ref[comps : comps + 16], all_ref[below : below + 16]], axis=0)
    spot, lanes = iota((columns, count * LANES), 0), iota((columns, count * LANES), 1)
    first_column = over(lanes, LANES) * width
    lanes = within(lanes, LANES) - 6 * rows
    inside = (lanes >= 0) & (lanes < width) & (spot == first_column + lanes)
    inland = moved(values, inside.astype(BF16))
    outside = ((lanes == 0) & (spot == first_column - 1)) | (
        (lanes == 1) & (spot == first_column + width)
    )
    shore = moved(values[:16], outside.astype(BF16))
    surfaces = [inland, shore]
    if size > 48:
        surfaces.append(jnp.zeros((size - 48, count * LANES), F32))
    surfaces = jnp.concatenate(surfaces, axis=0)

    source, target_lane = iota((cells, 2 * LANES), 0), iota((cells, 2 * LANES), 1)
    block = over(within(target_lane, LANES), rows)
    row_start = within(target_lane, rows) * width
    ends = []
    for group in range(groups):
        west = (target_lane < LANES) & (block == 2 * group) & (source == row_start + width - 1)
        east = (target_lane >= LANES) & (block == (2 * group + 7) % 8) & (source == row_start)
        ends.append((west | east).astype(BF16))
    source, target_lane = iota((LANES, 2 * LANES), 0), iota((LANES, 2 * LANES), 1)
    inner = within(target_lane, width)
    back = (target_lane - inner) & (LANES - 1)
    shifts = []
    for start in (0, 8):
        west = (target_lane < LANES) & (inner >= start) & (inner < start + 2)
        west = west & (source == back + width - 2 + inner - start)
        east = (target_lane >= LANES) & (inner >= start + 2) & (inner < start + 4)
        east = east & (source == back + inner - start - 2)
        shifts.append((west | east).astype(BF16))
    beside, beside_state = [], []
    half = levels // 2
    for target in range(count):
        total = jnp.zeros((size, 2 * LANES), F32)
        for group in range(groups):
            for tile in range(2):
                span = slice(tile * comps + group * size, tile * comps + (group + 1) * size)
                rows_of = slice(tile * LANES, (tile + 1) * LANES)
                total += moved(packed_ref[target, span, :], ends[group][rows_of])
        beside.append(total)
        start = 2 * comps + size
        low = moved(packed_ref[target, start : start + half, :], shifts[0])
        high = moved(packed_ref[target, start + half : start + levels, :], shifts[1])
        beside_state.append(low + high)
    for target in range(count):
        left, right = max(target - 1, 0), min(target + 1, count - 1)
        shared = riders + beside[left][:, :LANES] + beside[right][:, LANES:]
        shared += surfaces[:, target * LANES : (target + 1) * LANES]
        packed_ref[target, 2 * comps : 2 * comps + size, :] = shared.astype(BF16)
        start = 2 * comps + size + levels
        outer = beside_state[left][:, :LANES] + beside_state[right][:, LANES:]
        packed_ref[target, start : start + half, :] = outer.astype(BF16)


def coast_kernel(groups, count, rows, packed_ref, edge_ref, halo_ref, cx_ref, cy_ref, *out_refs):
    comps = cx_ref.shape[0]
    size = comps // groups
    levels = halo_ref.shape[0] - comps - 16
    cells = 2 * LANES
    width = cells // rows
    half = levels // 2
    block = over(iota((comps, LANES), 1), rows)
    near = jnp.where((block < 2) | (block >= 6), halo_ref[:comps], edge_ref[...])
    source, target = iota((LANES, 4 * LANES), 0), iota((LANES, 4 * LANES), 1)
    lane = within(target, LANES)
    row = within(lane, rows)
    kind = over(target, LANES)
    shift = jnp.where(
        kind == 0,
        within(lane - rows, LANES),
        jnp.where(
            kind == 1,
            within(lane + rows, LANES),
            lane - row + within(row + jnp.where(kind == 2, -1, 1), rows),
        ),
    )
    four = moved(near, (source == shift).astype(BF16))
    near = near.astype(F32)
    near = (
        near
        - upwind(near, cx_ref[...], four[:, :LANES], four[:, LANES : 2 * LANES])
        - upwind(near, cy_ref[...], four[:, 2 * LANES : 3 * LANES], four[:, 3 * LANES :])
    )
    source, target = iota((LANES, cells), 0), iota((LANES, cells), 1)
    column, row = within(target, width), over(target, width)
    spread = ((column == 0) & (source == 2 * rows + row)) | (
        (column == width - 1) & (source == 5 * rows + row)
    )
    ends = moved(near, spread.astype(BF16))
    shared = jnp.zeros((size, LANES), F32)
    source, target = iota((LANES, LANES), 0), iota((LANES, LANES), 1)
    for group in range(groups):
        there = over(target, rows)
        from_block = jnp.where(
            there == 2 * group, 1, jnp.where(there == (2 * group + 7) % 8, 6, LANES)
        )
        spread = source == from_block * rows + within(target, rows)
        shared += moved(near[group * size : (group + 1) * size], spread.astype(BF16))
    beyond = ((target == 6 * rows) & (source == LANES - 1)) | (
        (target == 6 * rows + 1) & (source == 0)
    )
    coast = moved(halo_ref[comps : comps + 16], beyond.astype(BF16))
    coast = [jnp.zeros((32, LANES), F32), coast]
    if size > 48:
        coast.append(jnp.zeros((size - 48, LANES), F32))
    shared += jnp.concatenate(coast, axis=0)
    inner = within(target, width)
    low = (source == target) & (inner < 4)
    high = (source == target - 8) & (inner >= 8) & (inner < 12)
    state = moved(halo_ref[comps + 16 : comps + 16 + half], low.astype(BF16))
    state += moved(halo_ref[comps + 16 + half :], high.astype(BF16))
    me = lax.axis_index(("cells", "lev"))
    for slot in range(count):
        target = lax.rem(me + slot, count)
        out_refs[slot][...] = packed_ref[target]
        place, lane = iota((size, LANES), 0), iota((size, LANES), 1)

        def patch(start, stop, where, values):
            old = out_refs[slot][start:stop].astype(F32)
            out_refs[slot][start:stop] = jnp.where(where, values, old).astype(BF16)

        def patch_ends(east):
            column = within(iota((comps, LANES), 1), width)
            for tile in range(2):
                values = ends[:, tile * LANES : (tile + 1) * LANES]
                where = column == (width - 1 if east else 0)
                patch(tile * comps, (tile + 1) * comps, where, values)
            own = over(lane, rows)
            where = (place >= 32) & (place < 48) & (lane == 6 * rows + (1 if east else 0))
            for group in range(groups):
                where = where | (own == ((2 * group + 7) % 8 if east else 2 * group))
            patch(2 * comps, 2 * comps + size, where, shared)
            start = 2 * comps + size
            start += levels
            inner = within(iota((half, LANES), 1), 8)
            patch(start, start + half, (inner >= 2) == east, state)

        @pl.when(target == 0)
        def _():
            patch_ends(False)

        @pl.when(target == count - 1)
        def _():
            patch_ends(True)


def steps_kernel(
    groups, count, rows, quartet_ref, coupler_ref, growth_ref, beside_ref, lateral_ref, *refs
):
    in_refs, refs = refs[:count], refs[count:]
    out_refs, refs = refs[:count], refs[count:]
    first_in, fresh, second_in, last, shares, factors, state, ends = refs
    total = quartet_ref.shape[0]
    comps = total // count
    size = comps // groups
    cells = 2 * LANES
    wide = 3 * LANES
    width = cells // rows
    levels = coupler_ref.shape[0] // 2
    half = shares.shape[1]
    lev_parts = levels // half
    tile_rows = rows * lev_parts // count
    me = lax.axis_index(("cells", "lev"))
    west_end = (me == 0) & (lax.axis_index("sect") == 0)
    east_end = (me == count - 1) & (lax.axis_index("sect") == lax.axis_size("sect") - 1)
    factors[:, 8:16] = column_of(0.1 * growth_ref[...], 8)

    source, target = iota((LANES, 2 * LANES), 0), iota((LANES, 2 * LANES), 1)
    block = over(target, rows)
    opened = []
    for group in range(groups):
        from_block = jnp.where(
            block == 0, 2 * group, jnp.where(block == 7, (2 * group + 7) % 8, LANES)
        )
        column = source == from_block * rows + within(target, rows)
        rider = source - (5 * rows + 4 * group)
        rider = (rider >= 0) & (rider < 4) & (over(rider, 2) == target - LANES)
        opened.append((column | rider).astype(BF16))
    source, target = iota((LANES, wide), 0), iota((LANES, wide), 1)
    on_side = target >= cells
    lane = within(target, width) + 6 * rows
    side = jnp.where(target < cells + rows, 0, 1) + 6 * rows
    repeat = (source == jnp.where(on_side, side, lane)).astype(BF16)
    place, target = iota((48, wide), 0), iota((48, wide), 1)
    on_side = target >= cells
    row_of_lane = jnp.where(on_side, within(target, rows), over(target, width))
    row_of_lane = jnp.where((place >= 32) == on_side, row_of_lane, -1) - within(place, tile_rows)
    terms = jnp.zeros((48, wide), F32)
    for slot in range(count):
        source = lax.rem(me - slot + count, count)
        start = pl.multiple_of(source * comps, 16)
        span = pl.ds(start, comps)
        for tile in range(2):
            values = in_refs[slot][tile * comps : (tile + 1) * comps]
            first_in[span, tile * LANES : (tile + 1) * LANES] = values
            values = values.astype(F32)
            first_in[span, wide + tile * LANES : wide + (tile + 1) * LANES] = (
                values * values
            ).astype(BF16)
        for group in range(groups):
            span = pl.ds(pl.multiple_of(start + group * size, 16), size)
            values = moved(in_refs[slot][2 * comps : 2 * comps + size], opened[group])
            first_in[span, cells:wide] = values[:, :LANES].astype(BF16)
            values_8 = values[:, LANES : LANES + 8]
            values = values[:, :LANES]
            first_in[span, wide + cells :] = (values * values).astype(BF16)
            factors[span, :8] = values_8
        place = 2 * comps
        spread = moved(in_refs[slot][place : place + 48], repeat)
        here = row_of_lane == over(source, lev_parts) * tile_rows
        terms += jnp.where(here, spread, 0.0)
        place += size
        state[source] = in_refs[slot][place : place + half]
        ends[source] = in_refs[slot][place + half :]

    place, source = iota((8, 48), 0), over(iota((8, 48), 1), tile_rows)
    source = jnp.where(source < 3, source, jnp.where(source < 8, source - 1, source - 8))
    skipped = over(iota((8, 48), 1), tile_rows) == 3
    terms = moved((place == jnp.where(skipped, 8, source)).astype(F32), terms.astype(BF16))

    def joined(rows_of):
        return rows_of[:1] + rows_of[1:2]

    surface, sea = joined(terms), terms[2:3]
    below = joined(terms[3:5])[:, :cells]
    wind = surface * surface

    def renew(values, products, growth, wind, sea):
        half = values.shape[1]
        paired, quad_square = products[:, :half], products[:, half:]
        below = 1.0 + 0.1 * values * values
        inverse = pl.reciprocal(below, approx=True)
        inverse = inverse * (2.0 - below * inverse)
        return (values + 0.3 * (values * paired - quad_square) + growth * wind) * inverse * sea

    part = total // 2
    for step in range(2):
        span = slice(step * part, (step + 1) * part)
        products = jnp.dot(quartet_ref[span, :], first_in[...], preferred_element_type=F32)
        values = first_in[span, :wide].astype(F32)
        fresh[span, :] = renew(values, products, factors[span, 8:9], wind, sea).astype(BF16)
    part = total // 8
    for step in range(8):
        span = slice(step * part, (step + 1) * part)
        beside = jnp.dot(fresh[span, :], beside_ref[...], preferred_element_type=F32)
        here = fresh[span, :cells].astype(F32)
        cx = jnp.broadcast_to(factors[span, 0:1], here.shape)
        cy = jnp.broadcast_to(factors[span, 1:2], here.shape)
        values = (
            here
            - upwind(here, cx, beside[:, :cells], beside[:, cells : 2 * cells])
            - upwind(here, cy, beside[:, 2 * cells : 3 * cells], beside[:, 3 * cells :])
        ).astype(BF16)
        second_in[span, :cells] = values
        values = values.astype(F32)
        second_in[span, cells:] = (values * values).astype(BF16)

    halves = iota((half, LANES), 1) < LANES // 2

    def collected(values):
        fields = []
        for kind in range(2):
            for part in range(lev_parts):
                tiles = []
                for pair in range(count // lev_parts // 2):
                    left = values[2 * pair * lev_parts + part].astype(F32)
                    right = values[(2 * pair + 1) * lev_parts + part].astype(F32)
                    if kind == 0:
                        right = pltpu.roll(right, LANES // 2, 1)
                    else:
                        left = pltpu.roll(left, LANES // 2, 1)
                    tiles.append(jnp.where(halves[: left.shape[0]], left, right))
                fields.append(jnp.concatenate(tiles, axis=1))
        return fields

    inner = jnp.concatenate(collected(state), axis=0)
    source, target = iota((cells, cells), 0), iota((cells, cells), 1)
    far = over(target, LANES)
    block = over(within(target, LANES), rows)
    order = jnp.where(block == 0, jnp.where(far == 0, 1, 0), jnp.where(far == 0, 2, 3))
    used = (block == 0) | (block == 7)
    spread = [
        ((source == within(target, rows) * width + order + 8 * high) & used).astype(BF16)
        for high in range(2)
    ]
    outer = []
    for field in collected(ends):
        outer += [moved(field, spread[0]), moved(field, spread[1])]
    outer = jnp.concatenate(outer, axis=0)

    def bounded(values):
        lane = iota(values.shape, 1)
        outside = (west_end & (lane < rows)) | (east_end & (lane >= LANES - rows))
        return jnp.where(outside, 0.0, values)

    outer = [bounded(outer[:, :LANES]), bounded(outer[:, LANES:])]

    def relaxed_once(here, lateral):
        level = within(iota(here.shape, 0), levels)
        lateral = lateral - 4.0 * here
        above = jnp.where(level == 0, 0.0, pltpu.roll(here, 1, 0))
        under = jnp.where(level == levels - 1, 0.0, pltpu.roll(here, 2 * levels - 1, 0))
        return here + 0.1 * lateral + 0.1 * (above + under - 2.0 * here)

    sign = jnp.where(iota((2 * levels, 1), 0) < levels, -0.3, 0.3)
    forced = jnp.dot(coupler_ref[...], fresh[...], preferred_element_type=F32) * sign
    here = jnp.concatenate([inner] + outer, axis=1)
    fields = relaxed_once(here[:, :wide], moved(here, lateral_ref[...])) + forced
    fields = jnp.concatenate([fields[:, :cells], bounded(fields[:, cells:])], axis=1)
    near = lateral_ref[:wide, :cells]
    head, tail = split(fields)
    fields = relaxed_once(fields[:, :cells], moved(head, near) + moved(tail, near))

    terms = jnp.concatenate([terms[:, :cells], bounded(terms[:, cells:])], axis=1)
    lateral = joined(moved(terms, near))
    calm = surface[:, :cells]
    calm = calm + 0.1 * (lateral - 4.0 * calm) + 0.1 * (below - 2.0 * calm)
    later = calm + forced[:1, :cells] - forced[levels : levels + 1, :cells]
    later = later * later

    part = total // 2
    for step in range(2):
        span = slice(step * part, (step + 1) * part)
        products = jnp.dot(quartet_ref[span, :], second_in[...], preferred_element_type=F32)
        values = second_in[span, :cells].astype(F32)
        done = renew(values, products, factors[span, 8:9], later, sea[:, :cells])
        last[span, :] = done.astype(BF16)

    forced = jnp.dot(coupler_ref[...], last[...], preferred_element_type=F32)
    carried = fields + sign * forced
    for target in range(count):
        cell_tile, lev_part = target // lev_parts, target % lev_parts
        columns = slice((cell_tile // 2) * LANES, (cell_tile // 2 + 1) * LANES)
        air = carried[lev_part * half : (lev_part + 1) * half, columns]
        sea_part = carried[levels + lev_part * half : levels + (lev_part + 1) * half, columns]
        if cell_tile % 2:
            air = pltpu.roll(air, LANES // 2, 1)
        else:
            sea_part = pltpu.roll(sea_part, LANES // 2, 1)
        shares[target] = jnp.where(halves, air, sea_part).astype(BF16)
    for slot in range(count):
        target = lax.rem(me + slot, count)
        span = pl.ds(pl.multiple_of(target * comps, 16), comps)
        out_refs[slot][:comps] = last[span, :LANES]
        out_refs[slot][comps : 2 * comps] = last[span, LANES:]
        out_refs[slot][2 * comps :] = shares[target]


def finish_kernel(count, swap_ref, *refs):
    in_refs, refs = refs[:count], refs[count:]
    energy_ref, air_ref, ocean_ref, gathered, wide, narrow = refs
    comps, rows, columns = energy_ref.shape
    levels, tile_rows, _ = air_ref.shape
    me = lax.axis_index(("cells", "lev"))
    for slot in range(count):
        source = lax.rem(me - slot + count, count)
        gathered[:, pl.ds(pl.multiple_of(source * columns, columns), columns)] = in_refs[slot][...]
    for pair in range(count // 2):
        lanes = slice(2 * pair * columns, 2 * (pair + 1) * columns)
        values = moved(gathered[...], swap_ref[:, lanes])
        for side in range(2):
            index = 2 * pair + side
            part = values[:, side * columns : (side + 1) * columns]
            for tile in range(rows // count):
                wide[pl.ds(tile * count + index, comps, stride=rows), :] = part[
                    tile * comps : (tile + 1) * comps
                ]
            kind, row = divmod(index, tile_rows)
            narrow[pl.ds(kind * levels * tile_rows + row, levels, stride=tile_rows), :] = part[
                2 * comps :
            ]
    energy_ref[...] = wide[...].reshape(comps, rows, columns).astype(energy_ref.dtype)
    size = levels * tile_rows
    air_ref[...] = narrow[:size, :].reshape(air_ref.shape)
    ocean_ref[...] = narrow[size:, :].reshape(ocean_ref.shape)


def spread_out(pieces, axes, count):
    received = [pieces[0]]
    for shift in range(1, count):
        pairs = [(index, (index + shift) % count) for index in range(count)]
        received.append(lax.ppermute(pieces[shift], axes, pairs))
    return received


def by_columns(
    spectrum, courant_x, courant_y, growth, quartet, coupler, atmosphere, ocean_state, sea_mask
):
    axes = ("cells", "lev")
    count = lax.axis_size("cells") * lax.axis_size("lev")
    sects = lax.axis_size("sect")
    comps, rows, columns = spectrum.shape
    total = comps * count
    width = columns // count
    cells = rows * width
    levels_own, tile_rows, _ = atmosphere.shape
    groups = 3
    whole = pl.BlockSpec(memory_space=VMEM)
    far = pl.BlockSpec(memory_space=pltpu.HBM)

    def shape(*dims, kind=BF16):
        return jax.ShapeDtypeStruct(dims, kind)

    def call(kernel, outs, *args, kept=(), place=whole, flops=0, mega=16):
        return pl.pallas_call(
            kernel,
            out_shape=outs,
            in_specs=[place] * len(args),
            out_specs=jax.tree.map(lambda _: place, outs),
            scratch_shapes=list(kept),
            compiler_params=pltpu.CompilerParams(vmem_limit_bytes=mega * 1024 * 1024),
            cost_estimate=pl.CostEstimate(flops=flops, bytes_accessed=4000000, transcendentals=0),
        )(*args)

    swap = jnp.asarray(swap_matrix(count, width), BF16)
    edges = comps + 16 + levels_own
    fields = (spectrum, atmosphere, ocean_state, sea_mask, courant_x[None], courant_y[None])
    fetched = shape(edges + rows * comps + 32 + count * levels_own, LANES)
    fetched, edge = call(
        edges_kernel,
        (fetched, shape(edges, LANES)),
        *fields,
        kept=[VMEM(array.shape, array.dtype) for array in fields + (fetched,)]
        + [VMEM((comps * rows, columns), F32), pltpu.SemaphoreType.DMA((10,))],
        place=far,
        mega=63,
    )
    halo = lax.ppermute(edge, "sect", [(0, 1), (1, 0)])

    size = 2 * comps + comps // groups + levels_own + levels_own // 2
    factor = shape(comps, LANES, kind=F32)
    packed, factor_x, factor_y, edge = call(
        functools.partial(advect_kernel, groups, count, rows, levels_own),
        (shape(count, size, LANES), factor, factor, shape(comps, LANES)),
        fetched,
        kept=[VMEM((2 * comps + levels_own, count * columns), BF16)],
        flops=2000000000,
    )
    pieces = call(
        functools.partial(coast_kernel, groups, count, rows),
        (shape(size, LANES),) * count,
        packed,
        edge,
        halo,
        factor_x,
        factor_y,
    )
    received = spread_out(pieces, axes, count)

    results = call(
        functools.partial(steps_kernel, groups, count, rows),
        (shape(2 * comps + levels_own, LANES),) * count,
        quartet,
        coupler,
        growth[None],
        jnp.asarray(neighbour_matrices(rows, width), BF16),
        jnp.asarray(lateral_matrix(rows, width), BF16),
        *received,
        kept=[
            VMEM((total, 6 * LANES), BF16),
            VMEM((total, 3 * LANES), BF16),
            VMEM((total, 4 * LANES), BF16),
            VMEM((total, cells), BF16),
            VMEM((count, levels_own, LANES), BF16),
            VMEM((total, LANES), F32),
            VMEM((count, levels_own, LANES), BF16),
            VMEM((count, levels_own // 2, LANES), BF16),
        ],
        mega=32,
    )
    returned = spread_out(results, axes, count)

    return call(
        functools.partial(finish_kernel, count),
        (
            shape(*spectrum.shape),
            shape(*atmosphere.shape, kind=F32),
            shape(*ocean_state.shape, kind=F32),
        ),
        swap,
        *returned,
        kept=[
            VMEM((2 * comps + levels_own, count * columns), BF16),
            VMEM((comps * rows, columns), F32),
            VMEM((2 * levels_own * tile_rows, columns), F32),
        ],
    )


def on_device(spectrum, *rest):
    atmosphere = rest[5]
    blocks = lax.axis_size("cells") * lax.axis_size("lev")
    comps, rows, columns = spectrum.shape
    fits = (
        columns == LANES
        and blocks == 8
        and lax.axis_size("sect") == 2
        and rows * (columns // blocks) == 2 * LANES
        and atmosphere.shape[1] * (columns // blocks) * 2 == LANES
        and comps % 48 == 0
        and comps >= 144
        and atmosphere.shape[0] % 16 == 0
        and NSTEP == 2
    )
    return (by_columns if fits else any_shape)(spectrum, *rest)


def solution(mesh):
    in_specs = (
        P(("cells", "lev"), "groups", "sect"),
        P(("cells", "lev")),
        P(("cells", "lev")),
        P(),
        P(),
        P(),
        P("lev", ("groups", "cells"), "sect"),
        P("lev", ("groups", "cells"), "sect"),
        P(("groups", "cells"), "sect"),
    )
    out_specs = (
        P(("cells", "lev"), "groups", "sect"),
        P("lev", ("groups", "cells"), "sect"),
        P("lev", ("groups", "cells"), "sect"),
    )
    return jax.shard_map(
        on_device, mesh=mesh, in_specs=in_specs, out_specs=out_specs, check_vma=False
    )
```

```python
import functools

import jax
import jax.numpy as jnp
import numpy as np
from jax import lax
from jax.experimental import pallas as pl
from jax.experimental.pallas import tpu as pltpu
from jax.sharding import PartitionSpec as P

NSTEP = 2
LANES = 128
F32 = jnp.float32
BF16 = jnp.bfloat16
VMEM = pltpu.VMEM


def from_root(block, axis, source):
    block = jnp.where(lax.axis_index(axis) == source, block, jnp.zeros_like(block))
    return lax.psum(block, axis)


def extended_2(block, sides, width, periodic):
    for axis, dim in sides:
        count = lax.axis_size(axis)
        forward = [(i, i + 1) for i in range(count - 1)]
        if periodic:
            forward.append((count - 1, 0))
        backward = [(target, source) for source, target in forward]
        low = lax.ppermute(
            lax.slice_in_dim(block, block.shape[dim] - width, None, axis=dim), axis, forward
        )
        high = lax.ppermute(lax.slice_in_dim(block, 0, width, axis=dim), axis, backward)
        block = jnp.concatenate([low, block, high], axis=dim)
    return block


def upwind(values, courant, before, after):
    return jnp.maximum(courant, 0.0) * (values - before) + jnp.minimum(courant, 0.0) * (
        after - values
    )


def any_shape(
    spectrum, courant_x, courant_y, growth, quartet, coupler, atmosphere, ocean_state, sea_mask
):
    cell_tiles = lax.axis_size("cells")
    lev_parts = lax.axis_size("lev")
    blocks = cell_tiles * lev_parts
    comps_own, rows_all, row_width = spectrum.shape
    total_comps = comps_own * blocks
    cell_rows = rows_all // blocks
    level_count = coupler.shape[0] // 2
    row_start = lax.axis_index("lev") * cell_rows
    shift_x = courant_x[:, None, None]
    shift_y = courant_y[:, None, None]
    sea_rows = (
        lax.dynamic_slice_in_dim(sea_mask, row_start, cell_rows, 0)
        .astype(jnp.float32)
        .reshape(1, cell_rows * row_width)
    )
    growth_column = growth[:, None]
    forcing_sign = jnp.array([-0.3, 0.3], jnp.float32)[:, None, None, None]
    state = jnp.stack([atmosphere, ocean_state])
    energy = spectrum
    for counter in range(NSTEP):
        surface = from_root(state[:, 0], "lev", 0)
        surface_wind = surface[0] - surface[1]
        wind_rows = lax.dynamic_slice_in_dim(
            surface_wind * surface_wind, row_start, cell_rows, 0
        ).reshape(1, cell_rows * row_width)
        padded = extended_2(energy, (("sect", 2),), 1, True)
        values = padded[:, :, 1:-1].astype(jnp.float32)
        west_side = padded[:, :, :-2].astype(jnp.float32)
        east_side = padded[:, :, 2:].astype(jnp.float32)
        moved = values - upwind(values, shift_x, west_side, east_side)
        moved = moved - upwind(
            values, shift_y, jnp.roll(values, 1, axis=1), jnp.roll(values, -1, axis=1)
        )
        advected = moved.astype(jnp.bfloat16)
        pieces = advected.reshape(1, comps_own, blocks, cell_rows, row_width)
        on_cells = lax.all_to_all(pieces, ("cells", "lev"), split_axis=2, concat_axis=0, tiled=True)
        on_cells = on_cells.reshape(total_comps, cell_rows * row_width)
        cell_values = on_cells.astype(jnp.float32)
        paired = jnp.dot(quartet, on_cells, preferred_element_type=jnp.float32)
        squared = (cell_values * cell_values).astype(jnp.bfloat16)
        quad_square = jnp.dot(quartet, squared, preferred_element_type=jnp.float32)
        fresh = (
            cell_values
            + 0.3 * (cell_values * paired - quad_square)
            + 0.1 * growth_column * wind_rows
        ) / (1.0 + 0.1 * cell_values * cell_values)
        fresh = (fresh * sea_rows).astype(jnp.bfloat16)
        profile = jnp.dot(coupler, fresh, preferred_element_type=jnp.float32).reshape(
            2, level_count, cell_rows, row_width
        )
        forcing = lax.all_to_all(profile, "lev", split_axis=1, concat_axis=2, tiled=True)
        returned = fresh.reshape(blocks, comps_own, 1, cell_rows, row_width)
        returned = lax.all_to_all(
            returned, ("cells", "lev"), split_axis=0, concat_axis=2, tiled=True
        )
        energy = returned.reshape(comps_own, rows_all, row_width)
        extended = extended_2(state, (("lev", 1), ("cells", 2), ("sect", 3)), 1, False)
        state = relaxed(extended, 1) + forcing_sign * forcing
    return (energy, state[0], state[1])


def relaxed(extended, first):
    centre = (slice(None),) * first + (slice(1, -1),) * 3
    middle = extended[centre]

    def moved(dim, start):
        where = list(centre)
        where[first + dim] = slice(start, extended.shape[first + dim] - 2 + start)
        return extended[tuple(where)]

    lateral = moved(1, 2) + moved(1, 0) + moved(2, 2) + moved(2, 0) - 4.0 * middle
    upright = moved(0, 2) + moved(0, 0) - 2.0 * middle
    return middle + 0.1 * lateral + 0.1 * upright


def iota(shape, dim):
    return lax.broadcasted_iota(jnp.int32, shape, dim)


def over(values, unit):
    return values >> (unit.bit_length() - 1)


def within(values, unit):
    return values & (unit - 1)


def moved(values, matrix):
    return jnp.dot(values.astype(BF16), matrix, preferred_element_type=F32)


def split(values):
    head = values.astype(BF16).astype(F32)
    return head, values - head


def column_of(row, lanes):
    return jnp.transpose(jnp.broadcast_to(row, (lanes, row.shape[1])))


def swap_matrix(count, unit):
    index = np.arange(count * count * unit)
    a, b, i = index // (count * unit), index // unit % count, index % unit
    return index[:, None] == ((b * count + a) * unit + i)[None, :]


def neighbour_matrices(rows, width):
    cells = rows * width
    row, column = np.divmod(np.arange(cells), width)
    west = np.where(column > 0, row * width + column - 1, cells + row)
    east = np.where(
        column < width - 1, row * width + column + 1, cells + LANES - rows + row
    )
    north = (row - 1) % rows * width + column
    south = (row + 1) % rows * width + column
    source = np.arange(cells + LANES)[:, None]
    return np.concatenate([source == move[None, :] for move in (west, east, north, south)], axis=1)


def lateral_matrix(rows, width):
    cells = rows * width
    far_west, west, east, far_east = cells + LANES, cells, cells + LANES - rows, cells + 2 * LANES - rows
    place = {}
    for row in range(rows):
        for column in range(width):
            place[row, column] = row * width + column
        for column, start in ((-2, far_west), (-1, west), (width, east), (width + 1, far_east)):
            place[row, column] = start + row
    matrix = np.zeros((cells + 2 * LANES, cells + LANES), bool)
    for (row, column), target in place.items():
        if not -1 <= column <= width:
            continue
        for near in ((row - 1, column), (row + 1, column), (row, column - 1), (row, column + 1)):
            if near in place:
                matrix[place[near], target] = True
    return matrix


def started(pairs, sems):
    copies = [pltpu.make_async_copy(*pair, sems.at[i]) for i, pair in enumerate(pairs)]
    for copy in copies:
        copy.start()
    return copies


def edges_kernel(
    x_hbm, air_hbm, ocean_hbm, sea_hbm, courant_x_hbm, courant_y_hbm, all_hbm, edge_hbm,
    x_ref, air_ref, ocean_ref, sea_ref, courant_x_ref, courant_y_ref, all_ref, wide, sems,
):
    comps, rows, columns = x_ref.shape
    levels, tile_rows, _ = air_ref.shape
    copies = started(
        [
            (x_hbm, x_ref),
            (air_hbm, air_ref),
            (ocean_hbm, ocean_ref),
            (sea_hbm, sea_ref),
            (courant_x_hbm, courant_x_ref),
            (courant_y_hbm, courant_y_ref),
        ],
        sems.at[pl.ds(0, 6)],
    )
    edges = comps + 16 + levels
    start = edges
    column, lane = iota((columns, LANES), 0), iota((columns, LANES), 1)

    block = within(over(lane, rows), 4)
    wanted = jnp.where(block < 2, columns - 2 + block, block - 2) == column
    row_of_lane = within(lane, rows)
    total = jnp.zeros((comps, LANES), F32)
    copies[0].wait()
    wide[...] = x_ref[...].astype(F32).reshape(comps * rows, columns)
    for row in range(rows):
        values = wide[pl.ds(row, comps, stride=rows), :].astype(BF16)
        all_ref[start : start + comps] = values
        start += comps
        total += moved(values, (wanted & (row_of_lane == row)).astype(BF16))
    all_ref[:comps] = total.astype(BF16)
    leaving = started(
        [(all_ref.at[edges:start], all_hbm.at[edges:start])], sems.at[pl.ds(6, 1)]
    )
    for copy in copies[1:]:
        copy.wait()
    owner = jnp.where(lax.axis_index("lev") == 0, 1.0, 0.0)
    head, tail = split((air_ref[0] - ocean_ref[0]) * owner)
    sea = sea_ref[...].astype(F32) * owner
    none = jnp.zeros_like(sea)
    all_ref[comps : comps + 16] = jnp.concatenate([head, tail, sea, none], axis=0).astype(BF16)
    head, tail = split((air_ref[1] - ocean_ref[1]) * owner)
    later = start
    below = jnp.concatenate([head, tail, none, none], axis=0)
    all_ref[start : start + 16] = below.astype(BF16)
    start += 16
    terms = []
    for ref in (courant_x_ref, courant_y_ref):
        for term in split(ref[...]):
            rest = jnp.zeros((1, 2 * columns - comps), F32)
            terms += [term[:, :columns], jnp.concatenate([term[:, columns:], rest], axis=1)]
    terms.append(jnp.zeros((8, columns), F32))
    all_ref[start : start + 16] = jnp.concatenate(terms, axis=0).astype(BF16)
    start += 16

    values = [ref[:, row, :] for ref in (air_ref, ocean_ref) for row in range(tile_rows)]
    unit = columns // len(values)
    inner = within(lane, unit)
    wanted = (jnp.where(inner < 2, columns - 2 + inner, inner - 2) == column) & (inner < 4)
    total = jnp.zeros((levels, LANES), F32)
    for index, value in enumerate(values):
        value = value.astype(BF16)
        all_ref[start : start + levels] = value
        start += levels
        total += moved(value, (wanted & (over(lane, unit) == index)).astype(BF16))
    all_ref[comps + 16 : edges] = total.astype(BF16)
    leaving += started(
        [
            (all_ref.at[:edges], edge_hbm),
            (all_ref.at[:edges], all_hbm.at[:edges]),
            (all_ref.at[later:], all_hbm.at[later:]),
        ],
        sems.at[pl.ds(7, 3)],
    )
    for copy in leaving:
        copy.wait()


def advect_kernel(
    groups, count, rows, levels, all_ref, packed_ref, cx_ref, cy_ref, edge_ref, gathered
):
    comps = cx_ref.shape[0]
    columns = LANES
    width = columns // count
    cells = rows * width
    first = comps + 16 + levels
    edge_ref[...] = all_ref[:comps]

    def by_row(row):
        row = (row + rows) % rows
        return all_ref[first + row * comps : first + (row + 1) * comps]

    below = first + rows * comps
    terms = all_ref[below + 16 : below + 32].astype(F32)
    for index, ref in enumerate((cx_ref, cy_ref)):
        own = terms[4 * index : 4 * index + 4]
        own = own[:2] + own[2:]
        ref[...] = column_of(jnp.concatenate([own[:1], own[1:, : comps - columns]], axis=1), LANES)
    source, target = iota((columns, 2 * columns), 0), iota((columns, 2 * columns), 1)
    step = jnp.where(target < columns, -1, 1)
    sides = (source == within(target + step, columns)).astype(BF16)
    for row in range(rows):
        here = by_row(row).astype(F32)
        beside = moved(by_row(row), sides)
        along = upwind(here, cx_ref[...], beside[:, :columns], beside[:, columns:])
        across = upwind(
            here,
            cy_ref[...],
            by_row(row - 1).astype(F32),
            by_row(row + 1).astype(F32),
        )
        tile, place = divmod(row, count)
        gathered[tile * comps : (tile + 1) * comps, place * columns : (place + 1) * columns] = (
            here - along - across
        ).astype(BF16)
    for index in range(count):
        start = below + 32 + index * levels
        gathered[2 * comps :, index * columns : (index + 1) * columns] = all_ref[
            start : start + levels
        ]
    source = iota((count * columns, 2 * LANES), 0)
    lane = iota((count * columns, 2 * LANES), 1)
    for target in range(count // 2):
        origin = over(within(lane, LANES), width) * columns + within(lane, width)
        origin = origin + (2 * target + over(lane, LANES)) * width
        swap = (source == origin).astype(BF16)
        values = moved(gathered[...], swap).astype(BF16)
        for side in range(2):
            half = values[:, side * LANES : (side + 1) * LANES]
            packed_ref[2 * target + side, : 2 * comps, :] = half[: 2 * comps]
            start = 2 * comps + comps // groups
            packed_ref[2 * target + side, start : start + levels, :] = half[2 * comps :]
    size = comps // groups

    own = iota((size, LANES), 1)
    riders = jnp.zeros((size, LANES), F32)
    for group in range(groups):
        span = slice(group * size, (group + 1) * size)
        for index, term in enumerate(split(cx_ref[span]) + split(cy_ref[span])):
            riders = jnp.where(own == 5 * rows + 4 * group + index, term, riders)

    values = jnp.concatenate([all_ref[comps : comps + 16], all_ref[below : below + 16]], axis=0)
    spot, lanes = iota((columns, count * LANES), 0), iota((columns, count * LANES), 1)
    first_column = over(lanes, LANES) * width
    lanes = within(lanes, LANES) - 6 * rows
    inside = (lanes >= 0) & (lanes < width) & (spot == first_column + lanes)
    inland = moved(values, inside.astype(BF16))
    outside = ((lanes == 0) & (spot == first_column - 1)) | (
        (lanes == 1) & (spot == first_column + width)
    )
    shore = moved(values[:16], outside.astype(BF16))
    surfaces = [inland, shore]
    if size > 48:
        surfaces.append(jnp.zeros((size - 48, count * LANES), F32))
    surfaces = jnp.concatenate(surfaces, axis=0)

    source, target_lane = iota((cells, 2 * LANES), 0), iota((cells, 2 * LANES), 1)
    block = over(within(target_lane, LANES), rows)
    row_start = within(target_lane, rows) * width
    ends = []
    for group in range(groups):
        west = (target_lane < LANES) & (block == 2 * group) & (source == row_start + width - 1)
        east = (target_lane >= LANES) & (block == (2 * group + 7) % 8) & (source == row_start)
        ends.append((west | east).astype(BF16))
    source, target_lane = iota((LANES, 2 * LANES), 0), iota((LANES, 2 * LANES), 1)
    inner = within(target_lane, width)
    back = (target_lane - inner) & (LANES - 1)
    shifts = []
    for start in (0, 8):
        west = (target_lane < LANES) & (inner >= start) & (inner < start + 2)
        west = west & (source == back + width - 2 + inner - start)
        east = (target_lane >= LANES) & (inner >= start + 2) & (inner < start + 4)
        east = east & (source == back + inner - start - 2)
        shifts.append((west | east).astype(BF16))
    beside, beside_state = [], []
    half = levels // 2
    for target in range(count):
        total = jnp.zeros((size, 2 * LANES), F32)
        for group in range(groups):
            for tile in range(2):
                span = slice(tile * comps + group * size, tile * comps + (group + 1) * size)
                rows_of = slice(tile * LANES, (tile + 1) * LANES)
                total += moved(packed_ref[target, span, :], ends[group][rows_of])
        beside.append(total)
        start = 2 * comps + size
        low = moved(packed_ref[target, start : start + half, :], shifts[0])
        high = moved(packed_ref[target, start + half : start + levels, :], shifts[1])
        beside_state.append(low + high)
    for target in range(count):
        left, right = max(target - 1, 0), min(target + 1, count - 1)
        shared = riders + beside[left][:, :LANES] + beside[right][:, LANES:]
        shared += surfaces[:, target * LANES : (target + 1) * LANES]
        packed_ref[target, 2 * comps : 2 * comps + size, :] = shared.astype(BF16)
        start = 2 * comps + size + levels
        outer = beside_state[left][:, :LANES] + beside_state[right][:, LANES:]
        packed_ref[target, start : start + half, :] = outer.astype(BF16)


def coast_kernel(groups, count, rows, packed_ref, edge_ref, halo_ref, cx_ref, cy_ref, *out_refs):
    comps = cx_ref.shape[0]
    size = comps // groups
    levels = halo_ref.shape[0] - comps - 16
    cells = 2 * LANES
    width = cells // rows
    half = levels // 2
    block = over(iota((comps, LANES), 1), rows)
    near = jnp.where((block < 2) | (block >= 6), halo_ref[:comps], edge_ref[...])
    source, target = iota((LANES, 4 * LANES), 0), iota((LANES, 4 * LANES), 1)
    lane = within(target, LANES)
    row = within(lane, rows)
    kind = over(target, LANES)
    shift = jnp.where(
        kind == 0,
        within(lane - rows, LANES),
        jnp.where(
            kind == 1,
            within(lane + rows, LANES),
            lane - row + within(row + jnp.where(kind == 2, -1, 1), rows),
        ),
    )
    four = moved(near, (source == shift).astype(BF16))
    near = near.astype(F32)
    near = (
        near
        - upwind(near, cx_ref[...], four[:, :LANES], four[:, LANES : 2 * LANES])
        - upwind(near, cy_ref[...], four[:, 2 * LANES : 3 * LANES], four[:, 3 * LANES :])
    )
    source, target = iota((LANES, cells), 0), iota((LANES, cells), 1)
    column, row = within(target, width), over(target, width)
    spread = ((column == 0) & (source == 2 * rows + row)) | (
        (column == width - 1) & (source == 5 * rows + row)
    )
    ends = moved(near, spread.astype(BF16))
    shared = jnp.zeros((size, LANES), F32)
    source, target = iota((LANES, LANES), 0), iota((LANES, LANES), 1)
    for group in range(groups):
        there = over(target, rows)
        from_block = jnp.where(
            there == 2 * group, 1, jnp.where(there == (2 * group + 7) % 8, 6, LANES)
        )
        spread = source == from_block * rows + within(target, rows)
        shared += moved(near[group * size : (group + 1) * size], spread.astype(BF16))
    beyond = ((target == 6 * rows) & (source == LANES - 1)) | (
        (target == 6 * rows + 1) & (source == 0)
    )
    coast = moved(halo_ref[comps : comps + 16], beyond.astype(BF16))
    coast = [jnp.zeros((32, LANES), F32), coast]
    if size > 48:
        coast.append(jnp.zeros((size - 48, LANES), F32))
    shared += jnp.concatenate(coast, axis=0)
    inner = within(target, width)
    low = (source == target) & (inner < 4)
    high = (source == target - 8) & (inner >= 8) & (inner < 12)
    state = moved(halo_ref[comps + 16 : comps + 16 + half], low.astype(BF16))
    state += moved(halo_ref[comps + 16 + half :], high.astype(BF16))
    me = lax.axis_index(("cells", "lev"))
    for slot in range(count):
        target = lax.rem(me + first_order(count)[slot], count)
        out_refs[slot][...] = packed_ref[target]
        place, lane = iota((size, LANES), 0), iota((size, LANES), 1)

        def patch(start, stop, where, values):
            old = out_refs[slot][start:stop].astype(F32)
            out_refs[slot][start:stop] = jnp.where(where, values, old).astype(BF16)

        def patch_ends(east):
            column = within(iota((comps, LANES), 1), width)
            for tile in range(2):
                values = ends[:, tile * LANES : (tile + 1) * LANES]
                where = column == (width - 1 if east else 0)
                patch(tile * comps, (tile + 1) * comps, where, values)
            own = over(lane, rows)
            where = (place >= 32) & (place < 48) & (lane == 6 * rows + (1 if east else 0))
            for group in range(groups):
                where = where | (own == ((2 * group + 7) % 8 if east else 2 * group))
            patch(2 * comps, 2 * comps + size, where, shared)
            start = 2 * comps + size
            start += levels
            inner = within(iota((half, LANES), 1), 8)
            patch(start, start + half, (inner >= 2) == east, state)

        @pl.when(target == 0)
        def _():
            patch_ends(False)

        @pl.when(target == count - 1)
        def _():
            patch_ends(True)


def steps_kernel(
    groups, count, rows, quartet_ref, coupler_ref, growth_ref, beside_ref, lateral_ref, *refs
):
    in_refs, refs = refs[:count], refs[count:]
    out_refs, refs = refs[:count], refs[count:]
    first_in, fresh, second_in, last, shares, factors, state, ends = refs
    total = quartet_ref.shape[0]
    comps = total // count
    size = comps // groups
    cells = 2 * LANES
    wide = 3 * LANES
    width = cells // rows
    levels = coupler_ref.shape[0] // 2
    half = shares.shape[1]
    lev_parts = levels // half
    tile_rows = rows * lev_parts // count
    me = lax.axis_index(("cells", "lev"))
    west_end = (me == 0) & (lax.axis_index("sect") == 0)
    east_end = (me == count - 1) & (lax.axis_index("sect") == lax.axis_size("sect") - 1)
    factors[:, 8:16] = column_of(0.1 * growth_ref[...], 8)

    source, target = iota((LANES, 2 * LANES), 0), iota((LANES, 2 * LANES), 1)
    block = over(target, rows)
    opened = []
    for group in range(groups):
        from_block = jnp.where(
            block == 0, 2 * group, jnp.where(block == 7, (2 * group + 7) % 8, LANES)
        )
        column = source == from_block * rows + within(target, rows)
        rider = source - (5 * rows + 4 * group)
        rider = (rider >= 0) & (rider < 4) & (over(rider, 2) == target - LANES)
        opened.append((column | rider).astype(BF16))
    source, target = iota((LANES, wide), 0), iota((LANES, wide), 1)
    on_side = target >= cells
    lane = within(target, width) + 6 * rows
    side = jnp.where(target < cells + rows, 0, 1) + 6 * rows
    repeat = (source == jnp.where(on_side, side, lane)).astype(BF16)
    place, target = iota((48, wide), 0), iota((48, wide), 1)
    on_side = target >= cells
    row_of_lane = jnp.where(on_side, within(target, rows), over(target, width))
    row_of_lane = jnp.where((place >= 32) == on_side, row_of_lane, -1) - within(place, tile_rows)
    terms = jnp.zeros((48, wide), F32)
    for slot in range(count):
        source = lax.rem(me - first_order(count)[slot] + count, count)
        start = pl.multiple_of(source * comps, 16)
        span = pl.ds(start, comps)
        for tile in range(2):
            values = in_refs[slot][tile * comps : (tile + 1) * comps]
            first_in[span, tile * LANES : (tile + 1) * LANES] = values
            values = values.astype(F32)
            first_in[span, wide + tile * LANES : wide + (tile + 1) * LANES] = (
                values * values
            ).astype(BF16)
        for group in range(groups):
            span = pl.ds(pl.multiple_of(start + group * size, 16), size)
            values = moved(in_refs[slot][2 * comps : 2 * comps + size], opened[group])
            first_in[span, cells:wide] = values[:, :LANES].astype(BF16)
            values_8 = values[:, LANES : LANES + 8]
            values = values[:, :LANES]
            first_in[span, wide + cells :] = (values * values).astype(BF16)
            factors[span, :8] = values_8
        place = 2 * comps
        spread = moved(in_refs[slot][place : place + 48], repeat)
        here = row_of_lane == over(source, lev_parts) * tile_rows
        terms += jnp.where(here, spread, 0.0)
        place += size
        state[source] = in_refs[slot][place : place + half]
        ends[source] = in_refs[slot][place + half :]

    place, source = iota((8, 48), 0), over(iota((8, 48), 1), tile_rows)
    source = jnp.where(source < 3, source, jnp.where(source < 8, source - 1, source - 8))
    skipped = over(iota((8, 48), 1), tile_rows) == 3
    terms = moved((place == jnp.where(skipped, 8, source)).astype(F32), terms.astype(BF16))

    def joined(rows_of):
        return rows_of[:1] + rows_of[1:2]

    surface, sea = joined(terms), terms[2:3]
    below = joined(terms[3:5])[:, :cells]
    wind = surface * surface

    def renew(values, products, growth, wind, sea):
        half = values.shape[1]
        paired, quad_square = products[:, :half], products[:, half:]
        below = 1.0 + 0.1 * values * values
        inverse = pl.reciprocal(below, approx=True)
        inverse = inverse * (2.0 - below * inverse)
        return (values + 0.3 * (values * paired - quad_square) + growth * wind) * inverse * sea

    part = total // 2
    for step in range(2):
        span = slice(step * part, (step + 1) * part)
        products = jnp.dot(quartet_ref[span, :], first_in[...], preferred_element_type=F32)
        values = first_in[span, :wide].astype(F32)
        fresh[span, :] = renew(values, products, factors[span, 8:9], wind, sea).astype(BF16)
    part = total // 8
    for step in range(8):
        span = slice(step * part, (step + 1) * part)
        beside = jnp.dot(fresh[span, :], beside_ref[...], preferred_element_type=F32)
        here = fresh[span, :cells].astype(F32)
        cx = jnp.broadcast_to(factors[span, 0:1], here.shape)
        cy = jnp.broadcast_to(factors[span, 1:2], here.shape)
        values = (
            here
            - upwind(here, cx, beside[:, :cells], beside[:, cells : 2 * cells])
            - upwind(here, cy, beside[:, 2 * cells : 3 * cells], beside[:, 3 * cells :])
        ).astype(BF16)
        second_in[span, :cells] = values
        values = values.astype(F32)
        second_in[span, cells:] = (values * values).astype(BF16)

    halves = iota((half, LANES), 1) < LANES // 2

    def collected(values):
        fields = []
        for kind in range(2):
            for part in range(lev_parts):
                tiles = []
                for pair in range(count // lev_parts // 2):
                    left = values[2 * pair * lev_parts + part].astype(F32)
                    right = values[(2 * pair + 1) * lev_parts + part].astype(F32)
                    if kind == 0:
                        right = pltpu.roll(right, LANES // 2, 1)
                    else:
                        left = pltpu.roll(left, LANES // 2, 1)
                    tiles.append(jnp.where(halves[: left.shape[0]], left, right))
                fields.append(jnp.concatenate(tiles, axis=1))
        return fields

    inner = jnp.concatenate(collected(state), axis=0)
    source, target = iota((cells, cells), 0), iota((cells, cells), 1)
    far = over(target, LANES)
    block = over(within(target, LANES), rows)
    order = jnp.where(block == 0, jnp.where(far == 0, 1, 0), jnp.where(far == 0, 2, 3))
    used = (block == 0) | (block == 7)
    spread = [
        ((source == within(target, rows) * width + order + 8 * high) & used).astype(BF16)
        for high in range(2)
    ]
    outer = []
    for field in collected(ends):
        outer += [moved(field, spread[0]), moved(field, spread[1])]
    outer = jnp.concatenate(outer, axis=0)

    def bounded(values):
        lane = iota(values.shape, 1)
        outside = (west_end & (lane < rows)) | (east_end & (lane >= LANES - rows))
        return jnp.where(outside, 0.0, values)

    outer = [bounded(outer[:, :LANES]), bounded(outer[:, LANES:])]

    def relaxed_once(here, lateral):
        level = within(iota(here.shape, 0), levels)
        lateral = lateral - 4.0 * here
        above = jnp.where(level == 0, 0.0, pltpu.roll(here, 1, 0))
        under = jnp.where(level == levels - 1, 0.0, pltpu.roll(here, 2 * levels - 1, 0))
        return here + 0.1 * lateral + 0.1 * (above + under - 2.0 * here)

    sign = jnp.where(iota((2 * levels, 1), 0) < levels, -0.3, 0.3)
    forced = jnp.dot(coupler_ref[...], fresh[...], preferred_element_type=F32) * sign
    here = jnp.concatenate([inner] + outer, axis=1)
    fields = relaxed_once(here[:, :wide], moved(here, lateral_ref[...])) + forced
    fields = jnp.concatenate([fields[:, :cells], bounded(fields[:, cells:])], axis=1)
    near = lateral_ref[:wide, :cells]
    head, tail = split(fields)
    fields = relaxed_once(fields[:, :cells], moved(head, near) + moved(tail, near))

    terms = jnp.concatenate([terms[:, :cells], bounded(terms[:, cells:])], axis=1)
    lateral = joined(moved(terms, near))
    calm = surface[:, :cells]
    calm = calm + 0.1 * (lateral - 4.0 * calm) + 0.1 * (below - 2.0 * calm)
    later = calm + forced[:1, :cells] - forced[levels : levels + 1, :cells]
    later = later * later

    part = total // 2
    for step in range(2):
        span = slice(step * part, (step + 1) * part)
        products = jnp.dot(quartet_ref[span, :], second_in[...], preferred_element_type=F32)
        values = second_in[span, :cells].astype(F32)
        done = renew(values, products, factors[span, 8:9], later, sea[:, :cells])
        last[span, :] = done.astype(BF16)

    forced = jnp.dot(coupler_ref[...], last[...], preferred_element_type=F32)
    carried = fields + sign * forced
    for target in range(count):
        cell_tile, lev_part = target // lev_parts, target % lev_parts
        columns = slice((cell_tile // 2) * LANES, (cell_tile // 2 + 1) * LANES)
        air = carried[lev_part * half : (lev_part + 1) * half, columns]
        sea_part = carried[levels + lev_part * half : levels + (lev_part + 1) * half, columns]
        if cell_tile % 2:
            air = pltpu.roll(air, LANES // 2, 1)
        else:
            sea_part = pltpu.roll(sea_part, LANES // 2, 1)
        shares[target] = jnp.where(halves, air, sea_part).astype(BF16)
    for slot in range(count):
        target = lax.rem(me + last_order(count)[slot], count)
        span = pl.ds(pl.multiple_of(target * comps, 16), comps)
        out_refs[slot][:comps] = last[span, :LANES]
        out_refs[slot][comps : 2 * comps] = last[span, LANES:]
        out_refs[slot][2 * comps :] = shares[target]


def finish_kernel(count, swap_ref, *refs):
    in_refs, refs = refs[:count], refs[count:]
    energy_ref, air_ref, ocean_ref, gathered, wide, narrow = refs
    comps, rows, columns = energy_ref.shape
    levels, tile_rows, _ = air_ref.shape
    me = lax.axis_index(("cells", "lev"))
    for slot in range(count):
        source = lax.rem(me - last_order(count)[slot] + count, count)
        gathered[:, pl.ds(pl.multiple_of(source * columns, columns), columns)] = in_refs[slot][...]
    for pair in range(count // 2):
        lanes = slice(2 * pair * columns, 2 * (pair + 1) * columns)
        values = moved(gathered[...], swap_ref[:, lanes])
        for side in range(2):
            index = 2 * pair + side
            part = values[:, side * columns : (side + 1) * columns]
            for tile in range(rows // count):
                wide[pl.ds(tile * count + index, comps, stride=rows), :] = part[
                    tile * comps : (tile + 1) * comps
                ]
            kind, row = divmod(index, tile_rows)
            narrow[pl.ds(kind * levels * tile_rows + row, levels, stride=tile_rows), :] = part[
                2 * comps :
            ]
    energy_ref[...] = wide[...].reshape(comps, rows, columns).astype(energy_ref.dtype)
    size = levels * tile_rows
    air_ref[...] = narrow[:size, :].reshape(air_ref.shape)
    ocean_ref[...] = narrow[size:, :].reshape(ocean_ref.shape)


def first_order(count):
    return tuple(range(count))


def last_order(count):
    return (0, count - 2, count - 1) + tuple(range(1, count - 2))


def spread_out(pieces, axes, order):
    count = len(pieces)
    received = [pieces[0]]
    for slot in range(1, count):
        pairs = [(index, (index + order[slot]) % count) for index in range(count)]
        received.append(lax.ppermute(pieces[slot], axes, pairs))
    return received


def by_columns(
    spectrum, courant_x, courant_y, growth, quartet, coupler, atmosphere, ocean_state, sea_mask
):
    axes = ("cells", "lev")
    count = lax.axis_size("cells") * lax.axis_size("lev")
    sects = lax.axis_size("sect")
    comps, rows, columns = spectrum.shape
    total = comps * count
    width = columns // count
    cells = rows * width
    levels_own, tile_rows, _ = atmosphere.shape
    groups = 3
    whole = pl.BlockSpec(memory_space=VMEM)
    far = pl.BlockSpec(memory_space=pltpu.HBM)

    def shape(*dims, kind=BF16):
        return jax.ShapeDtypeStruct(dims, kind)

    def call(kernel, outs, *args, kept=(), place=whole, flops=0, mega=16):
        return pl.pallas_call(
            kernel,
            out_shape=outs,
            in_specs=[place] * len(args),
            out_specs=jax.tree.map(lambda _: place, outs),
            scratch_shapes=list(kept),
            compiler_params=pltpu.CompilerParams(vmem_limit_bytes=mega * 1024 * 1024),
            cost_estimate=pl.CostEstimate(flops=flops, bytes_accessed=4000000, transcendentals=0),
        )(*args)

    swap = jnp.asarray(swap_matrix(count, width), BF16)
    edges = comps + 16 + levels_own
    fields = (spectrum, atmosphere, ocean_state, sea_mask, courant_x[None], courant_y[None])
    fetched = shape(edges + rows * comps + 32 + count * levels_own, LANES)
    fetched, edge = call(
        edges_kernel,
        (fetched, shape(edges, LANES)),
        *fields,
        kept=[VMEM(array.shape, array.dtype) for array in fields + (fetched,)]
        + [VMEM((comps * rows, columns), F32), pltpu.SemaphoreType.DMA((10,))],
        place=far,
        mega=63,
    )
    halo = lax.ppermute(edge, "sect", [(0, 1), (1, 0)])

    size = 2 * comps + comps // groups + levels_own + levels_own // 2
    factor = shape(comps, LANES, kind=F32)
    packed, factor_x, factor_y, edge = call(
        functools.partial(advect_kernel, groups, count, rows, levels_own),
        (shape(count, size, LANES), factor, factor, shape(comps, LANES)),
        fetched,
        kept=[VMEM((2 * comps + levels_own, count * columns), BF16)],
        flops=2000000000,
    )
    pieces = call(
        functools.partial(coast_kernel, groups, count, rows),
        (shape(size, LANES),) * count,
        packed,
        edge,
        halo,
        factor_x,
        factor_y,
    )
    received = spread_out(pieces, axes, first_order(count))

    results = call(
        functools.partial(steps_kernel, groups, count, rows),
        (shape(2 * comps + levels_own, LANES),) * count,
        quartet,
        coupler,
        growth[None],
        jnp.asarray(neighbour_matrices(rows, width), BF16),
        jnp.asarray(lateral_matrix(rows, width), BF16),
        *received,
        kept=[
            VMEM((total, 6 * LANES), BF16),
            VMEM((total, 3 * LANES), BF16),
            VMEM((total, 4 * LANES), BF16),
            VMEM((total, cells), BF16),
            VMEM((count, levels_own, LANES), BF16),
            VMEM((total, LANES), F32),
            VMEM((count, levels_own, LANES), BF16),
            VMEM((count, levels_own // 2, LANES), BF16),
        ],
        mega=32,
    )
    returned = spread_out(results, axes, last_order(count))

    return call(
        functools.partial(finish_kernel, count),
        (
            shape(*spectrum.shape),
            shape(*atmosphere.shape, kind=F32),
            shape(*ocean_state.shape, kind=F32),
        ),
        swap,
        *returned,
        kept=[
            VMEM((2 * comps + levels_own, count * columns), BF16),
            VMEM((comps * rows, columns), F32),
            VMEM((2 * levels_own * tile_rows, columns), F32),
        ],
    )


def on_device(spectrum, *rest):
    atmosphere = rest[5]
    blocks = lax.axis_size("cells") * lax.axis_size("lev")
    comps, rows, columns = spectrum.shape
    fits = (
        columns == LANES
        and blocks == 8
        and lax.axis_size("sect") == 2
        and rows * (columns // blocks) == 2 * LANES
        and atmosphere.shape[1] * (columns // blocks) * 2 == LANES
        and comps % 48 == 0
        and comps >= 144
        and atmosphere.shape[0] % 16 == 0
        and NSTEP == 2
    )
    return (by_columns if fits else any_shape)(spectrum, *rest)


def solution(mesh):
    in_specs = (
        P(("cells", "lev"), "groups", "sect"),
        P(("cells", "lev")),
        P(("cells", "lev")),
        P(),
        P(),
        P(),
        P("lev", ("groups", "cells"), "sect"),
        P("lev", ("groups", "cells"), "sect"),
        P(("groups", "cells"), "sect"),
    )
    out_specs = (
        P(("cells", "lev"), "groups", "sect"),
        P("lev", ("groups", "cells"), "sect"),
        P("lev", ("groups", "cells"), "sect"),
    )
    return jax.shard_map(
        on_device, mesh=mesh, in_specs=in_specs, out_specs=out_specs, check_vma=False
    )
```

```python
import functools

import jax
import jax.numpy as jnp
import numpy as np
from jax import lax
from jax.experimental import pallas as pl
from jax.experimental.pallas import tpu as pltpu
from jax.sharding import PartitionSpec as P

NSTEP = 2
LANES = 128
F32 = jnp.float32
BF16 = jnp.bfloat16
VMEM = pltpu.VMEM


def from_root(block, axis, source):
    block = jnp.where(lax.axis_index(axis) == source, block, jnp.zeros_like(block))
    return lax.psum(block, axis)


def extended_2(block, sides, width, periodic):
    for axis, dim in sides:
        count = lax.axis_size(axis)
        forward = [(i, i + 1) for i in range(count - 1)]
        if periodic:
            forward.append((count - 1, 0))
        backward = [(target, source) for source, target in forward]
        low = lax.ppermute(
            lax.slice_in_dim(block, block.shape[dim] - width, None, axis=dim), axis, forward
        )
        high = lax.ppermute(lax.slice_in_dim(block, 0, width, axis=dim), axis, backward)
        block = jnp.concatenate([low, block, high], axis=dim)
    return block


def upwind(values, courant, before, after):
    return jnp.maximum(courant, 0.0) * (values - before) + jnp.minimum(courant, 0.0) * (
        after - values
    )


def any_shape(
    spectrum, courant_x, courant_y, growth, quartet, coupler, atmosphere, ocean_state, sea_mask
):
    cell_tiles = lax.axis_size("cells")
    lev_parts = lax.axis_size("lev")
    blocks = cell_tiles * lev_parts
    comps_own, rows_all, row_width = spectrum.shape
    total_comps = comps_own * blocks
    cell_rows = rows_all // blocks
    level_count = coupler.shape[0] // 2
    row_start = lax.axis_index("lev") * cell_rows
    shift_x = courant_x[:, None, None]
    shift_y = courant_y[:, None, None]
    sea_rows = (
        lax.dynamic_slice_in_dim(sea_mask, row_start, cell_rows, 0)
        .astype(jnp.float32)
        .reshape(1, cell_rows * row_width)
    )
    growth_column = growth[:, None]
    forcing_sign = jnp.array([-0.3, 0.3], jnp.float32)[:, None, None, None]
    state = jnp.stack([atmosphere, ocean_state])
    energy = spectrum
    for counter in range(NSTEP):
        surface = from_root(state[:, 0], "lev", 0)
        surface_wind = surface[0] - surface[1]
        wind_rows = lax.dynamic_slice_in_dim(
            surface_wind * surface_wind, row_start, cell_rows, 0
        ).reshape(1, cell_rows * row_width)
        padded = extended_2(energy, (("sect", 2),), 1, True)
        values = padded[:, :, 1:-1].astype(jnp.float32)
        west_side = padded[:, :, :-2].astype(jnp.float32)
        east_side = padded[:, :, 2:].astype(jnp.float32)
        moved = values - upwind(values, shift_x, west_side, east_side)
        moved = moved - upwind(
            values, shift_y, jnp.roll(values, 1, axis=1), jnp.roll(values, -1, axis=1)
        )
        advected = moved.astype(jnp.bfloat16)
        pieces = advected.reshape(1, comps_own, blocks, cell_rows, row_width)
        on_cells = lax.all_to_all(pieces, ("cells", "lev"), split_axis=2, concat_axis=0, tiled=True)
        on_cells = on_cells.reshape(total_comps, cell_rows * row_width)
        cell_values = on_cells.astype(jnp.float32)
        paired = jnp.dot(quartet, on_cells, preferred_element_type=jnp.float32)
        squared = (cell_values * cell_values).astype(jnp.bfloat16)
        quad_square = jnp.dot(quartet, squared, preferred_element_type=jnp.float32)
        fresh = (
            cell_values
            + 0.3 * (cell_values * paired - quad_square)
            + 0.1 * growth_column * wind_rows
        ) / (1.0 + 0.1 * cell_values * cell_values)
        fresh = (fresh * sea_rows).astype(jnp.bfloat16)
        profile = jnp.dot(coupler, fresh, preferred_element_type=jnp.float32).reshape(
            2, level_count, cell_rows, row_width
        )
        forcing = lax.all_to_all(profile, "lev", split_axis=1, concat_axis=2, tiled=True)
        returned = fresh.reshape(blocks, comps_own, 1, cell_rows, row_width)
        returned = lax.all_to_all(
            returned, ("cells", "lev"), split_axis=0, concat_axis=2, tiled=True
        )
        energy = returned.reshape(comps_own, rows_all, row_width)
        extended = extended_2(state, (("lev", 1), ("cells", 2), ("sect", 3)), 1, False)
        state = relaxed(extended, 1) + forcing_sign * forcing
    return (energy, state[0], state[1])


def relaxed(extended, first):
    centre = (slice(None),) * first + (slice(1, -1),) * 3
    middle = extended[centre]

    def moved(dim, start):
        where = list(centre)
        where[first + dim] = slice(start, extended.shape[first + dim] - 2 + start)
        return extended[tuple(where)]

    lateral = moved(1, 2) + moved(1, 0) + moved(2, 2) + moved(2, 0) - 4.0 * middle
    upright = moved(0, 2) + moved(0, 0) - 2.0 * middle
    return middle + 0.1 * lateral + 0.1 * upright


def iota(shape, dim):
    return lax.broadcasted_iota(jnp.int32, shape, dim)


def over(values, unit):
    return values >> (unit.bit_length() - 1)


def within(values, unit):
    return values & (unit - 1)


def moved(values, matrix):
    return jnp.dot(values.astype(BF16), matrix, preferred_element_type=F32)


def split(values):
    head = values.astype(BF16).astype(F32)
    return head, values - head


def column_of(row, lanes):
    return jnp.transpose(jnp.broadcast_to(row, (lanes, row.shape[1])))


def swap_matrix(count, unit):
    index = np.arange(count * count * unit)
    a, b, i = index // (count * unit), index // unit % count, index % unit
    return index[:, None] == ((b * count + a) * unit + i)[None, :]


def neighbour_matrices(rows, width):
    cells = rows * width
    row, column = np.divmod(np.arange(cells), width)
    west = np.where(column > 0, row * width + column - 1, cells + row)
    east = np.where(
        column < width - 1, row * width + column + 1, cells + LANES - rows + row
    )
    north = (row - 1) % rows * width + column
    south = (row + 1) % rows * width + column
    source = np.arange(cells + LANES)[:, None]
    return np.concatenate([source == move[None, :] for move in (west, east, north, south)], axis=1)


def lateral_matrix(rows, width):
    cells = rows * width
    far_west, west, east, far_east = cells + LANES, cells, cells + LANES - rows, cells + 2 * LANES - rows
    place = {}
    for row in range(rows):
        for column in range(width):
            place[row, column] = row * width + column
        for column, start in ((-2, far_west), (-1, west), (width, east), (width + 1, far_east)):
            place[row, column] = start + row
    matrix = np.zeros((cells + 2 * LANES, cells + LANES), bool)
    for (row, column), target in place.items():
        if not -1 <= column <= width:
            continue
        for near in ((row - 1, column), (row + 1, column), (row, column - 1), (row, column + 1)):
            if near in place:
                matrix[place[near], target] = True
    return matrix


def started(pairs, sems):
    copies = [pltpu.make_async_copy(*pair, sems.at[i]) for i, pair in enumerate(pairs)]
    for copy in copies:
        copy.start()
    return copies


def edges_kernel(
    x_hbm, air_hbm, ocean_hbm, sea_hbm, courant_x_hbm, courant_y_hbm, all_hbm, edge_hbm,
    x_ref, air_ref, ocean_ref, sea_ref, courant_x_ref, courant_y_ref, all_ref, wide, sems,
):
    comps, rows, columns = x_ref.shape
    levels, tile_rows, _ = air_ref.shape
    copies = started(
        [
            (x_hbm, x_ref),
            (air_hbm, air_ref),
            (ocean_hbm, ocean_ref),
            (sea_hbm, sea_ref),
            (courant_x_hbm, courant_x_ref),
            (courant_y_hbm, courant_y_ref),
        ],
        sems.at[pl.ds(0, 6)],
    )
    edges = comps + 16 + levels
    start = edges
    column, lane = iota((columns, LANES), 0), iota((columns, LANES), 1)

    block = within(over(lane, rows), 4)
    wanted = jnp.where(block < 2, columns - 2 + block, block - 2) == column
    row_of_lane = within(lane, rows)
    total = jnp.zeros((comps, LANES), F32)
    copies[0].wait()
    wide[...] = x_ref[...].astype(F32).reshape(comps * rows, columns)
    for row in range(rows):
        values = wide[pl.ds(row, comps, stride=rows), :].astype(BF16)
        all_ref[start : start + comps] = values
        start += comps
        total += moved(values, (wanted & (row_of_lane == row)).astype(BF16))
    all_ref[:comps] = total.astype(BF16)
    leaving = started(
        [(all_ref.at[edges:start], all_hbm.at[edges:start])], sems.at[pl.ds(6, 1)]
    )
    for copy in copies[1:]:
        copy.wait()
    owner = jnp.where(lax.axis_index("lev") == 0, 1.0, 0.0)
    head, tail = split((air_ref[0] - ocean_ref[0]) * owner)
    sea = sea_ref[...].astype(F32) * owner
    none = jnp.zeros_like(sea)
    all_ref[comps : comps + 16] = jnp.concatenate([head, tail, sea, none], axis=0).astype(BF16)
    head, tail = split((air_ref[1] - ocean_ref[1]) * owner)
    later = start
    below = jnp.concatenate([head, tail, none, none], axis=0)
    all_ref[start : start + 16] = below.astype(BF16)
    start += 16
    terms = []
    for ref in (courant_x_ref, courant_y_ref):
        for term in split(ref[...]):
            rest = jnp.zeros((1, 2 * columns - comps), F32)
            terms += [term[:, :columns], jnp.concatenate([term[:, columns:], rest], axis=1)]
    terms.append(jnp.zeros((8, columns), F32))
    all_ref[start : start + 16] = jnp.concatenate(terms, axis=0).astype(BF16)
    start += 16

    values = [ref[:, row, :] for ref in (air_ref, ocean_ref) for row in range(tile_rows)]
    unit = columns // len(values)
    inner = within(lane, unit)
    wanted = (jnp.where(inner < 2, columns - 2 + inner, inner - 2) == column) & (inner < 4)
    total = jnp.zeros((levels, LANES), F32)
    for index, value in enumerate(values):
        value = value.astype(BF16)
        all_ref[start : start + levels] = value
        start += levels
        total += moved(value, (wanted & (over(lane, unit) == index)).astype(BF16))
    all_ref[comps + 16 : edges] = total.astype(BF16)
    leaving += started(
        [
            (all_ref.at[:edges], edge_hbm),
            (all_ref.at[:edges], all_hbm.at[:edges]),
            (all_ref.at[later:], all_hbm.at[later:]),
        ],
        sems.at[pl.ds(7, 3)],
    )
    for copy in leaving:
        copy.wait()


def advect_kernel(
    groups, count, rows, levels, all_ref, packed_ref, cx_ref, cy_ref, edge_ref, gathered
):
    comps = cx_ref.shape[0]
    columns = LANES
    width = columns // count
    cells = rows * width
    first = comps + 16 + levels
    edge_ref[...] = all_ref[:comps]

    def by_row(row):
        row = (row + rows) % rows
        return all_ref[first + row * comps : first + (row + 1) * comps]

    below = first + rows * comps
    terms = all_ref[below + 16 : below + 32].astype(F32)
    for index, ref in enumerate((cx_ref, cy_ref)):
        own = terms[4 * index : 4 * index + 4]
        own = own[:2] + own[2:]
        ref[...] = column_of(jnp.concatenate([own[:1], own[1:, : comps - columns]], axis=1), LANES)
    source, target = iota((columns, 2 * columns), 0), iota((columns, 2 * columns), 1)
    step = jnp.where(target < columns, -1, 1)
    sides = (source == within(target + step, columns)).astype(BF16)
    for row in range(rows):
        here = by_row(row).astype(F32)
        beside = moved(by_row(row), sides)
        along = upwind(here, cx_ref[...], beside[:, :columns], beside[:, columns:])
        across = upwind(
            here,
            cy_ref[...],
            by_row(row - 1).astype(F32),
            by_row(row + 1).astype(F32),
        )
        tile, place = divmod(row, count)
        gathered[tile * comps : (tile + 1) * comps, place * columns : (place + 1) * columns] = (
            here - along - across
        ).astype(BF16)
    for index in range(count):
        start = below + 32 + index * levels
        gathered[2 * comps :, index * columns : (index + 1) * columns] = all_ref[
            start : start + levels
        ]
    source = iota((count * columns, 2 * LANES), 0)
    lane = iota((count * columns, 2 * LANES), 1)
    for target in range(count // 2):
        origin = over(within(lane, LANES), width) * columns + within(lane, width)
        origin = origin + (2 * target + over(lane, LANES)) * width
        swap = (source == origin).astype(BF16)
        values = moved(gathered[...], swap).astype(BF16)
        for side in range(2):
            half = values[:, side * LANES : (side + 1) * LANES]
            packed_ref[2 * target + side, : 2 * comps, :] = half[: 2 * comps]
            start = 2 * comps + comps // groups
            packed_ref[2 * target + side, start : start + levels, :] = half[2 * comps :]
    size = comps // groups

    own = iota((size, LANES), 1)
    riders = jnp.zeros((size, LANES), F32)
    for group in range(groups):
        span = slice(group * size, (group + 1) * size)
        for index, term in enumerate(split(cx_ref[span]) + split(cy_ref[span])):
            riders = jnp.where(own == 5 * rows + 4 * group + index, term, riders)

    values = jnp.concatenate([all_ref[comps : comps + 16], all_ref[below : below + 16]], axis=0)
    spot, lanes = iota((columns, count * LANES), 0), iota((columns, count * LANES), 1)
    first_column = over(lanes, LANES) * width
    lanes = within(lanes, LANES) - 6 * rows
    inside = (lanes >= 0) & (lanes < width) & (spot == first_column + lanes)
    inland = moved(values, inside.astype(BF16))
    outside = ((lanes == 0) & (spot == first_column - 1)) | (
        (lanes == 1) & (spot == first_column + width)
    )
    shore = moved(values[:16], outside.astype(BF16))
    surfaces = [inland, shore]
    if size > 48:
        surfaces.append(jnp.zeros((size - 48, count * LANES), F32))
    surfaces = jnp.concatenate(surfaces, axis=0)

    source, target_lane = iota((cells, 2 * LANES), 0), iota((cells, 2 * LANES), 1)
    block = over(within(target_lane, LANES), rows)
    row_start = within(target_lane, rows) * width
    ends = []
    for group in range(groups):
        west = (target_lane < LANES) & (block == 2 * group) & (source == row_start + width - 1)
        east = (target_lane >= LANES) & (block == (2 * group + 7) % 8) & (source == row_start)
        ends.append((west | east).astype(BF16))
    source, target_lane = iota((LANES, 2 * LANES), 0), iota((LANES, 2 * LANES), 1)
    inner = within(target_lane, width)
    back = (target_lane - inner) & (LANES - 1)
    shifts = []
    for start in (0, 8):
        west = (target_lane < LANES) & (inner >= start) & (inner < start + 2)
        west = west & (source == back + width - 2 + inner - start)
        east = (target_lane >= LANES) & (inner >= start + 2) & (inner < start + 4)
        east = east & (source == back + inner - start - 2)
        shifts.append((west | east).astype(BF16))
    beside, beside_state = [], []
    half = levels // 2
    for target in range(count):
        total = jnp.zeros((size, 2 * LANES), F32)
        for group in range(groups):
            for tile in range(2):
                span = slice(tile * comps + group * size, tile * comps + (group + 1) * size)
                rows_of = slice(tile * LANES, (tile + 1) * LANES)
                total += moved(packed_ref[target, span, :], ends[group][rows_of])
        beside.append(total)
        start = 2 * comps + size
        low = moved(packed_ref[target, start : start + half, :], shifts[0])
        high = moved(packed_ref[target, start + half : start + levels, :], shifts[1])
        beside_state.append(low + high)
    for target in range(count):
        left, right = max(target - 1, 0), min(target + 1, count - 1)
        shared = riders + beside[left][:, :LANES] + beside[right][:, LANES:]
        shared += surfaces[:, target * LANES : (target + 1) * LANES]
        packed_ref[target, 2 * comps : 2 * comps + size, :] = shared.astype(BF16)
        start = 2 * comps + size + levels
        outer = beside_state[left][:, :LANES] + beside_state[right][:, LANES:]
        packed_ref[target, start : start + half, :] = outer.astype(BF16)


def coast_kernel(groups, count, rows, packed_ref, edge_ref, halo_ref, cx_ref, cy_ref, *out_refs):
    comps = cx_ref.shape[0]
    size = comps // groups
    levels = halo_ref.shape[0] - comps - 16
    cells = 2 * LANES
    width = cells // rows
    half = levels // 2
    block = over(iota((comps, LANES), 1), rows)
    near = jnp.where((block < 2) | (block >= 6), halo_ref[:comps], edge_ref[...])
    source, target = iota((LANES, 4 * LANES), 0), iota((LANES, 4 * LANES), 1)
    lane = within(target, LANES)
    row = within(lane, rows)
    kind = over(target, LANES)
    shift = jnp.where(
        kind == 0,
        within(lane - rows, LANES),
        jnp.where(
            kind == 1,
            within(lane + rows, LANES),
            lane - row + within(row + jnp.where(kind == 2, -1, 1), rows),
        ),
    )
    four = moved(near, (source == shift).astype(BF16))
    near = near.astype(F32)
    near = (
        near
        - upwind(near, cx_ref[...], four[:, :LANES], four[:, LANES : 2 * LANES])
        - upwind(near, cy_ref[...], four[:, 2 * LANES : 3 * LANES], four[:, 3 * LANES :])
    )
    source, target = iota((LANES, cells), 0), iota((LANES, cells), 1)
    column, row = within(target, width), over(target, width)
    spread = ((column == 0) & (source == 2 * rows + row)) | (
        (column == width - 1) & (source == 5 * rows + row)
    )
    ends = moved(near, spread.astype(BF16))
    shared = jnp.zeros((size, LANES), F32)
    source, target = iota((LANES, LANES), 0), iota((LANES, LANES), 1)
    for group in range(groups):
        there = over(target, rows)
        from_block = jnp.where(
            there == 2 * group, 1, jnp.where(there == (2 * group + 7) % 8, 6, LANES)
        )
        spread = source == from_block * rows + within(target, rows)
        shared += moved(near[group * size : (group + 1) * size], spread.astype(BF16))
    beyond = ((target == 6 * rows) & (source == LANES - 1)) | (
        (target == 6 * rows + 1) & (source == 0)
    )
    coast = moved(halo_ref[comps : comps + 16], beyond.astype(BF16))
    coast = [jnp.zeros((32, LANES), F32), coast]
    if size > 48:
        coast.append(jnp.zeros((size - 48, LANES), F32))
    shared += jnp.concatenate(coast, axis=0)
    inner = within(target, width)
    low = (source == target) & (inner < 4)
    high = (source == target - 8) & (inner >= 8) & (inner < 12)
    state = moved(halo_ref[comps + 16 : comps + 16 + half], low.astype(BF16))
    state += moved(halo_ref[comps + 16 + half :], high.astype(BF16))
    me = lax.axis_index(("cells", "lev"))
    for slot in range(count):
        target = lax.rem(me + first_order(count)[slot], count)
        out_refs[slot][...] = packed_ref[target]
        place, lane = iota((size, LANES), 0), iota((size, LANES), 1)

        def patch(start, stop, where, values):
            old = out_refs[slot][start:stop].astype(F32)
            out_refs[slot][start:stop] = jnp.where(where, values, old).astype(BF16)

        def patch_ends(east):
            column = within(iota((comps, LANES), 1), width)
            for tile in range(2):
                values = ends[:, tile * LANES : (tile + 1) * LANES]
                where = column == (width - 1 if east else 0)
                patch(tile * comps, (tile + 1) * comps, where, values)
            own = over(lane, rows)
            where = (place >= 32) & (place < 48) & (lane == 6 * rows + (1 if east else 0))
            for group in range(groups):
                where = where | (own == ((2 * group + 7) % 8 if east else 2 * group))
            patch(2 * comps, 2 * comps + size, where, shared)
            start = 2 * comps + size
            start += levels
            inner = within(iota((half, LANES), 1), 8)
            patch(start, start + half, (inner >= 2) == east, state)

        @pl.when(target == 0)
        def _():
            patch_ends(False)

        @pl.when(target == count - 1)
        def _():
            patch_ends(True)


def steps_kernel(
    groups, count, rows, quartet_ref, coupler_ref, growth_ref, beside_ref, lateral_ref, *refs
):
    in_refs, refs = refs[:count], refs[count:]
    out_refs, refs = refs[:count], refs[count:]
    first_in, fresh, second_in, last, shares, factors, state, ends = refs
    total = quartet_ref.shape[0]
    comps = total // count
    size = comps // groups
    cells = 2 * LANES
    wide = 3 * LANES
    width = cells // rows
    levels = coupler_ref.shape[0] // 2
    half = shares.shape[1]
    lev_parts = levels // half
    tile_rows = rows * lev_parts // count
    me = lax.axis_index(("cells", "lev"))
    west_end = (me == 0) & (lax.axis_index("sect") == 0)
    east_end = (me == count - 1) & (lax.axis_index("sect") == lax.axis_size("sect") - 1)
    factors[:, 8:16] = column_of(0.1 * growth_ref[...], 8)

    source, target = iota((LANES, 2 * LANES), 0), iota((LANES, 2 * LANES), 1)
    block = over(target, rows)
    opened = []
    for group in range(groups):
        from_block = jnp.where(
            block == 0, 2 * group, jnp.where(block == 7, (2 * group + 7) % 8, LANES)
        )
        column = source == from_block * rows + within(target, rows)
        rider = source - (5 * rows + 4 * group)
        rider = (rider >= 0) & (rider < 4) & (over(rider, 2) == target - LANES)
        opened.append((column | rider).astype(BF16))
    source, target = iota((LANES, wide), 0), iota((LANES, wide), 1)
    on_side = target >= cells
    lane = within(target, width) + 6 * rows
    side = jnp.where(target < cells + rows, 0, 1) + 6 * rows
    repeat = (source == jnp.where(on_side, side, lane)).astype(BF16)
    place, target = iota((48, wide), 0), iota((48, wide), 1)
    on_side = target >= cells
    row_of_lane = jnp.where(on_side, within(target, rows), over(target, width))
    row_of_lane = jnp.where((place >= 32) == on_side, row_of_lane, -1) - within(place, tile_rows)
    terms = jnp.zeros((48, wide), F32)
    for slot in range(count):
        source = lax.rem(me - first_order(count)[slot] + count, count)
        start = pl.multiple_of(source * comps, 16)
        span = pl.ds(start, comps)
        for tile in range(2):
            values = in_refs[slot][tile * comps : (tile + 1) * comps]
            first_in[span, tile * LANES : (tile + 1) * LANES] = values
            values = values.astype(F32)
            first_in[span, wide + tile * LANES : wide + (tile + 1) * LANES] = (
                values * values
            ).astype(BF16)
        for group in range(groups):
            span = pl.ds(pl.multiple_of(start + group * size, 16), size)
            values = moved(in_refs[slot][2 * comps : 2 * comps + size], opened[group])
            first_in[span, cells:wide] = values[:, :LANES].astype(BF16)
            values_8 = values[:, LANES : LANES + 8]
            values = values[:, :LANES]
            first_in[span, wide + cells :] = (values * values).astype(BF16)
            factors[span, :8] = values_8
        place = 2 * comps
        spread = moved(in_refs[slot][place : place + 48], repeat)
        here = row_of_lane == over(source, lev_parts) * tile_rows
        terms += jnp.where(here, spread, 0.0)
        place += size
        state[source] = in_refs[slot][place : place + half]
        ends[source] = in_refs[slot][place + half :]

    place, source = iota((8, 48), 0), over(iota((8, 48), 1), tile_rows)
    source = jnp.where(source < 3, source, jnp.where(source < 8, source - 1, source - 8))
    skipped = over(iota((8, 48), 1), tile_rows) == 3
    terms = moved((place == jnp.where(skipped, 8, source)).astype(F32), terms.astype(BF16))

    def joined(rows_of):
        return rows_of[:1] + rows_of[1:2]

    surface, sea = joined(terms), terms[2:3]
    below = joined(terms[3:5])[:, :cells]
    wind = surface * surface

    def renew(values, products, growth, wind, sea):
        half = values.shape[1]
        paired, quad_square = products[:, :half], products[:, half:]
        below = 1.0 + 0.1 * values * values
        inverse = pl.reciprocal(below, approx=True)
        inverse = inverse * (2.0 - below * inverse)
        return (values + 0.3 * (values * paired - quad_square) + growth * wind) * inverse * sea

    part = total // 2
    for step in range(2):
        span = slice(step * part, (step + 1) * part)
        products = jnp.dot(quartet_ref[span, :], first_in[...], preferred_element_type=F32)
        values = first_in[span, :wide].astype(F32)
        fresh[span, :] = renew(values, products, factors[span, 8:9], wind, sea).astype(BF16)
    part = total // 8
    for step in range(8):
        span = slice(step * part, (step + 1) * part)
        beside = jnp.dot(fresh[span, :], beside_ref[...], preferred_element_type=F32)
        here = fresh[span, :cells].astype(F32)
        cx = jnp.broadcast_to(factors[span, 0:1], here.shape)
        cy = jnp.broadcast_to(factors[span, 1:2], here.shape)
        values = (
            here
            - upwind(here, cx, beside[:, :cells], beside[:, cells : 2 * cells])
            - upwind(here, cy, beside[:, 2 * cells : 3 * cells], beside[:, 3 * cells :])
        ).astype(BF16)
        second_in[span, :cells] = values
        values = values.astype(F32)
        second_in[span, cells:] = (values * values).astype(BF16)

    halves = iota((half, LANES), 1) < LANES // 2

    def collected(values):
        fields = []
        for kind in range(2):
            for part in range(lev_parts):
                tiles = []
                for pair in range(count // lev_parts // 2):
                    left = values[2 * pair * lev_parts + part].astype(F32)
                    right = values[(2 * pair + 1) * lev_parts + part].astype(F32)
                    if kind == 0:
                        right = pltpu.roll(right, LANES // 2, 1)
                    else:
                        left = pltpu.roll(left, LANES // 2, 1)
                    tiles.append(jnp.where(halves[: left.shape[0]], left, right))
                fields.append(jnp.concatenate(tiles, axis=1))
        return fields

    inner = jnp.concatenate(collected(state), axis=0)
    source, target = iota((cells, cells), 0), iota((cells, cells), 1)
    far = over(target, LANES)
    block = over(within(target, LANES), rows)
    order = jnp.where(block == 0, jnp.where(far == 0, 1, 0), jnp.where(far == 0, 2, 3))
    used = (block == 0) | (block == 7)
    spread = [
        ((source == within(target, rows) * width + order + 8 * high) & used).astype(BF16)
        for high in range(2)
    ]
    outer = []
    for field in collected(ends):
        outer += [moved(field, spread[0]), moved(field, spread[1])]
    outer = jnp.concatenate(outer, axis=0)

    def bounded(values):
        lane = iota(values.shape, 1)
        outside = (west_end & (lane < rows)) | (east_end & (lane >= LANES - rows))
        return jnp.where(outside, 0.0, values)

    outer = [bounded(outer[:, :LANES]), bounded(outer[:, LANES:])]

    def relaxed_once(here, lateral):
        level = within(iota(here.shape, 0), levels)
        lateral = lateral - 4.0 * here
        above = jnp.where(level == 0, 0.0, pltpu.roll(here, 1, 0))
        under = jnp.where(level == levels - 1, 0.0, pltpu.roll(here, 2 * levels - 1, 0))
        return here + 0.1 * lateral + 0.1 * (above + under - 2.0 * here)

    sign = jnp.where(iota((2 * levels, 1), 0) < levels, -0.3, 0.3)
    forced = jnp.dot(coupler_ref[...], fresh[...], preferred_element_type=F32) * sign
    here = jnp.concatenate([inner] + outer, axis=1)
    fields = relaxed_once(here[:, :wide], moved(here, lateral_ref[...])) + forced
    fields = jnp.concatenate([fields[:, :cells], bounded(fields[:, cells:])], axis=1)
    near = lateral_ref[:wide, :cells]
    head, tail = split(fields)
    fields = relaxed_once(fields[:, :cells], moved(head, near) + moved(tail, near))

    terms = jnp.concatenate([terms[:, :cells], bounded(terms[:, cells:])], axis=1)
    lateral = joined(moved(terms, near))
    calm = surface[:, :cells]
    calm = calm + 0.1 * (lateral - 4.0 * calm) + 0.1 * (below - 2.0 * calm)
    later = calm + forced[:1, :cells] - forced[levels : levels + 1, :cells]
    later = later * later

    part = total // 2
    for step in range(2):
        span = slice(step * part, (step + 1) * part)
        products = jnp.dot(quartet_ref[span, :], second_in[...], preferred_element_type=F32)
        values = second_in[span, :cells].astype(F32)
        done = renew(values, products, factors[span, 8:9], later, sea[:, :cells])
        last[span, :] = done.astype(BF16)

    forced = jnp.dot(coupler_ref[...], last[...], preferred_element_type=F32)
    carried = fields + sign * forced
    for target in range(count):
        cell_tile, lev_part = target // lev_parts, target % lev_parts
        columns = slice((cell_tile // 2) * LANES, (cell_tile // 2 + 1) * LANES)
        air = carried[lev_part * half : (lev_part + 1) * half, columns]
        sea_part = carried[levels + lev_part * half : levels + (lev_part + 1) * half, columns]
        if cell_tile % 2:
            air = pltpu.roll(air, LANES // 2, 1)
        else:
            sea_part = pltpu.roll(sea_part, LANES // 2, 1)
        shares[target] = jnp.where(halves, air, sea_part).astype(BF16)
    for slot in range(count):
        target = lax.rem(me + last_order(count)[slot], count)
        span = pl.ds(pl.multiple_of(target * comps, 16), comps)
        out_refs[slot][:comps] = last[span, :LANES]
        out_refs[slot][comps : 2 * comps] = last[span, LANES:]
        out_refs[slot][2 * comps :] = shares[target]


def finish_kernel(count, swap_ref, *refs):
    in_refs, refs = refs[:count], refs[count:]
    energy_ref, air_ref, ocean_ref, gathered, wide, narrow = refs
    comps, rows, columns = energy_ref.shape
    levels, tile_rows, _ = air_ref.shape
    me = lax.axis_index(("cells", "lev"))
    for slot in range(count):
        source = lax.rem(me - last_order(count)[slot] + count, count)
        gathered[:, pl.ds(pl.multiple_of(source * columns, columns), columns)] = in_refs[slot][...]
    for pair in range(count // 2):
        lanes = slice(2 * pair * columns, 2 * (pair + 1) * columns)
        values = moved(gathered[...], swap_ref[:, lanes])
        for side in range(2):
            index = 2 * pair + side
            part = values[:, side * columns : (side + 1) * columns]
            for tile in range(rows // count):
                wide[pl.ds(tile * count + index, comps, stride=rows), :] = part[
                    tile * comps : (tile + 1) * comps
                ]
            kind, row = divmod(index, tile_rows)
            narrow[pl.ds(kind * levels * tile_rows + row, levels, stride=tile_rows), :] = part[
                2 * comps :
            ]
    energy_ref[...] = wide[...].reshape(comps, rows, columns).astype(energy_ref.dtype)
    size = levels * tile_rows
    air_ref[...] = narrow[:size, :].reshape(air_ref.shape)
    ocean_ref[...] = narrow[size:, :].reshape(ocean_ref.shape)


def first_order(count):
    return (0, 2, 1) + tuple(range(3, count))


def last_order(count):
    return (0, count - 2, count - 1, 2, 1) + tuple(range(3, count - 2))


def spread_out(pieces, axes, order):
    count = len(pieces)
    received = [pieces[0]]
    for slot in range(1, count):
        pairs = [(index, (index + order[slot]) % count) for index in range(count)]
        received.append(lax.ppermute(pieces[slot], axes, pairs))
    return received


def by_columns(
    spectrum, courant_x, courant_y, growth, quartet, coupler, atmosphere, ocean_state, sea_mask
):
    axes = ("cells", "lev")
    count = lax.axis_size("cells") * lax.axis_size("lev")
    sects = lax.axis_size("sect")
    comps, rows, columns = spectrum.shape
    total = comps * count
    width = columns // count
    cells = rows * width
    levels_own, tile_rows, _ = atmosphere.shape
    groups = 3
    whole = pl.BlockSpec(memory_space=VMEM)
    far = pl.BlockSpec(memory_space=pltpu.HBM)

    def shape(*dims, kind=BF16):
        return jax.ShapeDtypeStruct(dims, kind)

    def call(kernel, outs, *args, kept=(), place=whole, flops=0, mega=16):
        return pl.pallas_call(
            kernel,
            out_shape=outs,
            in_specs=[place] * len(args),
            out_specs=jax.tree.map(lambda _: place, outs),
            scratch_shapes=list(kept),
            compiler_params=pltpu.CompilerParams(vmem_limit_bytes=mega * 1024 * 1024),
            cost_estimate=pl.CostEstimate(flops=flops, bytes_accessed=4000000, transcendentals=0),
        )(*args)

    swap = jnp.asarray(swap_matrix(count, width), BF16)
    edges = comps + 16 + levels_own
    fields = (spectrum, atmosphere, ocean_state, sea_mask, courant_x[None], courant_y[None])
    fetched = shape(edges + rows * comps + 32 + count * levels_own, LANES)
    fetched, edge = call(
        edges_kernel,
        (fetched, shape(edges, LANES)),
        *fields,
        kept=[VMEM(array.shape, array.dtype) for array in fields + (fetched,)]
        + [VMEM((comps * rows, columns), F32), pltpu.SemaphoreType.DMA((10,))],
        place=far,
        mega=63,
    )
    halo = lax.ppermute(edge, "sect", [(0, 1), (1, 0)])

    size = 2 * comps + comps // groups + levels_own + levels_own // 2
    factor = shape(comps, LANES, kind=F32)
    packed, factor_x, factor_y, edge = call(
        functools.partial(advect_kernel, groups, count, rows, levels_own),
        (shape(count, size, LANES), factor, factor, shape(comps, LANES)),
        fetched,
        kept=[VMEM((2 * comps + levels_own, count * columns), BF16)],
        flops=2000000000,
    )
    pieces = call(
        functools.partial(coast_kernel, groups, count, rows),
        (shape(size, LANES),) * count,
        packed,
        edge,
        halo,
        factor_x,
        factor_y,
    )
    received = spread_out(pieces, axes, first_order(count))

    results = call(
        functools.partial(steps_kernel, groups, count, rows),
        (shape(2 * comps + levels_own, LANES),) * count,
        quartet,
        coupler,
        growth[None],
        jnp.asarray(neighbour_matrices(rows, width), BF16),
        jnp.asarray(lateral_matrix(rows, width), BF16),
        *received,
        kept=[
            VMEM((total, 6 * LANES), BF16),
            VMEM((total, 3 * LANES), BF16),
            VMEM((total, 4 * LANES), BF16),
            VMEM((total, cells), BF16),
            VMEM((count, levels_own, LANES), BF16),
            VMEM((total, LANES), F32),
            VMEM((count, levels_own, LANES), BF16),
            VMEM((count, levels_own // 2, LANES), BF16),
        ],
        mega=32,
    )
    returned = spread_out(results, axes, last_order(count))

    return call(
        functools.partial(finish_kernel, count),
        (
            shape(*spectrum.shape),
            shape(*atmosphere.shape, kind=F32),
            shape(*ocean_state.shape, kind=F32),
        ),
        swap,
        *returned,
        kept=[
            VMEM((2 * comps + levels_own, count * columns), BF16),
            VMEM((comps * rows, columns), F32),
            VMEM((2 * levels_own * tile_rows, columns), F32),
        ],
    )


def on_device(spectrum, *rest):
    atmosphere = rest[5]
    blocks = lax.axis_size("cells") * lax.axis_size("lev")
    comps, rows, columns = spectrum.shape
    fits = (
        columns == LANES
        and blocks == 8
        and lax.axis_size("sect") == 2
        and rows * (columns // blocks) == 2 * LANES
        and atmosphere.shape[1] * (columns // blocks) * 2 == LANES
        and comps % 48 == 0
        and comps >= 144
        and atmosphere.shape[0] % 16 == 0
        and NSTEP == 2
    )
    return (by_columns if fits else any_shape)(spectrum, *rest)


def solution(mesh):
    in_specs = (
        P(("cells", "lev"), "groups", "sect"),
        P(("cells", "lev")),
        P(("cells", "lev")),
        P(),
        P(),
        P(),
        P("lev", ("groups", "cells"), "sect"),
        P("lev", ("groups", "cells"), "sect"),
        P(("groups", "cells"), "sect"),
    )
    out_specs = (
        P(("cells", "lev"), "groups", "sect"),
        P("lev", ("groups", "cells"), "sect"),
        P("lev", ("groups", "cells"), "sect"),
    )
    return jax.shard_map(
        on_device, mesh=mesh, in_specs=in_specs, out_specs=out_specs, check_vma=False
    )
```
